128 devices in a mesh: shard: 4 (over y), context: 16 (over x, z), tensor: 2 (over core).
Axes of the slice: x: 4, y: 4, z: 4, core: 2. Of those that a mesh axis runs over, the one named last changes fastest.
Arguments:
- tokens: bfloat16 [4, 2560, 2560], P('shard', 'context'), may hold values from -6 to 6
- lengths: int32 [4], P('shard'), may hold values from 1024 to 2560, as said below
- attn_gain: bfloat16 [2560], P(('shard', 'context')), may hold values from 0.5 to 1.5
- w_query: bfloat16 [2560, 2560], P(('shard', 'context'), 'tensor'), may hold values from -0.25 to 0.25
- w_keyval: bfloat16 [2560, 512], P(('shard', 'context')), may hold values from -0.125 to 0.125
- w_output: bfloat16 [2560, 2560], P(('shard', 'context'), 'tensor'), may hold values from -0.625 to 0.625
- mlp_gain: bfloat16 [2560], P(('shard', 'context')), may hold values from 0.5 to 1.5
- w_gate: bfloat16 [2560, 7680], P(('shard', 'context'), 'tensor'), may hold values from -0.125 to 0.125
- w_up: bfloat16 [2560, 7680], P(('shard', 'context'), 'tensor'), may hold values from -0.125 to 0.125
- w_down: bfloat16 [2560, 7680], P(('shard', 'context'), 'tensor'), may hold values from -0.0625 to 0.0625
- cotangent: bfloat16 [4, 2560, 2560], P('shard', 'context'), may hold values from -6 to 6
Outputs:
- block_out: bfloat16 [4, 2560, 2560], P('shard', 'context')
- tokens_grad: bfloat16 [4, 2560, 2560], P('shard', 'context')
- attn_gain_grad: float32 [2560], P(('shard', 'context'))
- query_grad: float32 [2560, 2560], P(('shard', 'context'), 'tensor')
- keyval_grad: float32 [2560, 512], P(('shard', 'context'))
- output_grad: float32 [2560, 2560], P(('shard', 'context'), 'tensor')
- mlp_gain_grad: float32 [2560], P(('shard', 'context'))
- gate_grad: float32 [2560, 7680], P(('shard', 'context'), 'tensor')
- up_grad: float32 [2560, 7680], P(('shard', 'context'), 'tensor')
- down_grad: float32 [2560, 7680], P(('shard', 'context'), 'tensor')
The draws below stay inside these ranges and needn't reach their ends.
Inputs may be any that keep to these rules, and one draw needn't show every extreme that they name: `lengths`: valid tokens fill the end of each slot; at least one of the 4 slots holds 2560 valid tokens.
All inputs are finite; a program needn't handle non-finite values.
Results may differ from the reference program's by a relative error of at most 0.02.
Values may be sent and summed in bfloat16 or wider, within the bound.
No kernel may reach another device: no remote copies, remote signals or barrier semaphores. Data moves between devices by JAX's collectives and lax.ppermute only.
A program may use at most 448 MiB of HBM per device.

```python
import jax
import jax.numpy as jnp
from jax import lax

D = 2560
HEADS = 10
HD = 256
FF = 7680
WINDOW = 2048
SEQ_LEN = 2560
BATCH = 4
LEN_MIN = 1024


def draw_lengths(key, part):
    key = jax.random.fold_in(key, 7)
    length_key, slot_key = jax.random.split(key)
    drawn_lengths = jax.random.randint(length_key, (BATCH,), LEN_MIN, SEQ_LEN + 1)
    full_slot = jax.random.randint(slot_key, (), 0, BATCH)
    return jnp.where(jnp.arange(BATCH) == full_slot, SEQ_LEN, drawn_lengths).astype(jnp.int32)


def shard_levels(stream_key, dims, cuts, low, high):
    loudness = 1.0
    for axis_at, parts in cuts:
        draws = jax.random.uniform(jax.random.fold_in(jax.random.fold_in(stream_key, 6), axis_at), (parts,), jnp.float32, low / len(cuts), high / len(cuts))
        loudness = loudness * jnp.repeat(jnp.exp(draws), dims[axis_at] // parts).reshape((-1,) + (1,) * (len(dims) - 1 - axis_at))
    return loudness


def scatter_about(rng, shape, scale, limit, pieces=(), kind=jnp.bfloat16):
    loudness = shard_levels(rng, shape, pieces, -0.22, 0.18) if pieces else 1.0
    array = jax.random.normal(rng, shape, jnp.float32) * scale * loudness
    return jnp.minimum(jnp.maximum(array, -limit), limit).astype(kind)


def setup_inputs(seed: int = 0) -> dict:
    splits = jax.random.split(jax.random.key(seed), 12)
    return {
        "tokens": scatter_about(splits[0], (BATCH, SEQ_LEN, D), 1.0, 6.0, ((0, 4), (1, 16))),
        "lengths": draw_lengths(jax.random.fold_in(splits[11], 71), 0),
        "attn_gain": jnp.clip(1.0 + 0.1 * jax.random.normal(splits[2], (D,), jnp.float32), 0.5, 1.5).astype(jnp.bfloat16),
        "w_query": scatter_about(splits[3], (D, HEADS * HD), (D // 4) ** -0.5, 0.25, ((0, 64), (1, 2))),
        "w_keyval": scatter_about(splits[4], (D, 2 * HD), D ** -0.5, 0.125, ((0, 64),)),
        "w_output": scatter_about(splits[5], (D, HEADS * HD), (HEADS * HD // 32) ** -0.5, 0.625, ((0, 64), (1, 2))),
        "mlp_gain": jnp.clip(1.0 + 0.1 * jax.random.normal(splits[6], (D,), jnp.float32), 0.5, 1.5).astype(jnp.bfloat16),
        "w_gate": scatter_about(splits[7], (D, FF), D ** -0.5, 0.125, ((0, 64), (1, 2))),
        "w_up": scatter_about(splits[8], (D, FF), D ** -0.5, 0.125, ((0, 64), (1, 2))),
        "w_down": scatter_about(splits[9], (D, FF), FF ** -0.5, 0.0625, ((0, 64), (1, 2))),
        "cotangent": scatter_about(splits[10], (BATCH, SEQ_LEN, D), 1.0, 6.0, ((0, 4), (1, 16))),
    }


EPSILON = 1e-06
NEGATIVE_FILL = -1e+30
PRECISE = lax.Precision.HIGHEST

@jax.custom_vjp
def low(v):
    return lax.optimization_barrier(v.astype(jnp.bfloat16)).astype(jnp.float32)

@jax.custom_vjp
def low_back(v):
    return v

def low_keep(v):
    return (low(v), None)

def low_pass(kept, grad):
    return (grad,)

def back_keep(v):
    return (v, None)

def back_low(kept, grad):
    return (low(grad),)
low.defvjp(low_keep, low_pass)
low_back.defvjp(back_keep, back_low)

def product(left, right):
    return jnp.dot(left, right, precision=PRECISE, preferred_element_type=jnp.float32)

def scaled_norm(values, gain_vec):
    inverse = lax.rsqrt(lax.optimization_barrier(jnp.mean(values * values, axis=-1, keepdims=True)) + EPSILON)
    return values * inverse * gain_vec

def rotate(values, position):
    quarter = values.shape[-1] // 4
    frequency = 10000.0 ** (-jnp.arange(quarter, dtype=jnp.float32) / quarter)
    phase_angle = position[:, None].astype(jnp.float32) * frequency[None, :]
    cosine = jnp.cos(phase_angle)[:, None, :]
    sine_part = jnp.sin(phase_angle)[:, None, :]
    first_half = values[..., :quarter]
    second = values[..., quarter:2 * quarter]
    return jnp.concatenate([first_half * cosine - second * sine_part, second * cosine + first_half * sine_part, values[..., 2 * quarter:]], axis=-1)

def sequence_forward(inputs, length, attn_gain, w_query, w_keyval, w_output, mlp_gain, w_gate, w_up, w_down):
    seq_count = inputs.shape[0]
    token_index = jnp.arange(seq_count, dtype=jnp.int32)
    position = token_index - (seq_count - length)
    live_rows = position >= 0
    normed = low(scaled_norm(inputs, attn_gain))
    query_pre = low_back(product(normed, w_query)).reshape(seq_count, HEADS, HD)
    queries = low(rotate(query_pre, position) * HD ** (-0.5))
    keyval = product(normed, w_keyval)
    key_pre = low_back(keyval[:, :HD])
    key_rows = low(rotate(key_pre[:, None, :], position)[:, 0, :])
    value_rows = low(low_back(keyval[:, HD:]))
    block_rows = 512 if seq_count % 512 == 0 else seq_count

    def attend(row_start):
        query_block = lax.dynamic_slice_in_dim(queries, row_start, block_rows, 0)
        scores = low_back(jnp.einsum('qhd,kd->hqk', query_block, key_rows, precision=PRECISE))
        query_index = row_start + jnp.arange(block_rows, dtype=jnp.int32)
        offset = query_index[:, None] - token_index[None, :]
        allowed = ((offset >= 0) & (offset < WINDOW) & live_rows[None, :])[None]
        live = lax.dynamic_slice_in_dim(live_rows, row_start, block_rows, 0)[None, :, None]
        row_top = lax.optimization_barrier(jnp.max(jnp.where(allowed, scores, NEGATIVE_FILL), axis=-1, keepdims=True))
        row_top = jnp.where(live, row_top, 0.0)
        weights_exp = jnp.where(allowed, jnp.exp(scores - row_top), 0.0)
        row_total = jnp.where(live, lax.optimization_barrier(jnp.sum(weights_exp, axis=-1, keepdims=True)), 1.0)
        prob_low = low(weights_exp / row_total)
        return jnp.einsum('hqk,kd->qhd', prob_low, value_rows, precision=PRECISE)
    row_starts = jnp.arange(seq_count // block_rows, dtype=jnp.int32) * block_rows
    attended = lax.map(jax.checkpoint(attend), row_starts).reshape(seq_count, HEADS * HD)
    attended = low(low_back(attended))
    branch = low_back(product(attended, w_output.T))
    hidden_in = inputs + branch
    normed_two = low(scaled_norm(hidden_in, mlp_gain))
    gate_pre = low_back(product(normed_two, w_gate))
    up_pre = low_back(product(normed_two, w_up))
    hidden = low(jax.nn.gelu(gate_pre) * up_pre)
    mlp_branch = low_back(product(hidden, w_down.T))
    return jnp.where(live_rows[:, None], hidden_in + mlp_branch, 0.0)

def reference(tokens, lengths, attn_gain, w_query, w_keyval, w_output, mlp_gain, w_gate, w_up, w_down, cotangent):
    weight_list = tuple((weight.astype(jnp.float32) for weight in (attn_gain, w_query, w_keyval, w_output, mlp_gain, w_gate, w_up, w_down)))

    def seq_step(running, sequence_item):
        inputs, length, upstream = sequence_item

        def forward(values, gain_one, query_w, keyval_w, output_w, gain_two, gate_w, up_w, down_w):
            return sequence_forward(values, length, gain_one, query_w, keyval_w, output_w, gain_two, gate_w, up_w, down_w)
        block_value, pullback = jax.vjp(forward, inputs, *weight_list)
        gradients = pullback(upstream)
        running = tuple((total + grad_part for total, grad_part in zip(running, gradients[1:])))
        return (running, (block_value, gradients[0]))
    initial = tuple((jnp.zeros_like(weight) for weight in weight_list))
    summed, (outputs, input_grads) = lax.scan(seq_step, initial, (tokens.astype(jnp.float32), lengths, cotangent.astype(jnp.float32)))
    return (outputs.astype(jnp.bfloat16), input_grads.astype(jnp.bfloat16), summed[0], summed[1], summed[2], summed[3], summed[4], summed[5], summed[6], summed[7])
```

```python
import jax
import jax.numpy as jnp
from jax import lax
from jax.sharding import Mesh
from jax.sharding import PartitionSpec as P

WINDOW = 2048
SHARD_CONTEXT = ("shard", "context_0", "context_1")
CONTEXT = ("context_0", "context_1")
Y, X, Z, T = "shard", "context_0", "context_1", "tensor"

EPSILON = 1e-06
NEGATIVE_FILL = -1e30
BF = jnp.bfloat16
F32 = jnp.float32


def shift(x, axis, by):
    n = lax.axis_size(axis)
    return lax.ppermute(x, axis, [(i, (i + by) % n) for i in range(n)])


def ring_blocks(x, axis):
    after = shift(x, axis, -1)
    before = shift(x, axis, 1)
    return [x, after, shift(x, axis, 2), before]


def placed(blocks, axis, out, dim, rest):
    me = lax.axis_index(axis)
    for r, block in enumerate(blocks):
        start = list(rest)
        start[dim] = (me + r) % 4
        out = lax.dynamic_update_slice(out, jnp.expand_dims(block, dim), start)
    return out


def gather_context(block):
    rows, cols = block.shape
    half = rows // 2
    out = jnp.zeros((4, 4, rows, cols), block.dtype)
    lead = jnp.zeros((4, half, cols), block.dtype)
    tail = jnp.zeros((4, rows - half, cols), block.dtype)
    first = placed(ring_blocks(block[:half], X), X, lead, 0, (0, 0, 0))
    second = placed(ring_blocks(block[half:], Z), Z, tail, 0, (0, 0, 0))
    out = placed(ring_blocks(first, Z), Z, out, 1, (0, 0, 0, 0))
    out = placed(ring_blocks(second, X), X, out, 0, (0, 0, half, 0))
    return out.reshape(16 * rows, cols)


def summed_over(parts, axis, dim):
    me = lax.axis_index(axis)
    total = lax.dynamic_index_in_dim(parts, me, dim, keepdims=False).astype(F32)
    for r in (1, 3, 2):
        block = lax.dynamic_index_in_dim(parts, (me + r) % 4, dim, keepdims=False)
        total = total + shift(block, axis, r).astype(F32)
    return total


def scatter_context(parts, kind):
    rows, cols = parts.shape[0] // 16, parts.shape[1]
    half = rows // 2
    grid = parts.astype(kind).reshape(4, 4, rows, cols)
    one = summed_over(grid[:, :, :half], X, 0).astype(kind)
    two = summed_over(grid[:, :, half:], Z, 1).astype(kind)
    return jnp.concatenate([summed_over(one, Z, 0), summed_over(two, X, 0)], axis=0)


def gather_rows(mine):
    own = jnp.concatenate(ring_blocks(mine, Y), axis=0)
    return jnp.concatenate([own, shift(own, T, 1)], axis=0)


def scatter_rows(parts):
    half = parts.shape[0] // 2
    own = parts[:half] + shift(parts[half:].astype(BF), T, 1).astype(F32)
    blocks = own.reshape(4, half // 4, -1)
    low = blocks.astype(BF)
    total = blocks[0]
    for r in (1, 3, 2):
        total = total + shift(low[r], Y, r).astype(F32)
    return total


def rows_home(parts):
    me = lax.axis_index(Y)
    cols = parts.shape[1]
    blocks = parts.reshape(2, 4, 80, cols).swapaxes(0, 1).reshape(4, 160, cols)
    out = jnp.zeros((4, 160, cols), parts.dtype)
    for r in range(4):
        block = shift(blocks[r], Y, r) if r else blocks[0]
        out = lax.dynamic_update_slice(out, block[None], ((me - r) % 4, 0, 0))
    return out


def columns_out(blocks):
    me = lax.axis_index(Y)
    cols = blocks.shape[2]
    got = [None] * 4
    for r in range(4):
        block = lax.dynamic_index_in_dim(blocks, (me + r) % 4, 0, keepdims=False)
        got[(4 - r) % 4] = shift(block, Y, r) if r else block
    return jnp.stack(got).reshape(4, 2, 80, cols).swapaxes(0, 1).reshape(640, cols)


def quarters(x):
    rows = x.shape[0]
    return x.reshape(rows, 4, -1).swapaxes(0, 1)


def joined(blocks):
    return blocks.swapaxes(0, 1).reshape(blocks.shape[1], -1)


def to_piece_order(x):
    rows = x.shape[0]
    return x.reshape(rows, 4, 16, 40).swapaxes(1, 2).reshape(rows, 2560)


def from_piece_order(x):
    rows = x.shape[0]
    return x.reshape(rows, 16, 4, 40).swapaxes(1, 2).reshape(rows, 2560)


def halves_home(mine, t):
    other = shift(mine, T, 1)
    return jnp.where(t == 0, jnp.concatenate([mine, other]), jnp.concatenate([other, mine]))


def inverse_root(values):
    return lax.rsqrt(jnp.mean(values * values, axis=-1, keepdims=True) + EPSILON)


def norm_back(grad, values, inverse, gain):
    scaled = gain * grad
    return inverse * scaled - values * inverse**3 * jnp.mean(
        scaled * values, axis=-1, keepdims=True
    )


def angles(position, head_dim):
    quarter = head_dim // 4
    frequency = 10000.0 ** (-jnp.arange(quarter, dtype=F32) / quarter)
    phase_angle = position[:, None].astype(F32) * frequency[None, :]
    return (jnp.cos(phase_angle), jnp.sin(phase_angle))


def rotate(values, cosine, sine_part):
    quarter = cosine.shape[-1]
    first_half = values[..., :quarter]
    second = values[..., quarter : 2 * quarter]
    cos_rows = cosine[:, None, :]
    sin_rows = sine_part[:, None, :]
    return jnp.concatenate(
        [
            first_half * cos_rows - second * sin_rows,
            second * cos_rows + first_half * sin_rows,
            values[..., 2 * quarter :],
        ],
        axis=-1,
    )


def dot(a, b, da, db):
    return lax.dot_general(a, b, (((da,), (db,)), ((), ())), preferred_element_type=F32)


def shards(
    tokens,
    lengths,
    attn_gain,
    w_query,
    w_keyval,
    w_output,
    mlp_gain,
    w_gate,
    w_up,
    w_down,
    cotangent,
):
    t = lax.axis_index(T)
    piece = lax.axis_index(CONTEXT)
    head_dim = 256
    query_scale = head_dim ** (-0.5)
    seq_count = 2560
    padding = seq_count - lengths[0]
    row_start = piece * 160
    natural = row_start + jnp.arange(160, dtype=jnp.int32)
    turned = row_start + (jnp.arange(160, dtype=jnp.int32) + t * 80) % 160
    live_turned = turned >= padding
    live_mine = live_turned[:80, None]

    x_mine = to_piece_order(lax.dynamic_slice_in_dim(tokens[0], t * 80, 80, 0)).astype(F32)
    cot_mine = to_piece_order(lax.dynamic_slice_in_dim(cotangent[0], t * 80, 80, 0))
    grad_mine = jnp.where(live_mine, cot_mine, jnp.zeros_like(cot_mine))

    keyval_half = lax.dynamic_slice_in_dim(w_keyval, t * 256, 256, 1)
    gains = jnp.concatenate([attn_gain, mlp_gain])[None, :]
    gains = jnp.broadcast_to(jnp.pad(gains, ((0, 7), (0, 304)))[None], (4, 8, 384))
    attn_out = jnp.concatenate(
        [jnp.concatenate([quarters(w_query), quarters(keyval_half)], axis=2), gains], axis=1
    )
    attn_in = lax.all_to_all(attn_out, Y, 0, 0, tiled=True)
    gain_rows = attn_in[:, 40, :80].reshape(4, 2, 40).swapaxes(0, 1).reshape(1, 320)
    gain_block = jnp.pad(gain_rows, ((0, 15), (0, 64)))
    attn_block = jnp.concatenate([attn_in[:, :40].reshape(160, 384), gain_block], axis=0)
    attn_all = gather_context(attn_block).reshape(16, 176, 384)
    w_qkv = attn_all[:, :160].reshape(2560, 384)
    gain_one = attn_all[:, 160, :160].reshape(1, 2560).astype(F32)
    gain_two = attn_all[:, 160, 160:320].reshape(1, 2560).astype(F32)

    mlp_out_blocks = jnp.concatenate([quarters(w_gate), quarters(w_up), quarters(w_down)], axis=2)
    mlp_block = lax.all_to_all(mlp_out_blocks, Y, 0, 0, tiled=True).reshape(160, 2880)
    w_mlp = lax.all_gather(mlp_block, CONTEXT, axis=0, tiled=True)
    w_gate_up = w_mlp[:, :1920]
    w_down_all = w_mlp[:, 1920:]

    out_piece = gather_context(w_output).reshape(16, 40, 1280)
    w_out = placed(
        ring_blocks(out_piece, Y), Y, jnp.zeros((16, 4, 40, 1280), BF), 1, (0, 0, 0, 0)
    ).reshape(2560, 1280)

    inverse_one = inverse_root(x_mine)
    normed = gather_rows((x_mine * inverse_one * gain_one).astype(BF))
    projected = dot(normed, w_qkv, 1, 0).astype(BF)
    home = rows_home(projected)
    query_pre = joined(home[:, :, :320]).reshape(160, 5, head_dim).astype(F32)
    cosine, sine_part = angles(turned - padding, head_dim)
    queries = (rotate(query_pre, cosine, sine_part) * query_scale).astype(BF)
    keyval_turned = joined(home[:, :, 320:])
    keyval_own = jnp.where(
        t == 0, keyval_turned, jnp.concatenate([keyval_turned[80:], keyval_turned[:80]])
    )
    cosine_nat, sine_nat = angles(natural - padding, head_dim)
    keys_own = rotate(keyval_own[:, None].astype(F32), cosine_nat, sine_nat)[:, 0].astype(BF)
    kv_own = jnp.where(t == 0, keys_own, keyval_own)
    kv_mine = gather_context(kv_own)
    kv_other = shift(kv_mine, T, 1)
    keys = jnp.where(t == 0, kv_mine, kv_other)
    values = jnp.where(t == 0, kv_other, kv_mine)

    key_index = jnp.arange(seq_count, dtype=jnp.int32)
    offset = turned[:, None] - key_index[None, :]
    allowed = ((offset >= 0) & (offset < WINDOW) & (key_index >= padding)[None, :])[None]
    live = live_turned[None, :, None]
    scores = jnp.einsum("qhd,kd->hqk", queries, keys, preferred_element_type=F32)
    row_top = jnp.max(jnp.where(allowed, scores, NEGATIVE_FILL), axis=-1, keepdims=True)
    row_top = jnp.where(live, row_top, 0.0)
    weights_exp = jnp.where(allowed, jnp.exp(scores - row_top), 0.0)
    row_total = jnp.where(live, jnp.sum(weights_exp, axis=-1, keepdims=True), 1.0)
    prob = weights_exp / row_total
    prob_low = prob.astype(BF)
    attended = jnp.einsum("hqk,kd->qhd", prob_low, values, preferred_element_type=F32)
    attended = attended.reshape(160, 1280).astype(BF)
    attended_group = columns_out(quarters(attended))

    branch = dot(attended, w_out, 1, 1)
    hidden_mine = x_mine + branch[:80] + shift(branch[80:], T, 1)

    inverse_two = inverse_root(hidden_mine)
    normed_two = gather_rows((hidden_mine * inverse_two * gain_two).astype(BF))
    grad_group = gather_rows(grad_mine)
    gate_up = dot(normed_two, w_gate_up, 1, 0)
    gate_pre, up_pre = gate_up[:, :960], gate_up[:, 960:]
    activated, gelu_pull = jax.vjp(jax.nn.gelu, gate_pre)
    hidden = (activated * up_pre).astype(BF)
    grad_hidden = dot(grad_group, w_down_all, 1, 0)
    grad_gate = gelu_pull(grad_hidden * up_pre)[0].astype(BF)
    grad_up = (grad_hidden * activated).astype(BF)
    grad_gate_up = jnp.concatenate([grad_gate, grad_up], axis=1)
    grad_normed_two = scatter_rows(dot(grad_gate_up, w_gate_up, 1, 1))

    gate_up_part = dot(normed_two, grad_gate_up, 0, 0).astype(BF)
    down_part = dot(grad_group, hidden, 0, 0).astype(BF)
    mlp_part = jnp.concatenate([gate_up_part, down_part], axis=1)
    mlp_sum = lax.psum_scatter(mlp_part, CONTEXT, scatter_dimension=0, tiled=True)

    mlp_mine = scatter_rows(dot(hidden, w_down_all, 1, 1))
    block_mine = jnp.where(live_mine, hidden_mine + mlp_mine, 0.0).astype(BF)
    block_out = halves_home(from_piece_order(block_mine), t)

    grad_h_mine = grad_mine.astype(F32) + norm_back(
        grad_normed_two, hidden_mine, inverse_two, gain_two
    )
    branch_mine = grad_h_mine.astype(BF)
    branch_low = jnp.concatenate([branch_mine, shift(branch_mine, T, 1)])
    grad_attended = dot(branch_low, w_out, 1, 0).astype(BF).reshape(160, 5, head_dim)
    branch_group = gather_rows(branch_mine)
    output_part = dot(branch_group, attended_group, 0, 0)
    output_sum = scatter_context(output_part, BF)

    grad_prob = jnp.einsum("qhd,kd->hqk", grad_attended, values, preferred_element_type=F32)
    spread = jnp.sum(prob * grad_prob, axis=-1, keepdims=True)
    grad_scores = (prob * (grad_prob - spread)).astype(BF)
    grad_queries = jnp.einsum("hqk,kd->qhd", grad_scores, keys, preferred_element_type=F32)
    grad_query_pre = (
        rotate(grad_queries * query_scale, cosine, -sine_part).reshape(160, 1280).astype(BF)
    )
    grad_query_group = columns_out(quarters(grad_query_pre))
    grad_keys = jnp.einsum("hqk,qhd->kd", grad_scores, queries, preferred_element_type=F32)
    grad_values = jnp.einsum("hqk,qhd->kd", prob_low, grad_attended, preferred_element_type=F32)
    keep = jnp.where(t == 0, grad_keys, grad_values)
    give = jnp.where(t == 0, grad_values, grad_keys)
    kv_sum = scatter_context(keep + shift(give, T, 1), F32)
    keys_back = rotate(kv_sum[:, None], cosine_nat, -sine_nat)[:, 0]
    kv_back = jnp.where(t == 0, keys_back, kv_sum).astype(BF)
    kv_back = jnp.where(t == 0, kv_back, jnp.concatenate([kv_back[80:], kv_back[:80]]))
    grad_kv_group = columns_out(quarters(kv_back))
    grad_qkv_group = jnp.concatenate([grad_query_group, grad_kv_group], axis=1)
    grad_normed = scatter_rows(dot(grad_qkv_group, w_qkv, 1, 1))
    tokens_mine = grad_h_mine + norm_back(grad_normed, x_mine, inverse_one, gain_one)
    tokens_grad = halves_home(from_piece_order(tokens_mine.astype(BF)), t)

    qkv_part = dot(normed, grad_qkv_group, 0, 0)
    qkv_sum = scatter_context(qkv_part, BF)
    attn_sum = jnp.concatenate([qkv_sum, output_sum], axis=1).astype(BF)
    attn_home = lax.all_to_all(attn_sum.reshape(4, 40, 704), Y, 0, 0, tiled=True).astype(F32)
    query_grad = joined(attn_home[:, :, :320])
    kv_grad_half = joined(attn_home[:, :, 320:384])
    output_grad = joined(attn_home[:, :, 384:])
    kv_grad_other = shift(kv_grad_half, T, 1)
    keyval_grad = jnp.where(
        t == 0,
        jnp.concatenate([kv_grad_half, kv_grad_other], axis=1),
        jnp.concatenate([kv_grad_other, kv_grad_half], axis=1),
    )
    mlp_home = lax.all_to_all(mlp_sum.reshape(4, 40, 2880), Y, 0, 0, tiled=True).astype(F32)
    gate_grad = joined(mlp_home[:, :, :960])
    up_grad = joined(mlp_home[:, :, 960:1920])
    down_grad = joined(mlp_home[:, :, 1920:])

    one_part = jnp.sum(w_query.astype(F32) * query_grad, axis=1) + jnp.sum(
        keyval_half.astype(F32) * kv_grad_half, axis=1
    )
    two_part = jnp.sum(w_gate.astype(F32) * gate_grad + w_up.astype(F32) * up_grad, axis=1)
    both = jnp.stack([one_part, two_part])
    both = both + shift(both, T, 1)
    attn_gain_grad = both[0] / attn_gain.astype(F32)
    mlp_gain_grad = both[1] / mlp_gain.astype(F32)

    return (
        block_out[None],
        tokens_grad[None],
        attn_gain_grad,
        query_grad,
        keyval_grad,
        output_grad,
        mlp_gain_grad,
        gate_grad,
        up_grad,
        down_grad,
    )


def solution(mesh):
    torus = Mesh(
        mesh.devices.reshape(mesh.shape["shard"], 4, 4, mesh.shape["tensor"]),
        ("shard", "context_0", "context_1", "tensor"),
    )
    in_specs = (
        P("shard", CONTEXT, None),
        P("shard"),
        P(SHARD_CONTEXT),
        P(SHARD_CONTEXT, "tensor"),
        P(SHARD_CONTEXT, None),
        P(SHARD_CONTEXT, "tensor"),
        P(SHARD_CONTEXT),
        P(SHARD_CONTEXT, "tensor"),
        P(SHARD_CONTEXT, "tensor"),
        P(SHARD_CONTEXT, "tensor"),
        P("shard", CONTEXT, None),
    )
    out_specs = (
        P("shard", CONTEXT, None),
        P("shard", CONTEXT, None),
        P(SHARD_CONTEXT),
        P(SHARD_CONTEXT, "tensor"),
        P(SHARD_CONTEXT, None),
        P(SHARD_CONTEXT, "tensor"),
        P(SHARD_CONTEXT),
        P(SHARD_CONTEXT, "tensor"),
        P(SHARD_CONTEXT, "tensor"),
        P(SHARD_CONTEXT, "tensor"),
    )
    return jax.shard_map(
        shards, mesh=torus, in_specs=in_specs, out_specs=out_specs, check_vma=False
    )
```

```python
import functools

import jax
import jax.numpy as jnp
from jax import lax
from jax.experimental import pallas as pl
from jax.experimental.pallas import tpu as pltpu
from jax.sharding import Mesh
from jax.sharding import PartitionSpec as P

WINDOW = 2048
SHARD_CONTEXT = ("shard", "context_0", "context_1")
CONTEXT = ("context_0", "context_1")
PIECES = ("context_0", "context_1", "shard")
Y, X, Z, T = "shard", "context_0", "context_1", "tensor"
VMEM = pltpu.CompilerParams(vmem_limit_bytes=48 * 2**20)

EPSILON = 1e-06
NEGATIVE_FILL = -1e30
BF = jnp.bfloat16
F32 = jnp.float32


def shift(x, axis, by):
    n = lax.axis_size(axis)
    return lax.ppermute(x, axis, [(i, (i + by) % n) for i in range(n)])


def exchange(blocks, axis):
    return lax.all_to_all(blocks, axis, 0, 0, tiled=True)


def after(x, *others):
    return lax.optimization_barrier((x, *others))[0]


def ring_blocks(x, axis):
    return [x, shift(x, axis, -1), shift(x, axis, 2), shift(x, axis, 1)]


def place_kernel(axis, sign, lead, *refs):
    blocks, out, sems = refs[:-2], refs[-2], refs[-1]
    me = lax.axis_index(axis)
    copies = []
    for i, block in enumerate(blocks):
        first, rows, r = lead[i]
        j = lax.rem(me + (sign * r) % 4, 4)
        dst = out.at[j] if first is None else out.at[pl.ds(first, rows), j]
        copies.append(pltpu.make_async_copy(block, dst, sems.at[i]))
    for copy in copies:
        copy.start()
    for copy in copies:
        copy.wait()


def place(blocks, axis, shape, sign=1, lead=None):
    if lead is None:
        lead = [(None, 0, r) for r in range(4)]
    return pl.pallas_call(
        functools.partial(place_kernel, axis, sign, lead),
        out_shape=jax.ShapeDtypeStruct(shape, blocks[0].dtype),
        in_specs=[pl.BlockSpec(memory_space=pl.ANY)] * len(blocks),
        out_specs=pl.BlockSpec(memory_space=pl.ANY),
        scratch_shapes=[pltpu.SemaphoreType.DMA((len(blocks),))],
        compiler_params=VMEM,
    )(*blocks)


def gather_rows(mine):
    own = jnp.concatenate(ring_blocks(mine, Y), axis=0)
    return own, shift(own, T, 1)


def scatter_rows(own, other, weight, db):
    far = dot(other, weight, 1, db).astype(BF)
    low = (dot(own, weight, 1, db) + shift(far, T, 1).astype(F32)).astype(BF)
    total = low[:80].astype(F32)
    for r in (1, 3, 2):
        total = total + shift(low[80 * r : 80 * r + 80], Y, r).astype(F32)
    return total, low


def rows_home(own, other):
    blocks = []
    for r in range(4):
        block = jnp.concatenate([own[80 * r : 80 * r + 80], other[80 * r : 80 * r + 80]])
        blocks.append(shift(block, Y, r) if r else block)
    return place(blocks, Y, (4, *blocks[0].shape), sign=-1)


def columns_out(blocks):
    me = lax.axis_index(Y)
    got = [None] * 4
    for r in range(4):
        block = lax.dynamic_index_in_dim(blocks, (me + r) % 4, 0, keepdims=False)
        got[(4 - r) % 4] = shift(block, Y, r) if r else block
    return jnp.concatenate([b[:80] for b in got]), jnp.concatenate([b[80:] for b in got])


def gather_output(w_output):
    line = place(ring_blocks(w_output, X), X, (4, 40, 1280))
    lead = [(0, 4, r) for r in range(4)]
    plane = place(ring_blocks(line, Z), Z, (4, 4, 40, 1280), lead=lead).reshape(16, 40, 1280)
    before, behind = shift(plane, Y, 1), shift(plane, Y, -1)
    far_one, far_two = shift(before[:8], Y, 1), shift(behind[8:], Y, -1)
    lead = [(0, 16, 0), (0, 16, 1), (0, 16, 3), (0, 8, 2), (8, 8, 2)]
    blocks = (plane, behind, before, far_one, far_two)
    return place(blocks, Y, (16, 4, 40, 1280), lead=lead).reshape(2560, 1280)


def summed_over(parts, axis, dim):
    me = lax.axis_index(axis)
    total = lax.dynamic_index_in_dim(parts, me, dim, keepdims=False).astype(F32)
    for r in (1, 3, 2):
        block = lax.dynamic_index_in_dim(parts, (me + r) % 4, dim, keepdims=False)
        total = total + shift(block, axis, r).astype(F32)
    return total


def quarters(x):
    rows = x.shape[0]
    return x.reshape(rows, 4, -1).swapaxes(0, 1)


def joined(blocks):
    return blocks.swapaxes(0, 1).reshape(blocks.shape[1], -1)


def pack_kernel(q_ref, kv_ref, gains_ref, gate_ref, up_ref, down_ref, attn_ref, mlp_ref):
    attn_ref[...] = jnp.zeros_like(attn_ref)
    mlp_ref[...] = jnp.zeros_like(mlp_ref)
    for j in range(4):
        attn_ref[j, :40, :320] = q_ref[:, 320 * j : 320 * j + 320]
        attn_ref[j, :40, 320:] = kv_ref[:, 64 * j : 64 * j + 64]
        attn_ref[j, 40:48, :128] = gains_ref[...]
        mlp_ref[j, :, :960] = gate_ref[:, 960 * j : 960 * j + 960]
        mlp_ref[j, :, 1024:1984] = up_ref[:, 960 * j : 960 * j + 960]
        mlp_ref[j, :, 2048:3008] = down_ref[:, 960 * j : 960 * j + 960]


def pack(w_query, keyval_half, gains, w_gate, w_up, w_down):
    return pl.pallas_call(
        pack_kernel,
        out_shape=(
            jax.ShapeDtypeStruct((4, 48, 384), BF),
            jax.ShapeDtypeStruct((4, 40, 3072), BF),
        ),
        compiler_params=VMEM,
    )(w_query, keyval_half, gains, w_gate, w_up, w_down)


def mlp_grad_kernel(xa, xb, ya, yb, ga, gb, ha, hb, out):
    j = pl.program_id(1)

    def product(left_a, left_b, right_a, right_b):
        out[...] = (dot(left_a[...], right_a[...], 0, 0) + dot(left_b[...], right_b[...], 0, 0)).astype(BF)

    @pl.when(j < 2)
    def _():
        product(xa, xb, ga, gb)

    @pl.when(j == 2)
    def _():
        product(ya, yb, ha, hb)


def mlp_grads(normed, grads, gate_up, hidden):
    rows = 256
    left = pl.BlockSpec((320, rows), lambda i, j: (0, i))
    pair = pl.BlockSpec((320, 1024), lambda i, j: (0, jnp.minimum(j, 1)))
    whole = pl.BlockSpec((320, 1024), lambda i, j: (0, 0))
    return pl.pallas_call(
        mlp_grad_kernel,
        grid=(2560 // rows, 3),
        out_shape=jax.ShapeDtypeStruct((2560, 3072), BF),
        in_specs=[left, left, left, left, pair, pair, whole, whole],
        out_specs=pl.BlockSpec((rows, 1024), lambda i, j: (i, j)),
        compiler_params=VMEM,
        cost_estimate=pl.CostEstimate(flops=2 * 640 * 2560 * 3072, bytes_accessed=2 * 2560 * 3072, transcendentals=0),
    )(*normed, *grads, *gate_up, *hidden)


def to_piece_order(x):
    rows = x.shape[0]
    return x.reshape(rows, 4, 16, 40).swapaxes(1, 2).reshape(rows, 2560)


def from_piece_order(x):
    rows = x.shape[0]
    return x.reshape(rows, 16, 4, 40).swapaxes(1, 2).reshape(rows, 2560)


def halves_home(mine, t):
    other = shift(mine, T, 1)
    return jnp.where(t == 0, jnp.concatenate([mine, other]), jnp.concatenate([other, mine]))


def inverse_root(values):
    return lax.rsqrt(jnp.mean(values * values, axis=-1, keepdims=True) + EPSILON)


def norm_back(grad, values, inverse, gain):
    scaled = gain * grad
    return inverse * scaled - values * inverse**3 * jnp.mean(
        scaled * values, axis=-1, keepdims=True
    )


def angles(position, head_dim):
    quarter = head_dim // 4
    frequency = 10000.0 ** (-jnp.arange(quarter, dtype=F32) / quarter)
    phase_angle = position[:, None].astype(F32) * frequency[None, :]
    return (jnp.cos(phase_angle), jnp.sin(phase_angle))


def rotate(values, cosine, sine_part):
    quarter = cosine.shape[-1]
    first_half = values[..., :quarter]
    second = values[..., quarter : 2 * quarter]
    cos_rows = cosine[:, None, :]
    sin_rows = sine_part[:, None, :]
    return jnp.concatenate(
        [
            first_half * cos_rows - second * sin_rows,
            second * cos_rows + first_half * sin_rows,
            values[..., 2 * quarter :],
        ],
        axis=-1,
    )


def dot(a, b, da, db):
    return lax.dot_general(a, b, (((da,), (db,)), ((), ())), preferred_element_type=F32)


def feed_forward(gate_up, grad_hidden):
    gate_pre, up_pre = gate_up[:, :1024], gate_up[:, 1024:]
    activated, gelu_pull = jax.vjp(jax.nn.gelu, gate_pre)
    hidden = (activated * up_pre).astype(BF)
    grad_gate = gelu_pull(grad_hidden * up_pre)[0].astype(BF)
    grad_up = (grad_hidden * activated).astype(BF)
    return hidden, jnp.concatenate([grad_gate, grad_up], axis=1)


def shards(
    tokens,
    lengths,
    attn_gain,
    w_query,
    w_keyval,
    w_output,
    mlp_gain,
    w_gate,
    w_up,
    w_down,
    cotangent,
):
    t = lax.axis_index(T)
    piece = lax.axis_index(CONTEXT)
    head_dim = 256
    query_scale = head_dim ** (-0.5)
    seq_count = 2560
    padding = seq_count - lengths[0]
    row_start = piece * 160
    natural = row_start + jnp.arange(160, dtype=jnp.int32)
    turned = row_start + (jnp.arange(160, dtype=jnp.int32) + t * 80) % 160
    live_turned = turned >= padding
    live_mine = live_turned[:80, None]

    x_low = to_piece_order(lax.dynamic_slice_in_dim(tokens[0], t * 80, 80, 0))
    cot_mine = to_piece_order(lax.dynamic_slice_in_dim(cotangent[0], t * 80, 80, 0))
    grad_mine = jnp.where(live_mine, cot_mine, jnp.zeros_like(cot_mine))
    x_mine = x_low.astype(F32)
    x_halves = gather_rows(x_low)

    keyval_half = lax.dynamic_slice_in_dim(w_keyval, t * 256, 256, 1)
    gains = jnp.concatenate([attn_gain, mlp_gain])[None, :]
    gains = jnp.pad(gains, ((0, 7), (0, 48)))
    attn_blocks, mlp_blocks = pack(w_query, keyval_half, gains, w_gate, w_up, w_down)
    attn_copies = jnp.broadcast_to(attn_blocks[None], (16, 4, 48, 384)).reshape(64, 48, 384)
    attn_all = exchange(attn_copies, PIECES)
    w_qkv = attn_all[:, :40].reshape(2560, 384)
    gain_one = attn_all[:, 40, :40].reshape(1, 2560).astype(F32)
    gain_two = attn_all[:, 40, 40:80].reshape(1, 2560).astype(F32)
    me = lax.axis_index(Y)
    mlp_got = []
    for r in range(4):
        block = lax.dynamic_index_in_dim(mlp_blocks, (me + r) % 4, 0, keepdims=False)
        mlp_got.append(shift(block, Y, r) if r else block)
    mlp_block = place(mlp_got, Y, (4, 40, 3072), sign=-1).reshape(160, 3072)
    w_mlp = lax.all_gather(mlp_block, CONTEXT, axis=0, tiled=True)
    w_gate_up = w_mlp[:, :2048]
    w_down_all = w_mlp[:, 2048:]
    w_out = gather_output(after(w_output, mlp_blocks))

    normed, projected = [], []
    for x_half in x_halves:
        x_rows = x_half.astype(F32)
        normed.append((x_rows * inverse_root(x_rows) * gain_one).astype(BF))
        projected.append(dot(normed[-1], w_qkv, 1, 0).astype(BF))
    home = rows_home(*projected)
    query_pre = joined(home[:, :, :320]).reshape(160, 5, head_dim).astype(F32)
    cosine, sine_part = angles(turned - padding, head_dim)
    queries = (rotate(query_pre, cosine, sine_part) * query_scale).astype(BF)
    keyval_turned = joined(home[:, :, 320:])
    keyval_own = jnp.where(
        t == 0, keyval_turned, jnp.concatenate([keyval_turned[80:], keyval_turned[:80]])
    )
    cosine_nat, sine_nat = angles(natural - padding, head_dim)
    keys_own = rotate(keyval_own[:, None].astype(F32), cosine_nat, sine_nat)[:, 0].astype(BF)
    kv_own = jnp.where(t == 0, keys_own, keyval_own)
    kv_mine = exchange(jnp.broadcast_to(kv_own[None], (16, 160, 256)), CONTEXT).reshape(2560, 256)
    kv_other = shift(kv_mine, T, 1)
    keys = jnp.where(t == 0, kv_mine, kv_other)
    values = jnp.where(t == 0, kv_other, kv_mine)

    key_index = jnp.arange(seq_count, dtype=jnp.int32)
    offset = turned[:, None] - key_index[None, :]
    allowed = ((offset >= 0) & (offset < WINDOW) & (key_index >= padding)[None, :])[None]
    live = live_turned[None, :, None]
    scores = jnp.einsum("qhd,kd->hqk", queries, keys, preferred_element_type=F32)
    row_top = jnp.max(jnp.where(allowed, scores, NEGATIVE_FILL), axis=-1, keepdims=True)
    row_top = jnp.where(live, row_top, 0.0)
    weights_exp = jnp.where(allowed, jnp.exp(scores - row_top), 0.0)
    row_total = jnp.where(live, jnp.sum(weights_exp, axis=-1, keepdims=True), 1.0)
    prob = weights_exp / row_total
    prob_low = prob.astype(BF)
    attended = jnp.einsum("hqk,kd->qhd", prob_low, values, preferred_element_type=F32)
    attended = attended.reshape(160, 1280).astype(BF)

    branch = dot(attended, w_out, 1, 1)
    hidden_mine = x_mine + branch[:80] + shift(branch[80:], T, 1)

    inverse_two = inverse_root(hidden_mine)
    grad_halves = gather_rows(after(grad_mine, w_out))
    grad_halves = lax.optimization_barrier((*grad_halves, branch))[:2]
    normed_two = gather_rows((hidden_mine * inverse_two * gain_two).astype(BF))
    attended_halves = columns_out(quarters(after(attended, *normed_two)))
    hidden, grad_gate_up = [None, None], [None, None]
    for i in (0, 1):
        gate_up = dot(normed_two[i], w_gate_up, 1, 0)
        grad_hidden = dot(grad_halves[i], w_down_all, 1, 0)
        hidden[i], grad_gate_up[i] = feed_forward(gate_up, grad_hidden)
    grad_normed_two, normed_two_low = scatter_rows(*grad_gate_up, w_gate_up, 1)

    late = lax.optimization_barrier((*grad_gate_up, *hidden, normed_two_low))
    mlp_part = mlp_grads(normed_two, grad_halves, late[:2], late[2:4])
    mlp_sum = lax.psum_scatter(mlp_part, CONTEXT, scatter_dimension=0, tiled=True)

    grad_h_mine = grad_mine.astype(F32) + norm_back(
        grad_normed_two, hidden_mine, inverse_two, gain_two
    )
    branch_mine = grad_h_mine.astype(BF)
    branch_low = jnp.concatenate([branch_mine, shift(branch_mine, T, 1)])
    grad_attended = dot(branch_low, w_out, 1, 0).astype(BF).reshape(160, 5, head_dim)
    branch_halves = gather_rows(branch_mine)

    grad_prob = jnp.einsum("qhd,kd->hqk", grad_attended, values, preferred_element_type=F32)
    spread = jnp.sum(prob * grad_prob, axis=-1, keepdims=True)
    grad_scores = (prob * (grad_prob - spread)).astype(BF)
    grad_queries = jnp.einsum("hqk,kd->qhd", grad_scores, keys, preferred_element_type=F32)
    grad_query_pre = (
        rotate(grad_queries * query_scale, cosine, -sine_part).reshape(160, 1280).astype(BF)
    )
    grad_scores_late = after(grad_scores, grad_query_pre)
    grad_query_halves = columns_out(quarters(grad_query_pre))
    grad_keys = jnp.einsum(
        "hqk,qhd->kd", grad_scores_late, queries, preferred_element_type=F32
    )
    grad_values = jnp.einsum("hqk,qhd->kd", prob_low, grad_attended, preferred_element_type=F32)
    keep = jnp.where(t == 0, grad_keys, grad_values)
    give = jnp.where(t == 0, grad_values, grad_keys).astype(BF)
    kv_part = (keep + shift(give, T, 1).astype(F32)).astype(BF).reshape(4, 4, 160, 256)
    kv_line = summed_over(kv_part, X, 0).astype(BF)
    kv_sum = summed_over(kv_line, Z, 0)

    output_halves = lax.optimization_barrier((*branch_halves, kv_part))[:2]
    output_part = sum(dot(output_halves[i], attended_halves[i], 0, 0) for i in (0, 1))
    output_home = exchange(output_part.astype(BF).reshape(64, 40, 320), PIECES)

    keys_back = rotate(kv_sum[:, None], cosine_nat, -sine_nat)[:, 0]
    kv_back = jnp.where(t == 0, keys_back, kv_sum).astype(BF)
    kv_back = jnp.where(t == 0, kv_back, jnp.concatenate([kv_back[80:], kv_back[:80]]))
    grad_kv_halves = columns_out(quarters(kv_back))
    grad_qkv = [
        jnp.concatenate([q, kv], axis=1) for q, kv in zip(grad_query_halves, grad_kv_halves)
    ]
    qkv_part = sum(dot(normed[i], grad_qkv[i], 0, 0) for i in (0, 1))
    qkv_home = exchange(qkv_part.astype(BF).reshape(64, 40, 384), PIECES)
    grad_normed, _ = scatter_rows(*grad_qkv, w_qkv, 1)
    inverse_one = inverse_root(x_mine)
    tokens_mine = grad_h_mine + norm_back(grad_normed, x_mine, inverse_one, gain_one)
    tokens_grad = halves_home(from_piece_order(tokens_mine.astype(BF)), t)

    hidden_late = lax.optimization_barrier((*hidden, kv_part))[:2]
    mlp_mine, _ = scatter_rows(*hidden_late, w_down_all, 1)
    block_mine = jnp.where(live_mine, hidden_mine + mlp_mine, 0.0).astype(BF)
    block_out = halves_home(from_piece_order(block_mine), t)

    def owned(home):
        return joined(jnp.sum(home.reshape(16, 4, 40, -1).astype(F32), axis=0))

    query_grad = owned(qkv_home[:, :, :320])
    kv_grad_half = owned(qkv_home[:, :, 320:])
    output_grad = owned(output_home)
    kv_grad_other = shift(kv_grad_half, T, 1)
    keyval_grad = jnp.where(
        t == 0,
        jnp.concatenate([kv_grad_half, kv_grad_other], axis=1),
        jnp.concatenate([kv_grad_other, kv_grad_half], axis=1),
    )
    mlp_got = []
    mlp_rows = mlp_sum.reshape(4, 40, 3072)
    for r in range(4):
        block = lax.dynamic_index_in_dim(mlp_rows, (me + r) % 4, 0, keepdims=False)
        mlp_got.append(shift(block, Y, r) if r else block)
    mlp_home = place(mlp_got, Y, (4, 40, 3072), sign=-1).astype(F32)
    gate_grad = joined(mlp_home[:, :, :960])
    up_grad = joined(mlp_home[:, :, 1024:1984])
    down_grad = joined(mlp_home[:, :, 2048:3008])

    one_part = jnp.sum(w_query.astype(F32) * query_grad, axis=1) + jnp.sum(
        keyval_half.astype(F32) * kv_grad_half, axis=1
    )
    two_part = jnp.sum(w_gate.astype(F32) * gate_grad + w_up.astype(F32) * up_grad, axis=1)
    both = jnp.stack([one_part, two_part])
    both = both + shift(both, T, 1)
    attn_gain_grad = both[0] / attn_gain.astype(F32)
    mlp_gain_grad = both[1] / mlp_gain.astype(F32)

    return (
        block_out[None],
        tokens_grad[None],
        attn_gain_grad,
        query_grad,
        keyval_grad,
        output_grad,
        mlp_gain_grad,
        gate_grad,
        up_grad,
        down_grad,
    )


def solution(mesh):
    torus = Mesh(
        mesh.devices.reshape(mesh.shape["shard"], 4, 4, mesh.shape["tensor"]),
        ("shard", "context_0", "context_1", "tensor"),
    )
    in_specs = (
        P("shard", CONTEXT, None),
        P("shard"),
        P(SHARD_CONTEXT),
        P(SHARD_CONTEXT, "tensor"),
        P(SHARD_CONTEXT, None),
        P(SHARD_CONTEXT, "tensor"),
        P(SHARD_CONTEXT),
        P(SHARD_CONTEXT, "tensor"),
        P(SHARD_CONTEXT, "tensor"),
        P(SHARD_CONTEXT, "tensor"),
        P("shard", CONTEXT, None),
    )
    out_specs = (
        P("shard", CONTEXT, None),
        P("shard", CONTEXT, None),
        P(SHARD_CONTEXT),
        P(SHARD_CONTEXT, "tensor"),
        P(SHARD_CONTEXT, None),
        P(SHARD_CONTEXT, "tensor"),
        P(SHARD_CONTEXT),
        P(SHARD_CONTEXT, "tensor"),
        P(SHARD_CONTEXT, "tensor"),
        P(SHARD_CONTEXT, "tensor"),
    )
    return jax.shard_map(
        shards, mesh=torus, in_specs=in_specs, out_specs=out_specs, check_vma=False
    )
```

```python
import functools

import jax
import jax.numpy as jnp
from jax import lax
from jax.experimental import pallas as pl
from jax.experimental.pallas import tpu as pltpu
from jax.sharding import Mesh
from jax.sharding import PartitionSpec as P

WINDOW = 2048
SHARD_CONTEXT = ("shard", "context_0", "context_1")
CONTEXT = ("context_0", "context_1")
PIECES = ("context_0", "context_1", "shard")
Y, X, Z, T = "shard", "context_0", "context_1", "tensor"
VMEM = pltpu.CompilerParams(vmem_limit_bytes=48 * 2**20)
ANYWHERE = pl.BlockSpec(memory_space=pl.ANY)

EPSILON = 1e-06
NEGATIVE_FILL = -1e30
BF = jnp.bfloat16
F32 = jnp.float32


def shift(x, axis, by):
    n = lax.axis_size(axis)
    return lax.ppermute(x, axis, [(i, (i + by) % n) for i in range(n)])


def exchange(blocks, axis):
    return lax.all_to_all(blocks, axis, 0, 0, tiled=True)


def nothing(*refs):
    pass


def after(x, *others):
    return pl.pallas_call(
        nothing,
        out_shape=jax.ShapeDtypeStruct(x.shape, x.dtype),
        in_specs=[ANYWHERE] * (1 + len(others)),
        out_specs=ANYWHERE,
        input_output_aliases={0: 0},
        compiler_params=VMEM,
    )(x, *others)


def small_trip(x):
    return shift(x.reshape(-1, x.shape[-1])[:8, :128], T, 1)


def ring_blocks(x, axis):
    return [x, shift(x, axis, -1), shift(x, axis, 2), shift(x, axis, 1)]


def place_kernel(axis, sign, *refs):
    blocks, out, sems = refs[:-2], refs[-2], refs[-1]
    me = lax.axis_index(axis)
    copies = []
    for r, block in enumerate(blocks):
        j = lax.rem(me + (sign * r) % 4, 4)
        copies.append(pltpu.make_async_copy(block, out.at[j], sems.at[r]))
    for copy in copies:
        copy.start()
    for copy in copies:
        copy.wait()


def place(blocks, axis, sign=1):
    return pl.pallas_call(
        functools.partial(place_kernel, axis, sign),
        out_shape=jax.ShapeDtypeStruct((4, *blocks[0].shape), blocks[0].dtype),
        in_specs=[pl.BlockSpec(memory_space=pl.ANY)] * 4,
        out_specs=pl.BlockSpec(memory_space=pl.ANY),
        scratch_shapes=[pltpu.SemaphoreType.DMA((4,))],
        compiler_params=VMEM,
    )(*blocks)


def gather_rows(mine):
    own = exchange(jnp.broadcast_to(mine[None], (4, *mine.shape)), Y).reshape(320, -1)
    return jnp.concatenate([own, shift(own, T, 1)])


def scatter_parts(parts, weight, db):
    far = dot(parts[320:], weight, 1, db).astype(BF)
    near = dot(parts[:320], weight, 1, db) + shift(far, T, 1).astype(F32)
    return near.astype(BF).reshape(4, 80, -1)


def scatter_sum(low):
    return jnp.sum(exchange(low, Y).astype(F32), axis=0)


def scatter_sum_permutes(low):
    me = lax.axis_index(Y)
    total = lax.dynamic_index_in_dim(low, me, 0, keepdims=False).astype(F32)
    for r in (1, 3, 2):
        block = lax.dynamic_index_in_dim(low, (me + r) % 4, 0, keepdims=False)
        total = total + shift(block, Y, r).astype(F32)
    return total


def by_half(blocks):
    cols = blocks.shape[2]
    return blocks.reshape(4, 2, 80, cols).swapaxes(0, 1).reshape(640, cols)


def columns_out(x):
    return by_half(exchange(quarters(x), Y))


def columns_out_permutes(x):
    me = lax.axis_index(Y)
    blocks = quarters(x)
    got = []
    for r in range(4):
        block = lax.dynamic_index_in_dim(blocks, (me + r) % 4, 0, keepdims=False)
        got.append(shift(block, Y, r) if r else block)
    return by_half(place(got, Y, sign=-1))


def assemble_kernel(own_ref, behind_ref, before_ref, far_one_ref, far_two_ref, _, out_ref):
    me = lax.axis_index(Y)
    i = pl.program_id(0)
    out_ref[0, me] = own_ref[0]
    out_ref[0, lax.rem(me + 1, 4)] = behind_ref[0]
    out_ref[0, lax.rem(me + 3, 4)] = before_ref[0]

    @pl.when(i < 8)
    def _():
        out_ref[0, lax.rem(me + 2, 4)] = far_one_ref[0]

    @pl.when(i >= 8)
    def _():
        out_ref[0, lax.rem(me + 2, 4)] = far_two_ref[0]


def assemble(blocks, first):
    cols = blocks[0].shape[-1]
    whole = pl.BlockSpec((1, 40, cols), lambda i: (i, 0, 0))
    low = pl.BlockSpec((1, 40, cols), lambda i: (jnp.minimum(i, 7), 0, 0))
    high = pl.BlockSpec((1, 40, cols), lambda i: (jnp.maximum(i, 8) - 8, 0, 0))
    return pl.pallas_call(
        assemble_kernel,
        grid=(16,),
        out_shape=jax.ShapeDtypeStruct((16, 4, 40, cols), BF),
        in_specs=[whole, whole, whole, low, high, ANYWHERE],
        out_specs=pl.BlockSpec((1, 4, 40, cols), lambda i: (i, 0, 0, 0)),
        compiler_params=VMEM,
    )(*blocks, first).reshape(2560, cols)


def quarters(x):
    rows = x.shape[0]
    return x.reshape(rows, 4, -1).swapaxes(0, 1)


def joined(blocks):
    return blocks.swapaxes(0, 1).reshape(blocks.shape[1], -1)


def pack_attention_kernel(q_ref, kv_ref, gains_ref, attn_ref):
    attn_ref[...] = jnp.zeros_like(attn_ref)
    for j in range(4):
        attn_ref[j, :40, :320] = q_ref[:, 320 * j : 320 * j + 320]
        attn_ref[j, :40, 320:] = kv_ref[:, 64 * j : 64 * j + 64]
        attn_ref[j, 40:48, :128] = gains_ref[...]


def pack_attention(w_query, keyval_half, gains):
    return pl.pallas_call(
        pack_attention_kernel,
        out_shape=jax.ShapeDtypeStruct((4, 48, 384), BF),
        compiler_params=VMEM,
    )(w_query, keyval_half, gains)


def pack_mlp_kernel(gate_ref, up_ref, down_ref, _, mlp_ref):
    mlp_ref[...] = jnp.zeros_like(mlp_ref)
    for j in range(4):
        mlp_ref[j, :, :960] = gate_ref[:, 960 * j : 960 * j + 960]
        mlp_ref[j, :, 1024:1984] = up_ref[:, 960 * j : 960 * j + 960]
        mlp_ref[j, :, 2048:3008] = down_ref[:, 960 * j : 960 * j + 960]


def pack_mlp(w_gate, w_up, w_down, first):
    whole = pl.BlockSpec(memory_space=pltpu.VMEM)
    return pl.pallas_call(
        pack_mlp_kernel,
        out_shape=jax.ShapeDtypeStruct((4, 40, 3072), BF),
        in_specs=[whole, whole, whole, ANYWHERE],
        compiler_params=VMEM,
    )(w_gate, w_up, w_down, first)


def mlp_grad_kernel(x_ref, y_ref, gate_up_ref, hidden_ref, _, out_ref):
    j = pl.program_id(0)

    @pl.when(j < 2)
    def _():
        out_ref[...] = dot(x_ref[...], gate_up_ref[...], 0, 0).astype(BF)

    @pl.when(j == 2)
    def _():
        out_ref[...] = dot(y_ref[...], hidden_ref[...], 0, 0).astype(BF)


def mlp_grads(normed, grads, gate_up, hidden, first):
    rows = 512
    return pl.pallas_call(
        mlp_grad_kernel,
        grid=(3, 2560 // rows),
        out_shape=jax.ShapeDtypeStruct((2560, 3072), BF),
        in_specs=[
            pl.BlockSpec((640, rows), lambda j, i: (0, jnp.where(j < 2, i, 4))),
            pl.BlockSpec((640, rows), lambda j, i: (0, jnp.where(j < 2, 0, i))),
            pl.BlockSpec((640, 1024), lambda j, i: (0, jnp.minimum(j, 1))),
            pl.BlockSpec((640, 1024), lambda j, i: (0, 0)),
            ANYWHERE,
        ],
        out_specs=pl.BlockSpec((rows, 1024), lambda j, i: (i, j)),
        compiler_params=VMEM,
        cost_estimate=pl.CostEstimate(
            flops=2 * 640 * 2560 * 3072, bytes_accessed=2 * 2560 * 3072, transcendentals=0
        ),
    )(normed, grads, gate_up, hidden, first)


def to_piece_order(x):
    rows = x.shape[0]
    return x.reshape(rows, 4, 16, 40).swapaxes(1, 2).reshape(rows, 2560)


def inverse_root(values):
    return lax.rsqrt(jnp.mean(values * values, axis=-1, keepdims=True) + EPSILON)


def norm_back(grad, values, inverse, gain):
    scaled = gain * grad
    return inverse * scaled - values * inverse**3 * jnp.mean(
        scaled * values, axis=-1, keepdims=True
    )


def angles(position, head_dim):
    quarter = head_dim // 4
    frequency = 10000.0 ** (-jnp.arange(quarter, dtype=F32) / quarter)
    phase_angle = position[:, None].astype(F32) * frequency[None, :]
    return (jnp.cos(phase_angle), jnp.sin(phase_angle))


def rotate(values, cosine, sine_part):
    quarter = cosine.shape[-1]
    first_half = values[..., :quarter]
    second = values[..., quarter : 2 * quarter]
    cos_rows = cosine[:, None, :]
    sin_rows = sine_part[:, None, :]
    return jnp.concatenate(
        [
            first_half * cos_rows - second * sin_rows,
            second * cos_rows + first_half * sin_rows,
            values[..., 2 * quarter :],
        ],
        axis=-1,
    )


def dot(a, b, da, db):
    return lax.dot_general(a, b, (((da,), (db,)), ((), ())), preferred_element_type=F32)


def project_kernel(own_ref, other_ref, gain_ref, weight_ref, normed_ref, grad_ref, out_ref):
    def rows(block):
        x = block[:80].astype(F32)
        normed = (x * inverse_root(x) * gain_ref[...]).astype(BF)
        normed_ref[...] = normed
        grad_ref[...] = block[80:]
        out_ref[0] = dot(normed, weight_ref[...], 1, 0).astype(BF)

    i = pl.program_id(0)

    @pl.when(i < 4)
    def _():
        rows(own_ref[0])

    @pl.when(i >= 4)
    def _():
        rows(other_ref[0])


def project(own, other, gain, weight):
    return pl.pallas_call(
        project_kernel,
        grid=(8,),
        out_shape=(
            jax.ShapeDtypeStruct((640, 2560), BF),
            jax.ShapeDtypeStruct((640, 2560), BF),
            jax.ShapeDtypeStruct((4, 160, 384), BF),
        ),
        in_specs=[
            pl.BlockSpec((1, 160, 2560), lambda i: (jnp.minimum(i, 3), 0, 0)),
            pl.BlockSpec((1, 160, 2560), lambda i: (jnp.maximum(i, 4) - 4, 0, 0)),
            pl.BlockSpec((1, 2560), lambda i: (0, 0)),
            pl.BlockSpec((2560, 384), lambda i: (0, 0)),
        ],
        out_specs=(
            pl.BlockSpec((80, 2560), lambda i: (i, 0)),
            pl.BlockSpec((80, 2560), lambda i: (i, 0)),
            pl.BlockSpec((1, 80, 384), lambda i: (i % 4, i // 4, 0)),
        ),
        compiler_params=VMEM,
    )(own, other, gain, weight)


def owned_kernel(home_ref, out_ref):
    for j in range(4):
        total = home_ref[j].astype(F32)
        for p in range(1, 16):
            total = total + home_ref[4 * p + j].astype(F32)
        out_ref[:, 320 * j : 320 * j + 320] = total


def owned(home):
    return pl.pallas_call(
        owned_kernel, out_shape=jax.ShapeDtypeStruct((40, 1280), F32), compiler_params=VMEM
    )(home)


def owned_qkv_kernel(home_ref, query_ref, keyval_ref, query_out, keyval_out, gain_out):
    gain = jnp.zeros((40, 1), F32)
    for j in range(4):
        total = home_ref[j].astype(F32)
        for p in range(1, 16):
            total = total + home_ref[4 * p + j].astype(F32)
        query_out[:, 320 * j : 320 * j + 320] = total[:, :320]
        keyval_out[:, 64 * j : 64 * j + 64] = total[:, 320:]
    for weight, grad in ((query_ref, query_out), (keyval_ref, keyval_out)):
        gain += jnp.sum(weight[...].astype(F32) * grad[...], axis=1, keepdims=True)
    gain_out[...] = jnp.broadcast_to(gain, (40, 128))


def owned_qkv(home, w_query, keyval_half):
    return pl.pallas_call(
        owned_qkv_kernel,
        out_shape=(
            jax.ShapeDtypeStruct((40, 1280), F32),
            jax.ShapeDtypeStruct((40, 256), F32),
            jax.ShapeDtypeStruct((40, 128), F32),
        ),
        compiler_params=VMEM,
    )(home, w_query, keyval_half)


def owned_mlp_kernel(b0, b1, b2, b3, gate_ref, up_ref, gate_out, up_out, down_out, gain_out, held):
    me = lax.axis_index(Y)
    for r, block in enumerate((b0, b1, b2, b3)):
        held[lax.rem(me + 4 - r, 4)] = block[...]
    for j in range(4):
        columns = slice(960 * j, 960 * j + 960)
        gate_out[:, columns] = held[j, :, :960].astype(F32)
        up_out[:, columns] = held[j, :, 1024:1984].astype(F32)
        down_out[:, columns] = held[j, :, 2048:3008].astype(F32)
    products = gate_ref[...].astype(F32) * gate_out[...] + up_ref[...].astype(F32) * up_out[...]
    gain_out[...] = jnp.broadcast_to(jnp.sum(products, axis=1, keepdims=True), (40, 128))


def owned_mlp(blocks, w_gate, w_up):
    wide = jax.ShapeDtypeStruct((40, 3840), F32)
    return pl.pallas_call(
        owned_mlp_kernel,
        out_shape=(wide, wide, wide, jax.ShapeDtypeStruct((40, 128), F32)),
        scratch_shapes=[pltpu.VMEM((4, 40, 3072), BF)],
        compiler_params=VMEM,
    )(*blocks, w_gate, w_up)


def token_order_kernel(x_ref, out_ref):
    for j in range(4):
        for p in range(16):
            to, at = 40 * (16 * j + p), 40 * (4 * p + j)
            out_ref[:, to : to + 40] = x_ref[:, at : at + 40].astype(BF)


def from_piece_order(x):
    return pl.pallas_call(
        token_order_kernel, out_shape=jax.ShapeDtypeStruct(x.shape, BF), compiler_params=VMEM
    )(x)


def halves_kernel(mine_ref, other_ref, _, out_ref):
    at = 80 * lax.axis_index(T)
    out_ref[pl.ds(pl.multiple_of(at, 16), 80), :] = mine_ref[...]
    out_ref[pl.ds(pl.multiple_of(80 - at, 16), 80), :] = other_ref[...]


def halves_home(mine, first):
    whole = pl.BlockSpec(memory_space=pltpu.VMEM)
    return pl.pallas_call(
        halves_kernel,
        out_shape=jax.ShapeDtypeStruct((160, mine.shape[1]), BF),
        in_specs=[whole, whole, ANYWHERE],
        compiler_params=VMEM,
    )(mine, shift(mine, T, 1), first)


def feed_forward(gate_up, grad_hidden):
    gate_pre, up_pre = gate_up[:, :1024], gate_up[:, 1024:]
    activated, gelu_pull = jax.vjp(jax.nn.gelu, gate_pre)
    hidden = (activated * up_pre).astype(BF)
    grad_gate = gelu_pull(grad_hidden * up_pre)[0].astype(BF)
    grad_up = (grad_hidden * activated).astype(BF)
    return hidden, jnp.concatenate([grad_gate, grad_up], axis=1)


def shards(
    tokens,
    lengths,
    attn_gain,
    w_query,
    w_keyval,
    w_output,
    mlp_gain,
    w_gate,
    w_up,
    w_down,
    cotangent,
):
    t = lax.axis_index(T)
    me = lax.axis_index(Y)
    piece = lax.axis_index(CONTEXT)
    head_dim = 256
    query_scale = head_dim ** (-0.5)
    seq_count = 2560
    padding = seq_count - lengths[0]
    row_start = piece * 160
    natural = row_start + jnp.arange(160, dtype=jnp.int32)
    turned = row_start + (jnp.arange(160, dtype=jnp.int32) + t * 80) % 160
    live_turned = turned >= padding
    live_mine = live_turned[:80, None]

    out_piece = lax.all_gather(w_output, CONTEXT, axis=0, tiled=True).reshape(16, 40, 1280)

    x_low = to_piece_order(lax.dynamic_slice_in_dim(tokens[0], t * 80, 80, 0))
    cot_mine = to_piece_order(lax.dynamic_slice_in_dim(cotangent[0], t * 80, 80, 0))
    grad_mine = jnp.where(live_mine, cot_mine, jnp.zeros_like(cot_mine))
    x_mine = x_low.astype(F32)
    both_blocks = ring_blocks(jnp.concatenate([x_low, grad_mine]), Y)
    both_own = place(both_blocks, Y)
    both_other = shift(both_own, T, 1)

    keyval_half = lax.dynamic_slice_in_dim(w_keyval, t * 256, 256, 1)
    gains = jnp.concatenate([attn_gain, mlp_gain])[None, :]
    gains = jnp.pad(gains, ((0, 7), (0, 48)))
    attn_blocks = pack_attention(w_query, keyval_half, gains)
    attn_copies = jnp.broadcast_to(attn_blocks[None], (16, 4, 48, 384)).reshape(64, 48, 384)
    attn_all = exchange(attn_copies, PIECES)
    w_qkv = attn_all[:, :40].reshape(2560, 384)
    gain_one = attn_all[:, 40, :40].reshape(1, 2560).astype(F32)
    gain_two = attn_all[:, 40, 40:80].reshape(1, 2560).astype(F32)
    mlp_blocks = pack_mlp(w_gate, w_up, w_down, both_blocks[1])
    mlp_got = []
    for r in range(4):
        block = lax.dynamic_index_in_dim(mlp_blocks, (me + r) % 4, 0, keepdims=False)
        mlp_got.append(shift(block, Y, r) if r else block)
    mlp_block = place(mlp_got, Y, sign=-1).reshape(160, 3072)
    w_mlp = lax.all_gather(mlp_block, CONTEXT, axis=0, tiled=True)
    w_gate_up = w_mlp[:, :2048]
    w_down_all = w_mlp[:, 2048:]
    before, behind = shift(out_piece, Y, 1), shift(out_piece, Y, -1)
    far_one, far_two = shift(before[:8], Y, 1), shift(behind[8:], Y, -1)

    normed, grad_group, projected = project(both_own, both_other, gain_one, w_qkv)
    home = exchange(projected, Y)
    keyval_turned = joined(home[:, :, 320:])
    keyval_own = jnp.where(
        t == 0, keyval_turned, jnp.concatenate([keyval_turned[80:], keyval_turned[:80]])
    )
    cosine_nat, sine_nat = angles(natural - padding, head_dim)
    keys_own = rotate(keyval_own[:, None].astype(F32), cosine_nat, sine_nat)[:, 0].astype(BF)
    kv_own = jnp.where(t == 0, keys_own, keyval_own)
    kv_mine = exchange(jnp.broadcast_to(kv_own[None], (16, 160, 256)), CONTEXT).reshape(2560, 256)
    kv_other = shift(kv_mine, T, 1)
    keys = jnp.where(t == 0, kv_mine, kv_other)
    values = jnp.where(t == 0, kv_other, kv_mine)
    query_pre = joined(home[:, :, :320]).reshape(160, 5, head_dim).astype(F32)
    cosine, sine_part = angles(turned - padding, head_dim)
    queries = (rotate(query_pre, cosine, sine_part) * query_scale).astype(BF)

    key_index = jnp.arange(seq_count, dtype=jnp.int32)
    offset = turned[:, None] - key_index[None, :]
    allowed = ((offset >= 0) & (offset < WINDOW) & (key_index >= padding)[None, :])[None]
    live = live_turned[None, :, None]
    scores = jnp.einsum("qhd,kd->hqk", queries, keys, preferred_element_type=F32)
    row_top = jnp.max(jnp.where(allowed, scores, NEGATIVE_FILL), axis=-1, keepdims=True)
    row_top = jnp.where(live, row_top, 0.0)
    weights_exp = jnp.where(allowed, jnp.exp(scores - row_top), 0.0)
    row_total = jnp.where(live, jnp.sum(weights_exp, axis=-1, keepdims=True), 1.0)
    prob = weights_exp / row_total
    prob_low = prob.astype(BF)
    attended = jnp.einsum("hqk,kd->qhd", prob_low, values, preferred_element_type=F32)
    attended = attended.reshape(160, 1280).astype(BF)

    w_out = assemble((out_piece, behind, before, far_one, far_two), attended)
    branch = dot(attended, w_out, 1, 1)
    hidden_mine = x_mine + branch[:80] + shift(branch[80:], T, 1)

    inverse_two = inverse_root(hidden_mine)
    normed_two = gather_rows((hidden_mine * inverse_two * gain_two).astype(BF))
    attended_group = columns_out(after(attended, normed_two))
    gate_up = dot(normed_two, w_gate_up, 1, 0)
    grad_hidden = dot(grad_group, w_down_all, 1, 0)
    hidden, grad_gate_up = feed_forward(gate_up, grad_hidden)
    normed_two_low = scatter_parts(grad_gate_up, w_gate_up, 1)
    grad_normed_two = scatter_sum(normed_two_low)

    trip = small_trip(normed_two_low)
    mlp_part = mlp_grads(normed_two, grad_group, grad_gate_up, hidden, trip)
    mlp_sum = lax.psum_scatter(mlp_part, CONTEXT, scatter_dimension=0, tiled=True)
    mlp_low = scatter_parts(after(hidden, mlp_part), w_down_all, 1)

    grad_h_mine = grad_mine.astype(F32) + norm_back(
        grad_normed_two, hidden_mine, inverse_two, gain_two
    )
    branch_mine = grad_h_mine.astype(BF)
    branch_low = jnp.concatenate([branch_mine, shift(branch_mine, T, 1)])
    grad_attended = dot(branch_low, w_out, 1, 0).astype(BF).reshape(160, 5, head_dim)
    branch_own = place(ring_blocks(branch_mine, Y), Y).reshape(320, 2560)
    branch_group = jnp.concatenate([branch_own, shift(branch_own, T, 1)])

    grad_prob = jnp.einsum("qhd,kd->hqk", grad_attended, values, preferred_element_type=F32)
    spread = jnp.sum(prob * grad_prob, axis=-1, keepdims=True)
    grad_scores = (prob * (grad_prob - spread)).astype(BF)
    grad_keys = jnp.einsum("hqk,qhd->kd", grad_scores, queries, preferred_element_type=F32)
    grad_values = jnp.einsum("hqk,qhd->kd", prob_low, grad_attended, preferred_element_type=F32)
    keep = jnp.where(t == 0, grad_keys, grad_values)
    give = jnp.where(t == 0, grad_values, grad_keys).astype(BF)
    grad_queries = jnp.einsum("hqk,kd->qhd", grad_scores, keys, preferred_element_type=F32)
    grad_query_pre = (
        rotate(grad_queries * query_scale, cosine, -sine_part).reshape(160, 1280).astype(BF)
    )
    kv_part = (keep + shift(give, T, 1).astype(F32)).astype(BF).reshape(16, 160, 256)
    kv_sum = jnp.sum(exchange(kv_part, CONTEXT).astype(F32), axis=0)
    grad_query_group = columns_out_permutes(grad_query_pre)

    late_group = after(attended_group, small_trip(kv_part))
    output_part = dot(branch_group, late_group, 0, 0).astype(BF).reshape(64, 40, 320)
    output_home = exchange(after(output_part, kv_sum), PIECES)
    mlp_mine = scatter_sum_permutes(after(mlp_low, output_part))
    block_mine = jnp.where(live_mine, hidden_mine + mlp_mine, 0.0)

    keys_back = rotate(kv_sum[:, None], cosine_nat, -sine_nat)[:, 0]
    kv_back = jnp.where(t == 0, keys_back, kv_sum).astype(BF)
    kv_back = jnp.where(t == 0, kv_back, jnp.concatenate([kv_back[80:], kv_back[:80]]))
    grad_kv_group = columns_out_permutes(kv_back)
    grad_qkv = jnp.concatenate([grad_query_group, grad_kv_group], axis=1)
    qkv_part = dot(normed, grad_qkv, 0, 0).astype(BF).reshape(64, 40, 384)
    qkv_home = exchange(qkv_part, PIECES)
    grad_normed = scatter_sum_permutes(scatter_parts(grad_qkv, w_qkv, 1))
    inverse_one = inverse_root(x_mine)
    tokens_mine = grad_h_mine + norm_back(grad_normed, x_mine, inverse_one, gain_one)
    output_grad = owned(output_home)
    mlp_got = []
    mlp_rows = mlp_sum.reshape(4, 40, 3072)
    for r in range(4):
        block = lax.dynamic_index_in_dim(mlp_rows, (me + r) % 4, 0, keepdims=False)
        mlp_got.append(shift(block, Y, r) if r else block)
    gate_grad, up_grad, down_grad, two_part = owned_mlp(mlp_got, w_gate, w_up)
    block_out = halves_home(from_piece_order(block_mine), kv_sum)
    tokens_grad = halves_home(from_piece_order(tokens_mine), two_part)

    query_grad, kv_half, one_part = owned_qkv(qkv_home, w_query, keyval_half)
    mine = jnp.concatenate([kv_half, one_part, two_part], axis=1)
    other = shift(mine, T, 1)
    kv_other = other[:, :256]
    keyval_grad = jnp.where(
        t == 0,
        jnp.concatenate([kv_half, kv_other], axis=1),
        jnp.concatenate([kv_other, kv_half], axis=1),
    )
    attn_gain_grad = (mine[:, 256] + other[:, 256]) / attn_gain.astype(F32)
    mlp_gain_grad = (mine[:, 384] + other[:, 384]) / mlp_gain.astype(F32)

    return (
        block_out[None],
        tokens_grad[None],
        attn_gain_grad,
        query_grad,
        keyval_grad,
        output_grad,
        mlp_gain_grad,
        gate_grad,
        up_grad,
        down_grad,
    )


def solution(mesh):
    torus = Mesh(
        mesh.devices.reshape(mesh.shape["shard"], 4, 4, mesh.shape["tensor"]),
        ("shard", "context_0", "context_1", "tensor"),
    )
    in_specs = (
        P("shard", CONTEXT, None),
        P("shard"),
        P(SHARD_CONTEXT),
        P(SHARD_CONTEXT, "tensor"),
        P(SHARD_CONTEXT, None),
        P(SHARD_CONTEXT, "tensor"),
        P(SHARD_CONTEXT),
        P(SHARD_CONTEXT, "tensor"),
        P(SHARD_CONTEXT, "tensor"),
        P(SHARD_CONTEXT, "tensor"),
        P("shard", CONTEXT, None),
    )
    out_specs = (
        P("shard", CONTEXT, None),
        P("shard", CONTEXT, None),
        P(SHARD_CONTEXT),
        P(SHARD_CONTEXT, "tensor"),
        P(SHARD_CONTEXT, None),
        P(SHARD_CONTEXT, "tensor"),
        P(SHARD_CONTEXT),
        P(SHARD_CONTEXT, "tensor"),
        P(SHARD_CONTEXT, "tensor"),
        P(SHARD_CONTEXT, "tensor"),
    )
    return jax.shard_map(
        shards, mesh=torus, in_specs=in_specs, out_specs=out_specs, check_vma=False
    )
```

```python
import functools

import jax
import jax.numpy as jnp
from jax import lax
from jax.experimental import pallas as pl
from jax.experimental.pallas import tpu as pltpu
from jax.sharding import Mesh
from jax.sharding import PartitionSpec as P

WINDOW = 2048
SHARD_CONTEXT = ("shard", "context_0", "context_1")
CONTEXT = ("context_0", "context_1")
PIECES = ("context_0", "context_1", "shard")
Y, X, Z, T = "shard", "context_0", "context_1", "tensor"
VMEM = pltpu.CompilerParams(vmem_limit_bytes=48 * 2**20)
ANYWHERE = pl.BlockSpec(memory_space=pl.ANY)

EPSILON = 1e-06
NEGATIVE_FILL = -1e30
BF = jnp.bfloat16
F32 = jnp.float32


def shift(x, axis, by):
    n = lax.axis_size(axis)
    return lax.ppermute(x, axis, [(i, (i + by) % n) for i in range(n)])


def exchange(blocks, axis):
    return lax.all_to_all(blocks, axis, 0, 0, tiled=True)


def nothing(*refs):
    pass


def after(x, *others):
    return pl.pallas_call(
        nothing,
        out_shape=jax.ShapeDtypeStruct(x.shape, x.dtype),
        in_specs=[ANYWHERE] * (1 + len(others)),
        out_specs=ANYWHERE,
        input_output_aliases={0: 0},
        compiler_params=VMEM,
    )(x, *others)


def small_trip(x, *others):
    corner = x.reshape(-1, x.shape[-1])[:8, :128]
    return shift(after(corner, *others) if others else corner, T, 1)


def ring_blocks(x, axis):
    return [x, shift(x, axis, -1), shift(x, axis, 2), shift(x, axis, 1)]


def place_kernel(axis, sign, *refs):
    blocks, out = refs[:4], refs[-1]
    me = lax.axis_index(axis)
    for r, block in enumerate(blocks):
        out[lax.rem(me + (sign * r) % 4, 4)] = block[...]


def place(blocks, axis, *first, sign=1):
    whole = pl.BlockSpec(memory_space=pltpu.VMEM)
    return pl.pallas_call(
        functools.partial(place_kernel, axis, sign),
        out_shape=jax.ShapeDtypeStruct((4, *blocks[0].shape), blocks[0].dtype),
        in_specs=[whole] * 4 + [ANYWHERE] * len(first),
        out_specs=whole,
        compiler_params=VMEM,
    )(*blocks, *first)


def gather_rows(mine, *first):
    own = place(ring_blocks(mine, Y), Y, *first).reshape(320, -1)
    return own, shift(own, T, 1)


def rows_kernel(count, *refs):
    lefts, rights, (far_ref, near_ref) = refs[:count], refs[count : 2 * count], refs[-2:]
    total = dot(lefts[0][...], rights[0][...], 1, 1)
    for left, right in zip(lefts[1:], rights[1:]):
        total = total + dot(left[...], right[...], 1, 1)
    near_ref[...] = total[:320].astype(BF)
    far_ref[...] = total[320:].astype(BF)


def row_products(lefts, weight, at, width, *first):
    rows, count, n = 256, len(lefts), weight.shape[0]
    half = jax.ShapeDtypeStruct((320, n), BF)
    return pl.pallas_call(
        functools.partial(rows_kernel, count),
        grid=(n // rows,),
        out_shape=(half, half),
        in_specs=[pl.BlockSpec((640, width), lambda i: (0, 0))] * count
        + [pl.BlockSpec((rows, width), lambda i, j=j: (i, at + j)) for j in range(count)]
        + [ANYWHERE] * len(first),
        out_specs=(pl.BlockSpec((320, rows), lambda i: (0, i)),) * 2,
        compiler_params=VMEM,
    )(*lefts, *[weight] * count, *first)


def scatter_parts(lefts, weight, at, width, *first):
    far, near = row_products(lefts, weight, at, width, *first)
    return (near.astype(F32) + shift(far, T, 1).astype(F32)).astype(BF).reshape(4, 80, -1)


def scatter_blocks(low):
    me = lax.axis_index(Y)
    return [lax.dynamic_index_in_dim(low, (me + r) % 4, 0, keepdims=False) for r in range(4)]


def scatter_sum(blocks):
    return scatter_total(blocks[0], [shift(blocks[r], Y, r) for r in (1, 3, 2)])


def scatter_total(own, got):
    total = own.astype(F32)
    for block in got:
        total = total + block.astype(F32)
    return total


def outer_kernel(x_ref, g_ref, y_ref, h_ref, out_ref):
    split = g_ref.shape[1]
    out_ref[:, :split] = dot(x_ref[...], g_ref[...], 0, 0).astype(BF)
    out_ref[:, split:] = dot(y_ref[...], h_ref[...], 0, 0).astype(BF)


def outer(x, g, y, h):
    rows, n, cols = 512, x.shape[1], g.shape[1] + h.shape[1]
    left = pl.BlockSpec((640, rows), lambda i: (0, i))
    right = [pl.BlockSpec((640, a.shape[1]), lambda i: (0, 0)) for a in (g, h)]
    return pl.pallas_call(
        outer_kernel,
        grid=(n // rows,),
        out_shape=jax.ShapeDtypeStruct((n, cols), BF),
        in_specs=[left, right[0], left, right[1]],
        out_specs=pl.BlockSpec((rows, cols), lambda i: (i, 0)),
        compiler_params=VMEM,
    )(x, g, y, h)


def summed_over(parts, axis, dim):
    me = lax.axis_index(axis)
    own, *rest = [
        lax.dynamic_index_in_dim(parts, (me + r) % 4, dim, keepdims=False) for r in range(4)
    ]
    return scatter_total(own, [shift(rest[r - 1], axis, r) for r in (1, 3, 2)]).astype(BF)


def scatter_context(parts):
    grid = parts.reshape(4, 4, 160, -1)
    one = summed_over(grid[:, :, :80], X, 0)
    two = summed_over(grid[:, :, 80:], Z, 1)
    return jnp.concatenate([summed_over(one, Z, 0), summed_over(two, X, 0)])


def to_owners(sums):
    me = lax.axis_index(Y)
    rows = sums.reshape(4, 40, -1)
    got = []
    for r in range(4):
        block = lax.dynamic_index_in_dim(rows, (me + r) % 4, 0, keepdims=False)
        got.append(shift(block, Y, r) if r else block)
    return got


def by_half(blocks):
    cols = blocks.shape[2]
    return blocks.reshape(4, 2, 80, cols).swapaxes(0, 1).reshape(640, cols)


def columns_out(x):
    me = lax.axis_index(Y)
    blocks = quarters(x)
    got = []
    for r in range(4):
        block = lax.dynamic_index_in_dim(blocks, (me + r) % 4, 0, keepdims=False)
        got.append(shift(block, Y, r) if r else block)
    return by_half(place(got, Y, sign=-1))


def quarters(x):
    rows = x.shape[0]
    return x.reshape(rows, 4, -1).swapaxes(0, 1)


def joined(blocks):
    return blocks.swapaxes(0, 1).reshape(blocks.shape[1], -1)


def pack_attention_kernel(q_ref, kv_ref, gains_ref, _, attn_ref):
    attn_ref[...] = jnp.zeros_like(attn_ref)
    for j in range(4):
        attn_ref[j, :40, :320] = q_ref[:, 320 * j : 320 * j + 320]
        attn_ref[j, :40, 320:] = kv_ref[:, 64 * j : 64 * j + 64]
        attn_ref[j, 40:48, :128] = gains_ref[...]


def pack_attention(w_query, keyval_half, gains, first):
    whole = pl.BlockSpec(memory_space=pltpu.VMEM)
    return pl.pallas_call(
        pack_attention_kernel,
        out_shape=jax.ShapeDtypeStruct((4, 48, 384), BF),
        in_specs=[whole, whole, whole, ANYWHERE],
        compiler_params=VMEM,
    )(w_query, keyval_half, gains, first)


def pack_mlp_kernel(gate_ref, up_ref, down_ref, mlp_ref):
    mlp_ref[...] = jnp.zeros_like(mlp_ref)
    for j in range(4):
        mlp_ref[j, :, :960] = gate_ref[:, 960 * j : 960 * j + 960]
        mlp_ref[j, :, 1024:1984] = up_ref[:, 960 * j : 960 * j + 960]
        mlp_ref[j, :, 2048:3008] = down_ref[:, 960 * j : 960 * j + 960]


def pack_mlp(w_gate, w_up, w_down):
    return pl.pallas_call(
        pack_mlp_kernel,
        out_shape=jax.ShapeDtypeStruct((4, 40, 3072), BF),
        compiler_params=VMEM,
    )(w_gate, w_up, w_down)


def mlp_grad_kernel(x_ref, y_ref, gate_ref, up_ref, hidden_ref, *rest):
    out_ref = rest[-1]
    j = pl.program_id(0)

    @pl.when(j == 0)
    def _():
        out_ref[...] = dot(x_ref[...], gate_ref[...], 0, 0).astype(BF)

    @pl.when(j == 1)
    def _():
        out_ref[...] = dot(x_ref[...], up_ref[...], 0, 0).astype(BF)

    @pl.when(j == 2)
    def _():
        out_ref[...] = dot(y_ref[...], hidden_ref[...], 0, 0).astype(BF)


def mlp_grads(normed, grads, gate, up, hidden, *first):
    rows = 512
    whole = pl.BlockSpec((640, 1024), lambda j, i: (0, 0))
    return pl.pallas_call(
        mlp_grad_kernel,
        grid=(3, 2560 // rows),
        out_shape=jax.ShapeDtypeStruct((2560, 3072), BF),
        in_specs=[
            pl.BlockSpec((640, rows), lambda j, i: (0, jnp.where(j < 2, i, 4))),
            pl.BlockSpec((640, rows), lambda j, i: (0, jnp.where(j < 2, 0, i))),
            whole,
            whole,
            whole,
        ]
        + [ANYWHERE] * len(first),
        out_specs=pl.BlockSpec((rows, 1024), lambda j, i: (i, j)),
        compiler_params=VMEM,
    )(normed, grads, gate, up, hidden, *first)


def feed_forward_kernel(x_ref, y_ref, gate_ref, up_ref, down_ref, hidden_out, gate_out, up_out):
    gate = dot(x_ref[...], gate_ref[...], 1, 0)
    up = dot(x_ref[...], up_ref[...], 1, 0)
    grad = dot(y_ref[...], down_ref[...], 1, 0)
    scale = 0.7978845608028654
    square = gate * gate
    bent = jnp.tanh(scale * gate * (1.0 + 0.044715 * square))
    share = 0.5 * (1.0 + bent)
    slope = share + 0.5 * gate * (1.0 - bent * bent) * scale * (1.0 + 0.134145 * square)
    active = gate * share
    hidden_out[...] = (active * up).astype(BF)
    gate_out[...] = (grad * up * slope).astype(BF)
    up_out[...] = (grad * active).astype(BF)


def feed_forward(x, y, w_mlp):
    cols = 256
    steps = 1024 // cols
    part = jax.ShapeDtypeStruct((640, 1024), BF)
    whole = pl.BlockSpec((640, 2560), lambda j: (0, 0))
    out = pl.BlockSpec((640, cols), lambda j: (0, j))
    return pl.pallas_call(
        feed_forward_kernel,
        grid=(steps,),
        out_shape=(part, part, part),
        in_specs=[whole, whole]
        + [pl.BlockSpec((2560, cols), lambda j, k=k: (0, k * steps + j)) for k in range(3)],
        out_specs=(out, out, out),
        compiler_params=VMEM,
    )(x, y, w_mlp, w_mlp, w_mlp)


def to_piece_order(x):
    rows = x.shape[0]
    return x.reshape(rows, 4, 16, 40).swapaxes(1, 2).reshape(rows, 2560)


def inverse_root(values):
    return lax.rsqrt(jnp.mean(values * values, axis=-1, keepdims=True) + EPSILON)


def norm_back(grad, values, inverse, gain):
    scaled = gain * grad
    return inverse * scaled - values * inverse**3 * jnp.mean(
        scaled * values, axis=-1, keepdims=True
    )


def angles(position, head_dim):
    quarter = head_dim // 4
    frequency = 10000.0 ** (-jnp.arange(quarter, dtype=F32) / quarter)
    phase_angle = position[:, None].astype(F32) * frequency[None, :]
    return (jnp.cos(phase_angle), jnp.sin(phase_angle))


def rotate(values, cosine, sine_part):
    quarter = cosine.shape[-1]
    first_half = values[..., :quarter]
    second = values[..., quarter : 2 * quarter]
    cos_rows = cosine[:, None, :]
    sin_rows = sine_part[:, None, :]
    return jnp.concatenate(
        [
            first_half * cos_rows - second * sin_rows,
            second * cos_rows + first_half * sin_rows,
            values[..., 2 * quarter :],
        ],
        axis=-1,
    )


def dot(a, b, da, db):
    return lax.dot_general(a, b, (((da,), (db,)), ((), ())), preferred_element_type=F32)


def project_kernel(own_ref, other_ref, gain_ref, weight_ref, normed_ref, out_ref):
    def rows(block):
        x = block[...].astype(F32)
        normed = (x * inverse_root(x) * gain_ref[...]).astype(BF)
        normed_ref[...] = normed
        out_ref[0] = dot(normed, weight_ref[...], 1, 0).astype(BF)

    i = pl.program_id(0)

    @pl.when(i < 4)
    def _():
        rows(own_ref)

    @pl.when(i >= 4)
    def _():
        rows(other_ref)


def project(own, other, gain, weight):
    return pl.pallas_call(
        project_kernel,
        grid=(8,),
        out_shape=(
            jax.ShapeDtypeStruct((640, 2560), BF),
            jax.ShapeDtypeStruct((4, 160, 384), BF),
        ),
        in_specs=[
            pl.BlockSpec((80, 2560), lambda i: (jnp.minimum(i, 3), 0)),
            pl.BlockSpec((80, 2560), lambda i: (jnp.maximum(i, 4) - 4, 0)),
            pl.BlockSpec((1, 2560), lambda i: (0, 0)),
            pl.BlockSpec((2560, 384), lambda i: (0, 0)),
        ],
        out_specs=(
            pl.BlockSpec((80, 2560), lambda i: (i, 0)),
            pl.BlockSpec((1, 80, 384), lambda i: (i % 4, i // 4, 0)),
        ),
        compiler_params=VMEM,
    )(own, other, gain, weight)


def owned_kernel(b0, b1, b2, b3, query_ref, keyval_ref, *rest):
    query_out, keyval_out, output_out, gain_out, held = rest[-5:]
    me = lax.axis_index(Y)
    for r, block in enumerate((b0, b1, b2, b3)):
        held[lax.rem(me + 4 - r, 4)] = block[...]
    for j in range(4):
        total = held[j].astype(F32)
        query_out[:, 320 * j : 320 * j + 320] = total[:, :320]
        keyval_out[:, 64 * j : 64 * j + 64] = total[:, 320:384]
        output_out[:, 320 * j : 320 * j + 320] = total[:, 384:]
    gain = jnp.zeros((40, 1), F32)
    for weight, grad in ((query_ref, query_out), (keyval_ref, keyval_out)):
        gain += jnp.sum(weight[...].astype(F32) * grad[...], axis=1, keepdims=True)
    gain_out[...] = jnp.broadcast_to(gain, (40, 128))


def owned(blocks, w_query, keyval_half, *first):
    whole = pl.BlockSpec(memory_space=pltpu.VMEM)
    return pl.pallas_call(
        owned_kernel,
        in_specs=[whole] * 6 + [ANYWHERE] * len(first),
        out_shape=(
            jax.ShapeDtypeStruct((40, 1280), F32),
            jax.ShapeDtypeStruct((40, 256), F32),
            jax.ShapeDtypeStruct((40, 1280), F32),
            jax.ShapeDtypeStruct((40, 128), F32),
        ),
        scratch_shapes=[pltpu.VMEM((4, 40, 704), BF)],
        compiler_params=VMEM,
    )(*blocks, w_query, keyval_half, *first)


def owned_mlp_kernel(b0, b1, b2, b3, gate_ref, up_ref, gate_out, up_out, down_out, gain_out, held):
    me = lax.axis_index(Y)
    for r, block in enumerate((b0, b1, b2, b3)):
        held[lax.rem(me + 4 - r, 4)] = block[...]
    for j in range(4):
        columns = slice(960 * j, 960 * j + 960)
        gate_out[:, columns] = held[j, :, :960].astype(F32)
        up_out[:, columns] = held[j, :, 1024:1984].astype(F32)
        down_out[:, columns] = held[j, :, 2048:3008].astype(F32)
    products = gate_ref[...].astype(F32) * gate_out[...] + up_ref[...].astype(F32) * up_out[...]
    gain_out[...] = jnp.broadcast_to(jnp.sum(products, axis=1, keepdims=True), (40, 128))


def owned_mlp(blocks, w_gate, w_up):
    wide = jax.ShapeDtypeStruct((40, 3840), F32)
    return pl.pallas_call(
        owned_mlp_kernel,
        out_shape=(wide, wide, wide, jax.ShapeDtypeStruct((40, 128), F32)),
        scratch_shapes=[pltpu.VMEM((4, 40, 3072), BF)],
        compiler_params=VMEM,
    )(*blocks, w_gate, w_up)


def token_order_kernel(x_ref, out_ref):
    for j in range(4):
        for p in range(16):
            to, at = 40 * (16 * j + p), 40 * (4 * p + j)
            out_ref[:, to : to + 40] = x_ref[:, at : at + 40].astype(BF)


def from_piece_order(x):
    return pl.pallas_call(
        token_order_kernel, out_shape=jax.ShapeDtypeStruct(x.shape, BF), compiler_params=VMEM
    )(x)


def halves_kernel(mine_ref, other_ref, out_ref):
    at = 80 * lax.axis_index(T)
    out_ref[pl.ds(pl.multiple_of(at, 16), 80), :] = mine_ref[...]
    out_ref[pl.ds(pl.multiple_of(80 - at, 16), 80), :] = other_ref[...]


def halves_home(mine):
    return pl.pallas_call(
        halves_kernel,
        out_shape=jax.ShapeDtypeStruct((160, mine.shape[1]), BF),
        compiler_params=VMEM,
    )(mine, shift(mine, T, 1))


def shards(
    tokens,
    lengths,
    attn_gain,
    w_query,
    w_keyval,
    w_output,
    mlp_gain,
    w_gate,
    w_up,
    w_down,
    cotangent,
):
    t = lax.axis_index(T)
    me = lax.axis_index(Y)
    piece = lax.axis_index(CONTEXT)
    head_dim = 256
    query_scale = head_dim ** (-0.5)
    seq_count = 2560
    padding = seq_count - lengths[0]
    row_start = piece * 160
    natural = row_start + jnp.arange(160, dtype=jnp.int32)
    turned = row_start + (jnp.arange(160, dtype=jnp.int32) + t * 80) % 160
    live_turned = turned >= padding
    live_mine = live_turned[:80, None]

    w_out = lax.all_gather(w_output, PIECES, axis=0, tiled=True)

    x_low = to_piece_order(lax.dynamic_slice_in_dim(tokens[0], t * 80, 80, 0))
    cot_mine = to_piece_order(lax.dynamic_slice_in_dim(cotangent[0], t * 80, 80, 0))
    grad_mine = jnp.where(live_mine, cot_mine, jnp.zeros_like(cot_mine))
    x_mine = x_low.astype(F32)
    keyval_half = lax.dynamic_slice_in_dim(w_keyval, t * 256, 256, 1)
    gains = jnp.concatenate([attn_gain, mlp_gain])[None, :]
    gains = jnp.pad(gains, ((0, 7), (0, 48)))
    attn_blocks = pack_attention(w_query, keyval_half, gains, small_trip(x_low))
    attn_copies = jnp.broadcast_to(attn_blocks[None], (16, 4, 48, 384)).reshape(64, 48, 384)
    attn_all = exchange(attn_copies, PIECES)
    w_qkv = attn_all[:, :40].reshape(2560, 384)
    gain_one = attn_all[:, 40, :40].reshape(1, 2560).astype(F32)
    gain_two = attn_all[:, 40, 40:80].reshape(1, 2560).astype(F32)
    x_own, x_other = gather_rows(x_low, attn_all)
    mlp_blocks = pack_mlp(w_gate, w_up, w_down)
    mlp_got = to_owners(mlp_blocks)
    mlp_block = place(mlp_got, Y, x_own, sign=-1).reshape(160, 3072)
    w_mlp = lax.all_gather(mlp_block, CONTEXT, axis=0, tiled=True)

    normed, projected = project(x_own, x_other, gain_one, w_qkv)
    grad_own, grad_other = gather_rows(after(grad_mine, projected))
    home = exchange(projected, Y)
    keyval_turned = joined(home[:, :, 320:])
    keyval_own = jnp.where(
        t == 0, keyval_turned, jnp.concatenate([keyval_turned[80:], keyval_turned[:80]])
    )
    cosine_nat, sine_nat = angles(natural - padding, head_dim)
    keys_own = rotate(keyval_own[:, None].astype(F32), cosine_nat, sine_nat)[:, 0].astype(BF)
    kv_own = jnp.where(t == 0, keys_own, keyval_own)
    kv_mine = exchange(jnp.broadcast_to(kv_own[None], (16, 160, 256)), CONTEXT).reshape(2560, 256)
    grad_group = jnp.concatenate([grad_own, grad_other])
    kv_other = shift(kv_mine, T, 1)
    keys = jnp.where(t == 0, kv_mine, kv_other)
    values = jnp.where(t == 0, kv_other, kv_mine)
    query_pre = joined(home[:, :, :320]).reshape(160, 5, head_dim).astype(F32)
    cosine, sine_part = angles(turned - padding, head_dim)
    queries = (rotate(query_pre, cosine, sine_part) * query_scale).astype(BF)

    key_index = jnp.arange(seq_count, dtype=jnp.int32)
    offset = turned[:, None] - key_index[None, :]
    allowed = ((offset >= 0) & (offset < WINDOW) & (key_index >= padding)[None, :])[None]
    live = live_turned[None, :, None]
    scores = jnp.einsum("qhd,kd->hqk", queries, keys, preferred_element_type=F32)
    row_top = jnp.max(jnp.where(allowed, scores, NEGATIVE_FILL), axis=-1, keepdims=True)
    row_top = jnp.where(live, row_top, 0.0)
    weights_exp = jnp.where(allowed, jnp.exp(scores - row_top), 0.0)
    row_total = jnp.where(live, jnp.sum(weights_exp, axis=-1, keepdims=True), 1.0)
    prob = weights_exp / row_total
    prob_low = prob.astype(BF)
    attended = jnp.einsum("hqk,kd->qhd", prob_low, values, preferred_element_type=F32)
    attended = attended.reshape(160, 1280).astype(BF)

    branch = dot(attended, w_out, 1, 1)
    hidden_mine = x_mine + branch[:80] + shift(branch[80:], T, 1)

    inverse_two = inverse_root(hidden_mine)
    normed_two_mine = (hidden_mine * inverse_two * gain_two).astype(BF)
    normed_two = jnp.concatenate(gather_rows(after(normed_two_mine, grad_group)))
    hidden, grad_gate, grad_up = feed_forward(normed_two, grad_group, w_mlp)
    normed_two_low = scatter_parts((grad_gate, grad_up), w_mlp, 0, 1024)

    normed_two_blocks = scatter_blocks(normed_two_low)
    got = [shift(normed_two_blocks[r], Y, r) for r in (1, 3, 2)]
    trip = small_trip(normed_two_low, *normed_two_blocks[1:])
    mlp_low = scatter_parts((hidden,), w_mlp, 2, 1024, trip)
    attended_group = columns_out(attended)
    mlp_part = mlp_grads(
        normed_two, grad_group, grad_gate, grad_up, hidden, *got[:2], mlp_low, attended_group
    )
    mlp_sum = lax.psum_scatter(mlp_part, CONTEXT, scatter_dimension=0, tiled=True)
    grad_normed_two = scatter_total(after(normed_two_blocks[0], mlp_part), got)

    grad_h_mine = grad_mine.astype(F32) + norm_back(
        grad_normed_two, hidden_mine, inverse_two, gain_two
    )
    branch_mine = grad_h_mine.astype(BF)
    branch_low = jnp.concatenate([branch_mine, shift(branch_mine, T, 1)])
    grad_attended = dot(branch_low, w_out, 1, 0).astype(BF).reshape(160, 5, head_dim)
    branch_own, branch_other = gather_rows(branch_mine)
    branch_group = jnp.concatenate([branch_own, branch_other])

    grad_prob = jnp.einsum("qhd,kd->hqk", grad_attended, values, preferred_element_type=F32)
    spread = jnp.sum(prob * grad_prob, axis=-1, keepdims=True)
    grad_scores = (prob * (grad_prob - spread)).astype(BF)
    grad_keys = jnp.einsum("hqk,qhd->kd", grad_scores, queries, preferred_element_type=F32)
    grad_values = jnp.einsum("hqk,qhd->kd", prob_low, grad_attended, preferred_element_type=F32)
    keep = jnp.where(t == 0, grad_keys, grad_values)
    give = jnp.where(t == 0, grad_values, grad_keys).astype(BF)
    grad_queries = jnp.einsum("hqk,kd->qhd", grad_scores, keys, preferred_element_type=F32)
    grad_query_pre = (
        rotate(grad_queries * query_scale, cosine, -sine_part).reshape(160, 1280).astype(BF)
    )
    kv_part = (keep + shift(give, T, 1).astype(F32)).astype(BF).reshape(16, 160, 256)
    kv_part = after(kv_part, grad_query_pre)
    kv_home = after(exchange(kv_part, CONTEXT), branch_group)
    kv_sum = jnp.sum(kv_home.astype(F32), axis=0)
    grad_query_group = columns_out(grad_query_pre)

    keys_back = rotate(kv_sum[:, None], cosine_nat, -sine_nat)[:, 0]
    kv_back = jnp.where(t == 0, keys_back, kv_sum).astype(BF)
    kv_back = jnp.where(t == 0, kv_back, jnp.concatenate([kv_back[80:], kv_back[:80]]))
    grad_kv_group = columns_out(kv_back)
    grad_qkv = jnp.concatenate([grad_query_group, grad_kv_group], axis=1)
    normed_low = scatter_parts((grad_qkv,), w_qkv, 0, 384)
    normed_blocks = scatter_blocks(normed_low)
    part = outer(normed, grad_qkv, branch_group, attended_group)
    home = to_owners(scatter_context(part))

    mlp_mine = scatter_sum(scatter_blocks(after(mlp_low, *normed_blocks[1:])))
    block_mine = jnp.where(live_mine, hidden_mine + mlp_mine, 0.0)

    grad_normed = scatter_sum(normed_blocks)
    inverse_one = inverse_root(x_mine)
    tokens_mine = grad_h_mine + norm_back(grad_normed, x_mine, inverse_one, gain_one)
    gate_grad, up_grad, down_grad, two_part = owned_mlp(to_owners(mlp_sum), w_gate, w_up)
    block_out = halves_home(from_piece_order(block_mine))
    tokens_grad = halves_home(from_piece_order(tokens_mine))

    query_grad, kv_half, output_grad, one_part = owned(
        home, w_query, keyval_half, two_part, block_out, tokens_grad
    )
    mine = jnp.concatenate([kv_half, one_part, two_part], axis=1)
    other = shift(mine, T, 1)
    kv_other = other[:, :256]
    keyval_grad = jnp.where(
        t == 0,
        jnp.concatenate([kv_half, kv_other], axis=1),
        jnp.concatenate([kv_other, kv_half], axis=1),
    )
    attn_gain_grad = (mine[:, 256] + other[:, 256]) / attn_gain.astype(F32)
    mlp_gain_grad = (mine[:, 384] + other[:, 384]) / mlp_gain.astype(F32)

    return (
        block_out[None],
        tokens_grad[None],
        attn_gain_grad,
        query_grad,
        keyval_grad,
        output_grad,
        mlp_gain_grad,
        gate_grad,
        up_grad,
        down_grad,
    )


def solution(mesh):
    torus = Mesh(
        mesh.devices.reshape(mesh.shape["shard"], 4, 4, mesh.shape["tensor"]),
        ("shard", "context_0", "context_1", "tensor"),
    )
    in_specs = (
        P("shard", CONTEXT, None),
        P("shard"),
        P(SHARD_CONTEXT),
        P(SHARD_CONTEXT, "tensor"),
        P(SHARD_CONTEXT, None),
        P(SHARD_CONTEXT, "tensor"),
        P(SHARD_CONTEXT),
        P(SHARD_CONTEXT, "tensor"),
        P(SHARD_CONTEXT, "tensor"),
        P(SHARD_CONTEXT, "tensor"),
        P("shard", CONTEXT, None),
    )
    out_specs = (
        P("shard", CONTEXT, None),
        P("shard", CONTEXT, None),
        P(SHARD_CONTEXT),
        P(SHARD_CONTEXT, "tensor"),
        P(SHARD_CONTEXT, None),
        P(SHARD_CONTEXT, "tensor"),
        P(SHARD_CONTEXT),
        P(SHARD_CONTEXT, "tensor"),
        P(SHARD_CONTEXT, "tensor"),
        P(SHARD_CONTEXT, "tensor"),
    )
    return jax.shard_map(
        shards, mesh=torus, in_specs=in_specs, out_specs=out_specs, check_vma=False
    )
```

```python
import functools

import jax
import jax.numpy as jnp
from jax import lax
from jax.experimental import pallas as pl
from jax.experimental.pallas import tpu as pltpu
from jax.sharding import Mesh
from jax.sharding import PartitionSpec as P

WINDOW = 2048
SHARD_CONTEXT = ("shard", "context_0", "context_1")
CONTEXT = ("context_0", "context_1")
PIECES = ("context_0", "context_1", "shard")
Y, X, Z, T = "shard", "context_0", "context_1", "tensor"
VMEM = pltpu.CompilerParams(vmem_limit_bytes=48 * 2**20)
ANYWHERE = pl.BlockSpec(memory_space=pl.ANY)
FREE = pl.CostEstimate(flops=0, bytes_accessed=0, transcendentals=0)

EPSILON = 1e-06
NEGATIVE_FILL = -1e30
BF = jnp.bfloat16
F32 = jnp.float32


def shift(x, axis, by):
    n = lax.axis_size(axis)
    return lax.ppermute(x, axis, [(i, (i + by) % n) for i in range(n)])


def exchange(blocks, axis):
    return lax.all_to_all(blocks, axis, 0, 0, tiled=True)


def nothing(*refs):
    pass


def after(x, *others):
    return pl.pallas_call(
        nothing,
        out_shape=jax.ShapeDtypeStruct(x.shape, x.dtype),
        in_specs=[ANYWHERE] * (1 + len(others)),
        out_specs=ANYWHERE,
        input_output_aliases={0: 0},
        compiler_params=VMEM,
        cost_estimate=FREE,
    )(x, *others)


def small_trip(x, *others):
    corner = x.reshape(-1, x.shape[-1])[:8, :128]
    return shift(after(corner, *others) if others else corner, T, 1)


def ring_blocks(x, axis):
    return [x, shift(x, axis, -1), shift(x, axis, 2), shift(x, axis, 1)]


def place_kernel(axis, sign, *refs):
    blocks, out = refs[:4], refs[-1]
    me = lax.axis_index(axis)
    for r, block in enumerate(blocks):
        out[lax.rem(me + (sign * r) % 4, 4)] = block[...]


def place(blocks, axis, *first, sign=1):
    whole = pl.BlockSpec(memory_space=pltpu.VMEM)
    return pl.pallas_call(
        functools.partial(place_kernel, axis, sign),
        out_shape=jax.ShapeDtypeStruct((4, *blocks[0].shape), blocks[0].dtype),
        in_specs=[whole] * 4 + [ANYWHERE] * len(first),
        out_specs=whole,
        compiler_params=VMEM,
        cost_estimate=FREE,
    )(*blocks, *first)


def gather_rows(mine, *first):
    own = place(ring_blocks(mine, Y), Y, *first).reshape(320, -1)
    return own, shift(own, T, 1)


def rows_kernel(count, *refs):
    lefts, rights, (far_ref, near_ref) = refs[:count], refs[count : 2 * count], refs[-2:]
    total = dot(lefts[0][...], rights[0][...], 1, 1)
    for left, right in zip(lefts[1:], rights[1:]):
        total = total + dot(left[...], right[...], 1, 1)
    near_ref[...] = total[:320].astype(BF)
    far_ref[...] = total[320:].astype(BF)


def row_products(lefts, weight, at, width, *first):
    rows, count, n = 256, len(lefts), weight.shape[0]
    half = jax.ShapeDtypeStruct((320, n), BF)
    return pl.pallas_call(
        functools.partial(rows_kernel, count),
        grid=(n // rows,),
        out_shape=(half, half),
        in_specs=[pl.BlockSpec((640, width), lambda i: (0, 0))] * count
        + [pl.BlockSpec((rows, width), lambda i, j=j: (i, at + j)) for j in range(count)]
        + [ANYWHERE] * len(first),
        out_specs=(pl.BlockSpec((320, rows), lambda i: (0, i)),) * 2,
        compiler_params=VMEM,
        cost_estimate=FREE,
    )(*lefts, *[weight] * count, *first)


def core_sum(far, near):
    return (near.astype(F32) + shift(far, T, 1).astype(F32)).astype(BF).reshape(4, 80, -1)


def own_and_received(parts, axis, dim):
    me = lax.axis_index(axis)
    own, *rest = [
        lax.dynamic_index_in_dim(parts, (me + r) % 4, dim, keepdims=False) for r in range(4)
    ]
    return [own] + [shift(rest[r - 1], axis, r) for r in (1, 3, 2)]


def sums_kernel(kinds, *refs):
    for i, out in enumerate(refs[4 * len(kinds) :]):
        total = refs[4 * i][...].astype(F32)
        for ref in refs[4 * i + 1 : 4 * i + 4]:
            total = total + ref[...].astype(F32)
        out[...] = total.astype(kinds[i])


def sums(groups, kinds):
    return pl.pallas_call(
        functools.partial(sums_kernel, kinds),
        out_shape=tuple(jax.ShapeDtypeStruct(g[0].shape, k) for g, k in zip(groups, kinds)),
        compiler_params=VMEM,
        cost_estimate=FREE,
    )(*[block for group in groups for block in group])


def outer_kernel(x_ref, g_ref, y_ref, h_ref, one_ref, two_ref):
    split = g_ref.shape[1]
    for left, right, columns in (
        (x_ref, g_ref, slice(0, split)),
        (y_ref, h_ref, slice(split, split + h_ref.shape[1])),
    ):
        part = dot(left[...], right[...], 0, 0).astype(BF).reshape(4, 160, right.shape[1])
        one_ref[0, :, :, columns] = part[:, :80]
        two_ref[0, :, :, columns] = part[:, 80:]


def outer(x, g, y, h):
    rows, cols = 640, g.shape[1] + h.shape[1]
    left = pl.BlockSpec((640, rows), lambda i: (0, i))
    right = [pl.BlockSpec((640, a.shape[1]), lambda i: (0, 0)) for a in (g, h)]
    return pl.pallas_call(
        outer_kernel,
        grid=(4,),
        out_shape=(jax.ShapeDtypeStruct((4, 4, 80, cols), BF),) * 2,
        in_specs=[left, right[0], left, right[1]],
        out_specs=(pl.BlockSpec((1, 4, 80, cols), lambda i: (i, 0, 0, 0)),) * 2,
        compiler_params=VMEM,
        cost_estimate=FREE,
    )(x, g, y, h)


def to_owners(sums):
    me = lax.axis_index(Y)
    rows = sums.reshape(4, 40, -1)
    got = []
    for r in range(4):
        block = lax.dynamic_index_in_dim(rows, (me + r) % 4, 0, keepdims=False)
        got.append(shift(block, Y, r) if r else block)
    return got


def by_half(blocks):
    cols = blocks.shape[2]
    return blocks.reshape(4, 2, 80, cols).swapaxes(0, 1).reshape(640, cols)


def columns_out(x, *first):
    me = lax.axis_index(Y)
    blocks = quarters(x)
    got = []
    for r in range(4):
        block = lax.dynamic_index_in_dim(blocks, (me + r) % 4, 0, keepdims=False)
        got.append(shift(block, Y, r) if r else block)
    return by_half(place(got, Y, *first, sign=-1))


def quarters(x):
    rows = x.shape[0]
    return x.reshape(rows, 4, -1).swapaxes(0, 1)


def joined(blocks):
    return blocks.swapaxes(0, 1).reshape(blocks.shape[1], -1)


def pack_attention_kernel(q_ref, kv_ref, gains_ref, _, attn_ref):
    attn_ref[...] = jnp.zeros_like(attn_ref)
    for j in range(4):
        attn_ref[j, :40, :320] = q_ref[:, 320 * j : 320 * j + 320]
        attn_ref[j, :40, 320:] = kv_ref[:, 64 * j : 64 * j + 64]
        attn_ref[j, 40:48, :128] = gains_ref[...]


def pack_attention(w_query, keyval_half, gains, first):
    whole = pl.BlockSpec(memory_space=pltpu.VMEM)
    return pl.pallas_call(
        pack_attention_kernel,
        out_shape=jax.ShapeDtypeStruct((4, 48, 384), BF),
        in_specs=[whole, whole, whole, ANYWHERE],
        compiler_params=VMEM,
        cost_estimate=FREE,
    )(w_query, keyval_half, gains, first)


def pack_mlp_kernel(gate_ref, up_ref, down_ref, mlp_ref):
    mlp_ref[...] = jnp.zeros_like(mlp_ref)
    for j in range(4):
        mlp_ref[j, :, :960] = gate_ref[:, 960 * j : 960 * j + 960]
        mlp_ref[j, :, 1024:1984] = up_ref[:, 960 * j : 960 * j + 960]
        mlp_ref[j, :, 2048:3008] = down_ref[:, 960 * j : 960 * j + 960]


def pack_mlp(w_gate, w_up, w_down):
    return pl.pallas_call(
        pack_mlp_kernel,
        out_shape=jax.ShapeDtypeStruct((4, 40, 3072), BF),
        compiler_params=VMEM,
        cost_estimate=FREE,
    )(w_gate, w_up, w_down)


def mlp_grad_kernel(x_ref, y_ref, gate_ref, up_ref, hidden_ref, *rest):
    out_ref = rest[-1]
    j = pl.program_id(0)

    @pl.when(j == 0)
    def _():
        out_ref[...] = dot(x_ref[...], gate_ref[...], 0, 0).astype(BF)

    @pl.when(j == 1)
    def _():
        out_ref[...] = dot(x_ref[...], up_ref[...], 0, 0).astype(BF)

    @pl.when(j == 2)
    def _():
        out_ref[...] = dot(y_ref[...], hidden_ref[...], 0, 0).astype(BF)


def mlp_grads(normed, grads, gate, up, hidden, *first):
    rows = 512
    whole = pl.BlockSpec((640, 1024), lambda j, i: (0, 0))
    return pl.pallas_call(
        mlp_grad_kernel,
        grid=(3, 2560 // rows),
        out_shape=jax.ShapeDtypeStruct((2560, 3072), BF),
        in_specs=[
            pl.BlockSpec((640, rows), lambda j, i: (0, jnp.where(j < 2, i, 4))),
            pl.BlockSpec((640, rows), lambda j, i: (0, jnp.where(j < 2, 0, i))),
            whole,
            whole,
            whole,
        ]
        + [ANYWHERE] * len(first),
        out_specs=pl.BlockSpec((rows, 1024), lambda j, i: (i, j)),
        compiler_params=VMEM,
        cost_estimate=FREE,
    )(normed, grads, gate, up, hidden, *first)


def feed_forward_kernel(x_ref, y_ref, gate_ref, up_ref, down_ref, hidden_out, gate_out, up_out):
    gate = dot(x_ref[...], gate_ref[...], 1, 0)
    up = dot(x_ref[...], up_ref[...], 1, 0)
    grad = dot(y_ref[...], down_ref[...], 1, 0)
    scale = 0.7978845608028654
    square = gate * gate
    bent = jnp.tanh(scale * gate * (1.0 + 0.044715 * square))
    share = 0.5 * (1.0 + bent)
    slope = share + 0.5 * gate * (1.0 - bent * bent) * scale * (1.0 + 0.134145 * square)
    active = gate * share
    hidden_out[...] = (active * up).astype(BF)
    gate_out[...] = (grad * up * slope).astype(BF)
    up_out[...] = (grad * active).astype(BF)


def feed_forward(x, y, w_mlp):
    cols = 256
    steps = 1024 // cols
    part = jax.ShapeDtypeStruct((640, 1024), BF)
    whole = pl.BlockSpec((640, 2560), lambda j: (0, 0))
    out = pl.BlockSpec((640, cols), lambda j: (0, j))
    return pl.pallas_call(
        feed_forward_kernel,
        grid=(steps,),
        out_shape=(part, part, part),
        in_specs=[whole, whole]
        + [pl.BlockSpec((2560, cols), lambda j, k=k: (0, k * steps + j)) for k in range(3)],
        out_specs=(out, out, out),
        compiler_params=VMEM,
        cost_estimate=FREE,
    )(x, y, w_mlp, w_mlp, w_mlp)


def to_piece_order(x):
    rows = x.shape[0]
    return x.reshape(rows, 4, 16, 40).swapaxes(1, 2).reshape(rows, 2560)


def inverse_root(values):
    return lax.rsqrt(jnp.mean(values * values, axis=-1, keepdims=True) + EPSILON)


def norm_back(grad, values, inverse, gain):
    scaled = gain * grad
    return inverse * scaled - values * inverse**3 * jnp.mean(
        scaled * values, axis=-1, keepdims=True
    )


def angles(position, head_dim):
    quarter = head_dim // 4
    frequency = 10000.0 ** (-jnp.arange(quarter, dtype=F32) / quarter)
    phase_angle = position[:, None].astype(F32) * frequency[None, :]
    return (jnp.cos(phase_angle), jnp.sin(phase_angle))


def rotate(values, cosine, sine_part):
    quarter = cosine.shape[-1]
    first_half = values[..., :quarter]
    second = values[..., quarter : 2 * quarter]
    cos_rows = cosine[:, None, :]
    sin_rows = sine_part[:, None, :]
    return jnp.concatenate(
        [
            first_half * cos_rows - second * sin_rows,
            second * cos_rows + first_half * sin_rows,
            values[..., 2 * quarter :],
        ],
        axis=-1,
    )


def dot(a, b, da, db):
    return lax.dot_general(a, b, (((da,), (db,)), ((), ())), preferred_element_type=F32)


def project_kernel(own_ref, other_ref, gain_ref, weight_ref, normed_ref, out_ref):
    def rows(block):
        x = block[...].astype(F32)
        normed = (x * inverse_root(x) * gain_ref[...]).astype(BF)
        normed_ref[...] = normed
        out_ref[0] = dot(normed, weight_ref[...], 1, 0).astype(BF)

    i = pl.program_id(0)

    @pl.when(i < 4)
    def _():
        rows(own_ref)

    @pl.when(i >= 4)
    def _():
        rows(other_ref)


def project(own, other, gain, weight):
    return pl.pallas_call(
        project_kernel,
        grid=(8,),
        out_shape=(
            jax.ShapeDtypeStruct((640, 2560), BF),
            jax.ShapeDtypeStruct((4, 160, 384), BF),
        ),
        in_specs=[
            pl.BlockSpec((80, 2560), lambda i: (jnp.minimum(i, 3), 0)),
            pl.BlockSpec((80, 2560), lambda i: (jnp.maximum(i, 4) - 4, 0)),
            pl.BlockSpec((1, 2560), lambda i: (0, 0)),
            pl.BlockSpec((2560, 384), lambda i: (0, 0)),
        ],
        out_specs=(
            pl.BlockSpec((80, 2560), lambda i: (i, 0)),
            pl.BlockSpec((1, 80, 384), lambda i: (i % 4, i // 4, 0)),
        ),
        compiler_params=VMEM,
        cost_estimate=FREE,
    )(own, other, gain, weight)


def owners_kernel(*refs):
    home, mlp = refs[:4], refs[4:8]
    query_ref, keyval_ref, gate_ref, up_ref, block_mine, block_other, rows_mine, rows_other = refs[8:16]
    query_out, keyval_out, output_out, gate_out, up_out, down_out, gain_out, block_out, rows_out = refs[16:25]
    held, held_mlp = refs[25:]
    me = lax.axis_index(Y)
    for r in range(4):
        held[lax.rem(me + 4 - r, 4)] = home[r][...]
        held_mlp[lax.rem(me + 4 - r, 4)] = mlp[r][...]
    for j in range(4):
        columns = slice(960 * j, 960 * j + 960)
        gate_out[:, columns] = held_mlp[j, :, :960].astype(F32)
        up_out[:, columns] = held_mlp[j, :, 1024:1984].astype(F32)
        down_out[:, columns] = held_mlp[j, :, 2048:3008].astype(F32)
        total = held[j].astype(F32)
        query_out[:, 320 * j : 320 * j + 320] = total[:, :320]
        keyval_out[:, 64 * j : 64 * j + 64] = total[:, 320:384]
        output_out[:, 320 * j : 320 * j + 320] = total[:, 384:]

    def products(weight, grad):
        return jnp.sum(weight[...].astype(F32) * grad[...], axis=1, keepdims=True)

    one = products(query_ref, query_out) + products(keyval_ref, keyval_out)
    two = products(gate_ref, gate_out) + products(up_ref, up_out)
    gain_out[:, :128] = jnp.broadcast_to(one, (40, 128))
    gain_out[:, 128:] = jnp.broadcast_to(two, (40, 128))
    at = 80 * lax.axis_index(T)
    for mine, other, out in ((block_mine, block_other, block_out), (rows_mine, rows_other, rows_out)):
        out[pl.ds(pl.multiple_of(at, 16), 80), :] = mine[...]
        out[pl.ds(pl.multiple_of(80 - at, 16), 80), :] = other[...]


def owners(home, mlp, w_query, keyval_half, w_gate, w_up, block, rows):
    wide, narrow = (jax.ShapeDtypeStruct((40, n), F32) for n in (3840, 1280))
    small = jax.ShapeDtypeStruct((40, 256), F32)
    tokens = jax.ShapeDtypeStruct((160, 2560), BF)
    return pl.pallas_call(
        owners_kernel,
        out_shape=(narrow, small, narrow, wide, wide, wide, small, tokens, tokens),
        scratch_shapes=[pltpu.VMEM((4, 40, 704), BF), pltpu.VMEM((4, 40, 3072), BF)],
        compiler_params=VMEM,
        cost_estimate=FREE,
    )(*home, *mlp, w_query, keyval_half, w_gate, w_up, *block, *rows)


def token_order_kernel(x_ref, out_ref):
    for j in range(4):
        for p in range(16):
            to, at = 40 * (16 * j + p), 40 * (4 * p + j)
            out_ref[:, to : to + 40] = x_ref[:, at : at + 40].astype(BF)


def from_piece_order(x):
    return pl.pallas_call(
        token_order_kernel, out_shape=jax.ShapeDtypeStruct(x.shape, BF), compiler_params=VMEM, cost_estimate=FREE
    )(x)


def shards(
    tokens,
    lengths,
    attn_gain,
    w_query,
    w_keyval,
    w_output,
    mlp_gain,
    w_gate,
    w_up,
    w_down,
    cotangent,
):
    t = lax.axis_index(T)
    me = lax.axis_index(Y)
    piece = lax.axis_index(CONTEXT)
    head_dim = 256
    query_scale = head_dim ** (-0.5)
    seq_count = 2560
    padding = seq_count - lengths[0]
    row_start = piece * 160
    natural = row_start + jnp.arange(160, dtype=jnp.int32)
    turned = row_start + (jnp.arange(160, dtype=jnp.int32) + t * 80) % 160
    live_turned = turned >= padding
    live_mine = live_turned[:80, None]

    out_rows = place(ring_blocks(w_output, Y), Y).reshape(160, 1280)
    w_out = lax.all_gather(out_rows, CONTEXT, axis=0, tiled=True)

    x_low = to_piece_order(lax.dynamic_slice_in_dim(tokens[0], t * 80, 80, 0))
    cot_mine = to_piece_order(lax.dynamic_slice_in_dim(cotangent[0], t * 80, 80, 0))
    grad_mine = jnp.where(live_mine, cot_mine, jnp.zeros_like(cot_mine))
    x_mine = x_low.astype(F32)
    keyval_half = lax.dynamic_slice_in_dim(w_keyval, t * 256, 256, 1)
    gains = jnp.concatenate([attn_gain, mlp_gain])[None, :]
    gains = jnp.pad(gains, ((0, 7), (0, 48)))
    attn_blocks = pack_attention(w_query, keyval_half, gains, small_trip(x_low))
    attn_copies = jnp.broadcast_to(attn_blocks[None], (16, 4, 48, 384)).reshape(64, 48, 384)
    attn_all = exchange(attn_copies, PIECES)
    w_qkv = attn_all[:, :40].reshape(2560, 384)
    gain_one = attn_all[:, 40, :40].reshape(1, 2560).astype(F32)
    gain_two = attn_all[:, 40, 40:80].reshape(1, 2560).astype(F32)
    x_own, x_other = gather_rows(x_low, attn_all)
    mlp_blocks = pack_mlp(w_gate, w_up, w_down)
    mlp_got = to_owners(mlp_blocks)
    mlp_block = place(mlp_got, Y, x_own, sign=-1).reshape(160, 3072)
    w_mlp = lax.all_gather(mlp_block, CONTEXT, axis=0, tiled=True)

    normed, projected = project(x_own, x_other, gain_one, w_qkv)
    home = exchange(projected, Y)
    keyval_turned = joined(home[:, :, 320:])
    keyval_own = jnp.where(
        t == 0, keyval_turned, jnp.concatenate([keyval_turned[80:], keyval_turned[:80]])
    )
    cosine_nat, sine_nat = angles(natural - padding, head_dim)
    keys_own = rotate(keyval_own[:, None].astype(F32), cosine_nat, sine_nat)[:, 0].astype(BF)
    kv_own = jnp.where(t == 0, keys_own, keyval_own)
    kv_mine = exchange(jnp.broadcast_to(kv_own[None], (16, 160, 256)), CONTEXT).reshape(2560, 256)
    grad_own, grad_other = gather_rows(after(grad_mine, kv_own), kv_mine)
    grad_group = jnp.concatenate([grad_own, grad_other])
    kv_other = shift(kv_mine, T, 1)
    keys = jnp.where(t == 0, kv_mine, kv_other)
    values = jnp.where(t == 0, kv_other, kv_mine)
    query_pre = joined(home[:, :, :320]).reshape(160, 5, head_dim).astype(F32)
    cosine, sine_part = angles(turned - padding, head_dim)
    queries = (rotate(query_pre, cosine, sine_part) * query_scale).astype(BF)

    key_index = jnp.arange(seq_count, dtype=jnp.int32)
    offset = turned[:, None] - key_index[None, :]
    allowed = ((offset >= 0) & (offset < WINDOW) & (key_index >= padding)[None, :])[None]
    live = live_turned[None, :, None]
    scores = jnp.einsum("qhd,kd->hqk", queries, keys, preferred_element_type=F32)
    row_top = jnp.max(jnp.where(allowed, scores, NEGATIVE_FILL), axis=-1, keepdims=True)
    row_top = jnp.where(live, row_top, 0.0)
    weights_exp = jnp.where(allowed, jnp.exp(scores - row_top), 0.0)
    row_total = jnp.where(live, jnp.sum(weights_exp, axis=-1, keepdims=True), 1.0)
    prob = weights_exp / row_total
    prob_low = prob.astype(BF)
    attended = jnp.einsum("hqk,kd->qhd", prob_low, values, preferred_element_type=F32)
    attended = attended.reshape(160, 1280).astype(BF)

    branch = dot(attended, w_out, 1, 1)
    hidden_mine = x_mine + branch[:80] + shift(branch[80:], T, 1)

    inverse_two = inverse_root(hidden_mine)
    normed_two_mine = (hidden_mine * inverse_two * gain_two).astype(BF)
    normed_two = jnp.concatenate(gather_rows(after(normed_two_mine, grad_group)))
    hidden, grad_gate, grad_up = feed_forward(normed_two, grad_group, w_mlp)
    normed_two_low = core_sum(*row_products((grad_gate, grad_up), w_mlp, 0, 1024))
    got = own_and_received(normed_two_low, Y, 0)

    mlp_rows = row_products((hidden,), w_mlp, 2, 1024, normed_two_low)
    mlp_part = mlp_grads(
        normed_two, grad_group, grad_gate, grad_up, hidden, *got, *mlp_rows
    )
    mlp_sum = lax.psum_scatter(mlp_part, CONTEXT, scatter_dimension=0, tiled=True)
    grad_normed_two = sum(block.astype(F32) for block in got)

    grad_h_mine = grad_mine.astype(F32) + norm_back(
        grad_normed_two, hidden_mine, inverse_two, gain_two
    )
    branch_mine = grad_h_mine.astype(BF)
    branch_low = jnp.concatenate([branch_mine, shift(branch_mine, T, 1)])
    grad_attended = dot(branch_low, w_out, 1, 0).astype(BF).reshape(160, 5, head_dim)

    grad_prob = jnp.einsum("qhd,kd->hqk", grad_attended, values, preferred_element_type=F32)
    spread = jnp.sum(prob * grad_prob, axis=-1, keepdims=True)
    grad_scores = (prob * (grad_prob - spread)).astype(BF)
    grad_keys = jnp.einsum("hqk,qhd->kd", grad_scores, queries, preferred_element_type=F32)
    grad_values = jnp.einsum("hqk,qhd->kd", prob_low, grad_attended, preferred_element_type=F32)
    keep = jnp.where(t == 0, grad_keys, grad_values)
    give = jnp.where(t == 0, grad_values, grad_keys).astype(BF)
    grad_queries = jnp.einsum("hqk,kd->qhd", grad_scores, keys, preferred_element_type=F32)
    grad_query_pre = (
        rotate(grad_queries * query_scale, cosine, -sine_part).reshape(160, 1280).astype(BF)
    )
    kv_part = (keep + shift(give, T, 1).astype(F32)).astype(BF).reshape(16, 160, 256)
    kv_part = after(kv_part, grad_query_pre)
    kv_home = exchange(kv_part, CONTEXT)
    branch_group = jnp.concatenate(gather_rows(branch_mine, kv_home))
    attended_group = columns_out(attended, kv_home)
    kv_sum = jnp.sum(kv_home.astype(F32), axis=0)
    grad_query_group = columns_out(grad_query_pre, kv_home)

    keys_back = rotate(kv_sum[:, None], cosine_nat, -sine_nat)[:, 0]
    kv_back = jnp.where(t == 0, keys_back, kv_sum).astype(BF)
    kv_back = jnp.where(t == 0, kv_back, jnp.concatenate([kv_back[80:], kv_back[:80]]))
    grad_kv_group = columns_out(kv_back)
    grad_qkv = jnp.concatenate([grad_query_group, grad_kv_group], axis=1)
    normed_low = core_sum(*row_products((grad_qkv,), w_qkv, 0, 384))
    first_half, last_half = outer(normed, grad_qkv, branch_group, attended_group)
    one, two, grad_normed = sums(
        (
            own_and_received(first_half, X, 0),
            own_and_received(last_half, Z, 1),
            own_and_received(normed_low, Y, 0),
        ),
        (BF, BF, F32),
    )
    mlp_low = core_sum(*mlp_rows)
    one, two, mlp_mine = sums(
        (
            own_and_received(one, Z, 0),
            own_and_received(two, X, 0),
            own_and_received(after(mlp_low, one), Y, 0),
        ),
        (BF, BF, F32),
    )
    home = to_owners(jnp.concatenate([one, two]))
    block_mine = from_piece_order(jnp.where(live_mine, hidden_mine + mlp_mine, 0.0))
    inverse_one = inverse_root(x_mine)
    tokens_mine = from_piece_order(
        grad_h_mine + norm_back(grad_normed, x_mine, inverse_one, gain_one)
    )
    query_grad, kv_half, output_grad, gate_grad, up_grad, down_grad, gain_part, block_out, tokens_grad = owners(
        home,
        to_owners(mlp_sum),
        w_query,
        keyval_half,
        w_gate,
        w_up,
        (block_mine, shift(block_mine, T, 1)),
        (tokens_mine, shift(tokens_mine, T, 1)),
    )

    mine = jnp.concatenate([kv_half, gain_part], axis=1)
    other = shift(mine, T, 1)
    kv_other = other[:, :256]
    keyval_grad = jnp.where(
        t == 0,
        jnp.concatenate([kv_half, kv_other], axis=1),
        jnp.concatenate([kv_other, kv_half], axis=1),
    )
    attn_gain_grad = (mine[:, 256] + other[:, 256]) / attn_gain.astype(F32)
    mlp_gain_grad = (mine[:, 384] + other[:, 384]) / mlp_gain.astype(F32)

    return (
        block_out[None],
        tokens_grad[None],
        attn_gain_grad,
        query_grad,
        keyval_grad,
        output_grad,
        mlp_gain_grad,
        gate_grad,
        up_grad,
        down_grad,
    )


def solution(mesh):
    torus = Mesh(
        mesh.devices.reshape(mesh.shape["shard"], 4, 4, mesh.shape["tensor"]),
        ("shard", "context_0", "context_1", "tensor"),
    )
    in_specs = (
        P("shard", CONTEXT, None),
        P("shard"),
        P(SHARD_CONTEXT),
        P(SHARD_CONTEXT, "tensor"),
        P(SHARD_CONTEXT, None),
        P(SHARD_CONTEXT, "tensor"),
        P(SHARD_CONTEXT),
        P(SHARD_CONTEXT, "tensor"),
        P(SHARD_CONTEXT, "tensor"),
        P(SHARD_CONTEXT, "tensor"),
        P("shard", CONTEXT, None),
    )
    out_specs = (
        P("shard", CONTEXT, None),
        P("shard", CONTEXT, None),
        P(SHARD_CONTEXT),
        P(SHARD_CONTEXT, "tensor"),
        P(SHARD_CONTEXT, None),
        P(SHARD_CONTEXT, "tensor"),
        P(SHARD_CONTEXT),
        P(SHARD_CONTEXT, "tensor"),
        P(SHARD_CONTEXT, "tensor"),
        P(SHARD_CONTEXT, "tensor"),
    )
    return jax.shard_map(
        shards, mesh=torus, in_specs=in_specs, out_specs=out_specs, check_vma=False
    )
```

```python
import functools

import jax
import jax.numpy as jnp
from jax import lax
from jax.experimental import pallas as pl
from jax.experimental.pallas import tpu as pltpu
from jax.sharding import Mesh
from jax.sharding import PartitionSpec as P

WINDOW = 2048
SHARD_CONTEXT = ("shard", "context_0", "context_1")
CONTEXT = ("context_0", "context_1")
PIECES = ("context_0", "context_1", "shard")
Y, X, Z, T = "shard", "context_0", "context_1", "tensor"
VMEM = pltpu.CompilerParams(vmem_limit_bytes=48 * 2**20)
ANYWHERE = pl.BlockSpec(memory_space=pl.ANY)
FREE = pl.CostEstimate(flops=0, bytes_accessed=0, transcendentals=0)

EPSILON = 1e-06
NEGATIVE_FILL = -1e30
BF = jnp.bfloat16
F32 = jnp.float32


def shift(x, axis, by):
    n = lax.axis_size(axis)
    return lax.ppermute(x, axis, [(i, (i + by) % n) for i in range(n)])


def exchange(blocks, axis):
    return lax.all_to_all(blocks, axis, 0, 0, tiled=True)


def nothing(*refs):
    pass


def after(x, *others):
    return pl.pallas_call(
        nothing,
        out_shape=jax.ShapeDtypeStruct(x.shape, x.dtype),
        in_specs=[ANYWHERE] * (1 + len(others)),
        out_specs=ANYWHERE,
        input_output_aliases={0: 0},
        compiler_params=VMEM,
        cost_estimate=FREE,
    )(x, *others)


def small_trip(x, *others):
    corner = x.reshape(-1, x.shape[-1])[:8, :128]
    return shift(after(corner, *others) if others else corner, T, 1)


def ring_blocks(x, axis):
    return [x, shift(x, axis, -1), shift(x, axis, 2), shift(x, axis, 1)]


def place_kernel(axis, sign, *refs):
    blocks, out = refs[:4], refs[-1]
    me = lax.axis_index(axis)
    for r, block in enumerate(blocks):
        out[lax.rem(me + (sign * r) % 4, 4)] = block[...]


def place(blocks, axis, *first, sign=1):
    whole = pl.BlockSpec(memory_space=pltpu.VMEM)
    return pl.pallas_call(
        functools.partial(place_kernel, axis, sign),
        out_shape=jax.ShapeDtypeStruct((4, *blocks[0].shape), blocks[0].dtype),
        in_specs=[whole] * 4 + [ANYWHERE] * len(first),
        out_specs=whole,
        compiler_params=VMEM,
        cost_estimate=FREE,
    )(*blocks, *first)


def gather_rows(mine, *first):
    own = place(ring_blocks(mine, Y), Y, *first).reshape(320, -1)
    return own, shift(own, T, 1)


def rows_kernel(count, *refs):
    lefts, rights, (far_ref, near_ref) = refs[:count], refs[count : 2 * count], refs[-2:]
    total = dot(lefts[0][...], rights[0][...], 1, 1)
    for left, right in zip(lefts[1:], rights[1:]):
        total = total + dot(left[...], right[...], 1, 1)
    near_ref[...] = total[:320].astype(BF)
    far_ref[...] = total[320:].astype(BF)


def row_products(lefts, weight, at, width, *first):
    rows, count, n = 256, len(lefts), weight.shape[0]
    half = jax.ShapeDtypeStruct((320, n), BF)
    return pl.pallas_call(
        functools.partial(rows_kernel, count),
        grid=(n // rows,),
        out_shape=(half, half),
        in_specs=[pl.BlockSpec((640, width), lambda i: (0, 0))] * count
        + [pl.BlockSpec((rows, width), lambda i, j=j: (i, at + j)) for j in range(count)]
        + [ANYWHERE] * len(first),
        out_specs=(pl.BlockSpec((320, rows), lambda i: (0, i)),) * 2,
        compiler_params=VMEM,
        cost_estimate=FREE,
    )(*lefts, *[weight] * count, *first)


def core_sum(far, near):
    return (near.astype(F32) + shift(far, T, 1).astype(F32)).astype(BF).reshape(4, 80, -1)


def own_and_received(parts, axis, dim):
    me = lax.axis_index(axis)
    own, *rest = [
        lax.dynamic_index_in_dim(parts, (me + r) % 4, dim, keepdims=False) for r in range(4)
    ]
    return [own] + [shift(rest[r - 1], axis, r) for r in (1, 3, 2)]


def sums_kernel(kinds, *refs):
    for i, out in enumerate(refs[4 * len(kinds) :]):
        total = refs[4 * i][...].astype(F32)
        for ref in refs[4 * i + 1 : 4 * i + 4]:
            total = total + ref[...].astype(F32)
        out[...] = total.astype(kinds[i])


def sums(groups, kinds):
    return pl.pallas_call(
        functools.partial(sums_kernel, kinds),
        out_shape=tuple(jax.ShapeDtypeStruct(g[0].shape, k) for g, k in zip(groups, kinds)),
        compiler_params=VMEM,
        cost_estimate=FREE,
    )(*[block for group in groups for block in group])


def outer_kernel(x_ref, g_ref, own_ref, other_ref, h_ref, out_ref):
    split, cols = g_ref.shape[1], h_ref.shape[1]
    part = dot(x_ref[...], g_ref[...], 0, 0)
    out_ref[:, :, :split] = part.astype(BF).reshape(4, 160, split)
    part = dot(own_ref[...], h_ref[:320], 0, 0) + dot(other_ref[...], h_ref[320:], 0, 0)
    out_ref[:, :, split:] = part.astype(BF).reshape(4, 160, cols)


def outer(x, g, own, other, h):
    rows, cols = 640, g.shape[1] + h.shape[1]
    whole, half = (pl.BlockSpec((n, rows), lambda i: (0, i)) for n in (640, 320))
    right = [pl.BlockSpec((640, a.shape[1]), lambda i: (0, 0)) for a in (g, h)]
    return pl.pallas_call(
        outer_kernel,
        grid=(4,),
        out_shape=jax.ShapeDtypeStruct((16, 160, cols), BF),
        in_specs=[whole, right[0], half, half, right[1]],
        out_specs=pl.BlockSpec((4, 160, cols), lambda i: (i, 0, 0)),
        compiler_params=VMEM,
        cost_estimate=FREE,
    )(x, g, own, other, h)


def to_owners(sums):
    me = lax.axis_index(Y)
    rows = sums.reshape(4, -1, sums.shape[-1])
    got = []
    for r in range(4):
        block = lax.dynamic_index_in_dim(rows, (me + r) % 4, 0, keepdims=False)
        got.append(shift(block, Y, r) if r else block)
    return got


def by_half(blocks):
    cols = blocks.shape[2]
    return blocks.reshape(4, 2, 80, cols).swapaxes(0, 1).reshape(640, cols)


def columns_out(blocks):
    me = lax.axis_index(Y)
    got = []
    for r in range(4):
        block = lax.dynamic_index_in_dim(blocks, (me + r) % 4, 0, keepdims=False)
        got.append(shift(block, Y, r) if r else block)
    return by_half(place(got, Y, sign=-1))


def quarters(x):
    rows = x.shape[0]
    return x.reshape(rows, 4, -1).swapaxes(0, 1)


def pack_attention_kernel(q_ref, kv_ref, gains_ref, attn_ref):
    attn_ref[...] = jnp.zeros_like(attn_ref)
    for j in range(4):
        attn_ref[j, :40, :320] = q_ref[:, 320 * j : 320 * j + 320]
        attn_ref[j, :40, 320:] = kv_ref[:, 64 * j : 64 * j + 64]
        attn_ref[j, 40:48, :128] = gains_ref[...]


def pack_attention(w_query, keyval_half, gains):
    return pl.pallas_call(
        pack_attention_kernel,
        out_shape=jax.ShapeDtypeStruct((4, 48, 384), BF),
        compiler_params=VMEM,
        cost_estimate=FREE,
    )(w_query, keyval_half, gains)


def pack_mlp_kernel(gate_ref, up_ref, down_ref, mlp_ref):
    mlp_ref[...] = jnp.zeros_like(mlp_ref)
    for j in range(4):
        mlp_ref[j, :, :960] = gate_ref[:, 960 * j : 960 * j + 960]
        mlp_ref[j, :, 1024:1984] = up_ref[:, 960 * j : 960 * j + 960]
        mlp_ref[j, :, 2048:3008] = down_ref[:, 960 * j : 960 * j + 960]


def pack_mlp(w_gate, w_up, w_down):
    return pl.pallas_call(
        pack_mlp_kernel,
        out_shape=jax.ShapeDtypeStruct((4, 40, 3072), BF),
        compiler_params=VMEM,
        cost_estimate=FREE,
    )(w_gate, w_up, w_down)


def mlp_grad_kernel(x_ref, y_ref, gate_ref, up_ref, hidden_ref, *rest):
    out_ref = rest[-1]
    j = pl.program_id(0)

    @pl.when(j == 0)
    def _():
        out_ref[...] = dot(x_ref[...], gate_ref[...], 0, 0).astype(BF)

    @pl.when(j == 1)
    def _():
        out_ref[...] = dot(x_ref[...], up_ref[...], 0, 0).astype(BF)

    @pl.when(j == 2)
    def _():
        out_ref[...] = dot(y_ref[...], hidden_ref[...], 0, 0).astype(BF)


def mlp_grads(normed, grads, gate, up, hidden, *first):
    rows = 512
    whole = pl.BlockSpec((640, 1024), lambda j, i: (0, 0))
    return pl.pallas_call(
        mlp_grad_kernel,
        grid=(3, 2560 // rows),
        out_shape=jax.ShapeDtypeStruct((2560, 3072), BF),
        in_specs=[
            pl.BlockSpec((640, rows), lambda j, i: (0, jnp.where(j < 2, i, 4))),
            pl.BlockSpec((640, rows), lambda j, i: (0, jnp.where(j < 2, 0, i))),
            whole,
            whole,
            whole,
        ]
        + [ANYWHERE] * len(first),
        out_specs=pl.BlockSpec((rows, 1024), lambda j, i: (i, j)),
        compiler_params=VMEM,
        cost_estimate=FREE,
    )(normed, grads, gate, up, hidden, *first)


def feed_forward_kernel(x_ref, y_ref, gate_ref, up_ref, down_ref, *rest):
    hidden_out, gate_out, up_out = rest[-3:]
    gate = dot(x_ref[...], gate_ref[...], 1, 0)
    up = dot(x_ref[...], up_ref[...], 1, 0)
    grad = dot(y_ref[...], down_ref[...], 1, 0)
    scale = 0.7978845608028654
    square = gate * gate
    bent = jnp.tanh(scale * gate * (1.0 + 0.044715 * square))
    share = 0.5 * (1.0 + bent)
    slope = share + 0.5 * gate * (1.0 - bent * bent) * scale * (1.0 + 0.134145 * square)
    active = gate * share
    hidden_out[...] = (active * up).astype(BF)
    gate_out[...] = (grad * up * slope).astype(BF)
    up_out[...] = (grad * active).astype(BF)


def feed_forward(x, y, w_mlp, *first):
    cols = 256
    steps = 1024 // cols
    part = jax.ShapeDtypeStruct((640, 1024), BF)
    whole = pl.BlockSpec((640, 2560), lambda j: (0, 0))
    out = pl.BlockSpec((640, cols), lambda j: (0, j))
    return pl.pallas_call(
        feed_forward_kernel,
        grid=(steps,),
        out_shape=(part, part, part),
        in_specs=[whole, whole]
        + [pl.BlockSpec((2560, cols), lambda j, k=k: (0, k * steps + j)) for k in range(3)]
        + [ANYWHERE] * len(first),
        out_specs=(out, out, out),
        compiler_params=VMEM,
        cost_estimate=FREE,
    )(x, y, w_mlp, w_mlp, w_mlp, *first)


def to_piece_order(x):
    rows = x.shape[0]
    return x.reshape(rows, 4, 16, 40).swapaxes(1, 2).reshape(rows, 2560)


def inverse_root(values):
    return lax.rsqrt(jnp.mean(values * values, axis=-1, keepdims=True) + EPSILON)


def norm_back(grad, values, inverse, gain):
    scaled = gain * grad
    return inverse * scaled - values * inverse**3 * jnp.mean(
        scaled * values, axis=-1, keepdims=True
    )


def angles(position, head_dim):
    quarter = head_dim // 4
    frequency = 10000.0 ** (-jnp.arange(quarter, dtype=F32) / quarter)
    phase_angle = position[:, None].astype(F32) * frequency[None, :]
    return (jnp.cos(phase_angle), jnp.sin(phase_angle))


def dot(a, b, da, db):
    return lax.dot_general(a, b, (((da,), (db,)), ((), ())), preferred_element_type=F32)


def project_kernel(own_ref, other_ref, gain_ref, weight_ref, *rest):
    normed_ref, out_ref = rest[-2:]

    def rows(block):
        x = block[0].astype(F32)
        normed = (x * inverse_root(x) * gain_ref[...]).astype(BF)
        normed_ref[...] = normed
        out_ref[0] = dot(normed, weight_ref[...], 1, 0).astype(BF)

    i = pl.program_id(0)

    @pl.when(i < 4)
    def _():
        rows(own_ref)

    @pl.when(i >= 4)
    def _():
        rows(other_ref)


def project(own, other, gain, weight, *first):
    return pl.pallas_call(
        project_kernel,
        grid=(8,),
        out_shape=(
            jax.ShapeDtypeStruct((640, 2560), BF),
            jax.ShapeDtypeStruct((4, 160, 384), BF),
        ),
        in_specs=[
            pl.BlockSpec((1, 80, 2560), lambda i: (jnp.minimum(i, 3), 0, 0)),
            pl.BlockSpec((1, 80, 2560), lambda i: (jnp.maximum(i, 4) - 4, 0, 0)),
            pl.BlockSpec((1, 2560), lambda i: (0, 0)),
            pl.BlockSpec((2560, 384), lambda i: (0, 0)),
        ]
        + [ANYWHERE] * len(first),
        out_specs=(
            pl.BlockSpec((80, 2560), lambda i: (i, 0)),
            pl.BlockSpec((1, 80, 384), lambda i: (i % 4, i // 4, 0)),
        ),
        compiler_params=VMEM,
        cost_estimate=FREE,
    )(own, other, gain, weight, *first)


def owners_kernel(*refs):
    home, mlp = refs[:4], refs[4:8]
    query_ref, keyval_ref, gate_ref, up_ref, block_mine, block_other, rows_mine, rows_other = refs[8:16]
    query_out, keyval_out, output_out, gate_out, up_out, down_out, gain_out, block_out, rows_out = refs[16:25]
    held, held_mlp = refs[25:]
    me = lax.axis_index(Y)
    for r in range(4):
        held[lax.rem(me + 4 - r, 4)] = home[r][...]
        held_mlp[lax.rem(me + 4 - r, 4)] = mlp[r][...]
    for j in range(4):
        columns = slice(960 * j, 960 * j + 960)
        gate_out[:, columns] = held_mlp[j, :, :960].astype(F32)
        up_out[:, columns] = held_mlp[j, :, 1024:1984].astype(F32)
        down_out[:, columns] = held_mlp[j, :, 2048:3008].astype(F32)
        total = held[j].astype(F32)
        query_out[:, 320 * j : 320 * j + 320] = total[:, :320]
        keyval_out[:, 64 * j : 64 * j + 64] = total[:, 320:384]
        output_out[:, 320 * j : 320 * j + 320] = total[:, 384:]

    def products(weight, grad):
        return jnp.sum(weight[...].astype(F32) * grad[...], axis=1, keepdims=True)

    one = products(query_ref, query_out) + products(keyval_ref, keyval_out)
    two = products(gate_ref, gate_out) + products(up_ref, up_out)
    gain_out[:, :128] = jnp.broadcast_to(one, (40, 128))
    gain_out[:, 128:] = jnp.broadcast_to(two, (40, 128))
    at = 80 * lax.axis_index(T)
    for mine, other, out in ((block_mine, block_other, block_out), (rows_mine, rows_other, rows_out)):
        out[pl.ds(pl.multiple_of(at, 16), 80), :] = mine[...]
        out[pl.ds(pl.multiple_of(80 - at, 16), 80), :] = other[...]


def owners(home, mlp, w_query, keyval_half, w_gate, w_up, block, rows):
    wide, narrow = (jax.ShapeDtypeStruct((40, n), F32) for n in (3840, 1280))
    small = jax.ShapeDtypeStruct((40, 256), F32)
    tokens = jax.ShapeDtypeStruct((160, 2560), BF)
    return pl.pallas_call(
        owners_kernel,
        out_shape=(narrow, small, narrow, wide, wide, wide, small, tokens, tokens),
        scratch_shapes=[pltpu.VMEM((4, 40, 704), BF), pltpu.VMEM((4, 40, 3072), BF)],
        compiler_params=VMEM,
        cost_estimate=FREE,
    )(*home, *mlp, w_query, keyval_half, w_gate, w_up, *block, *rows)


def turned(values, cosine, sine):
    one, two = values[:, :64], values[:, 64:128]
    return jnp.concatenate(
        [one * cosine - two * sine, two * cosine + one * sine, values[:, 128:]], axis=1
    )


def prepare_kernel(scale, home_ref, cosine_ref, sine_ref, query_ref, kv_ref, wide):
    cosine, sine = cosine_ref[...], sine_ref[...]
    for j in range(4):
        wide[:, 320 * j : 320 * j + 320] = home_ref[j, :, :320].astype(F32)
    for h in range(5):
        head = turned(wide[:, 256 * h : 256 * h + 256], cosine, sine)
        query_ref[h] = (head * scale).astype(BF)
    for j in range(4):
        wide[:, 64 * j : 64 * j + 64] = home_ref[j, :, 320:].astype(F32)
    first = lax.axis_index(T) == 0
    kv = wide[:, :256]
    kv = jnp.where(first, turned(kv, cosine, sine), kv).astype(BF)
    at = 80 * lax.axis_index(T)
    kv_ref[pl.ds(pl.multiple_of(at, 16), 80), :] = kv[:80]
    kv_ref[pl.ds(pl.multiple_of(80 - at, 16), 80), :] = kv[80:]


def prepare(home, cosine, sine, scale):
    return pl.pallas_call(
        functools.partial(prepare_kernel, scale),
        out_shape=(
            jax.ShapeDtypeStruct((5, 160, 256), BF),
            jax.ShapeDtypeStruct((160, 256), BF),
        ),
        scratch_shapes=[pltpu.VMEM((160, 1280), F32)],
        compiler_params=VMEM,
        cost_estimate=FREE,
    )(home, cosine, sine)


def unturn_kernel(scale, grad_ref, cosine_ref, sine_ref, out_ref, wide):
    cosine, sine = cosine_ref[...], -sine_ref[...]
    for h in range(5):
        wide[:, 256 * h : 256 * h + 256] = turned(grad_ref[h] * scale, cosine, sine)
    for j in range(4):
        out_ref[j] = wide[:, 320 * j : 320 * j + 320].astype(BF)


def unturn(grad, cosine, sine, scale):
    return pl.pallas_call(
        functools.partial(unturn_kernel, scale),
        out_shape=jax.ShapeDtypeStruct((4, 160, 320), BF),
        scratch_shapes=[pltpu.VMEM((160, 1280), F32)],
        compiler_params=VMEM,
        cost_estimate=FREE,
    )(grad, cosine, sine)


def unturn_kv_kernel(home_ref, cosine_ref, sine_ref, out_ref, held):
    total = home_ref[0].astype(F32)
    for p in range(1, 16):
        total = total + home_ref[p].astype(F32)
    held[...] = total
    at = 80 * lax.axis_index(T)
    total = jnp.concatenate(
        [held[pl.ds(pl.multiple_of(at, 16), 80), :], held[pl.ds(pl.multiple_of(80 - at, 16), 80), :]]
    )
    back = turned(total, cosine_ref[...], -sine_ref[...])
    total = jnp.where(lax.axis_index(T) == 0, back, total).astype(BF)
    for j in range(4):
        out_ref[j] = total[:, 64 * j : 64 * j + 64]


def unturn_kv(home, cosine, sine):
    return pl.pallas_call(
        unturn_kv_kernel,
        out_shape=jax.ShapeDtypeStruct((4, 160, 64), BF),
        scratch_shapes=[pltpu.VMEM((160, 256), F32)],
        compiler_params=VMEM,
        cost_estimate=FREE,
    )(home, cosine, sine)


def pieces_kernel(home_ref, *rest):
    total = home_ref[0].astype(F32)
    for p in range(1, 16):
        total = total + home_ref[p].astype(F32)
    rest[-1][...] = total.astype(BF)


def pieces_sum(home, *first):
    cols = home.shape[2]
    return pl.pallas_call(
        pieces_kernel,
        grid=(2,),
        in_specs=[pl.BlockSpec((16, 80, cols), lambda i: (0, i, 0))] + [ANYWHERE] * len(first),
        out_specs=pl.BlockSpec((80, cols), lambda i: (i, 0)),
        out_shape=jax.ShapeDtypeStruct((160, cols), BF),
        compiler_params=VMEM,
        cost_estimate=FREE,
    )(home, *first)


def token_order_kernel(x_ref, out_ref):
    for j in range(4):
        for p in range(16):
            to, at = 40 * (16 * j + p), 40 * (4 * p + j)
            out_ref[:, to : to + 40] = x_ref[:, at : at + 40].astype(BF)


def from_piece_order(x):
    return pl.pallas_call(
        token_order_kernel, out_shape=jax.ShapeDtypeStruct(x.shape, BF), compiler_params=VMEM, cost_estimate=FREE
    )(x)


def shards(
    tokens,
    lengths,
    attn_gain,
    w_query,
    w_keyval,
    w_output,
    mlp_gain,
    w_gate,
    w_up,
    w_down,
    cotangent,
):
    t = lax.axis_index(T)
    me = lax.axis_index(Y)
    piece = lax.axis_index(CONTEXT)
    head_dim = 256
    query_scale = head_dim ** (-0.5)
    seq_count = 2560
    padding = seq_count - lengths[0]
    row_start = piece * 160
    turned_index = row_start + (jnp.arange(160, dtype=jnp.int32) + t * 80) % 160
    live_turned = turned_index >= padding
    live_mine = live_turned[:80, None]

    x_low = to_piece_order(lax.dynamic_slice_in_dim(tokens[0], t * 80, 80, 0))
    cot_mine = to_piece_order(lax.dynamic_slice_in_dim(cotangent[0], t * 80, 80, 0))
    grad_mine = jnp.where(live_mine, cot_mine, jnp.zeros_like(cot_mine))
    x_mine = x_low.astype(F32)
    x_blocks = ring_blocks(x_low, Y)
    out_rows = place(ring_blocks(w_output, Y), Y).reshape(160, 1280)
    w_out = lax.all_gather(out_rows, CONTEXT, axis=0, tiled=True)

    keyval_half = lax.dynamic_slice_in_dim(w_keyval, t * 256, 256, 1)
    gains = jnp.concatenate([attn_gain, mlp_gain])[None, :]
    gains = jnp.pad(gains, ((0, 7), (0, 48)))
    attn_blocks = pack_attention(w_query, keyval_half, gains)
    attn_rows = place(to_owners(attn_blocks), Y, sign=-1)
    attn_copies = jnp.broadcast_to(attn_rows[None], (16, 4, 48, 384))
    attn_all = exchange(attn_copies, CONTEXT).reshape(64, 48, 384)
    w_qkv = attn_all[:, :40].reshape(2560, 384)
    gain_one = attn_all[:, 40, :40].reshape(1, 2560).astype(F32)
    gain_two = attn_all[:, 40, 40:80].reshape(1, 2560).astype(F32)
    x_own = place(x_blocks, Y, attn_all)
    x_other = shift(x_own, T, 1)
    mlp_blocks = pack_mlp(w_gate, w_up, w_down)
    mlp_got = to_owners(mlp_blocks)
    mlp_block = place(mlp_got, Y, x_own, sign=-1).reshape(160, 3072)
    w_mlp = lax.all_gather(mlp_block, CONTEXT, axis=0, tiled=True)

    normed, projected = project(x_own, x_other, gain_one, w_qkv)
    home = exchange(projected, Y)
    cosine, sine = angles(turned_index - padding, head_dim)
    queries, kv_own = prepare(home, cosine, sine, query_scale)
    kv_mine = exchange(jnp.broadcast_to(kv_own[None], (16, 160, 256)), CONTEXT).reshape(2560, 256)
    grad_own = place(ring_blocks(after(grad_mine, kv_own), Y), Y).reshape(320, 2560)
    grad_group = jnp.concatenate([grad_own, shift(grad_own, T, 1)])
    kv_mine = after(kv_mine, grad_own)
    kv_other = shift(kv_mine, T, 1)
    keys = jnp.where(t == 0, kv_mine, kv_other)
    values = jnp.where(t == 0, kv_other, kv_mine)

    key_index = jnp.arange(seq_count, dtype=jnp.int32)
    offset = turned_index[:, None] - key_index[None, :]
    allowed = ((offset >= 0) & (offset < WINDOW) & (key_index >= padding)[None, :])[None]
    live = live_turned[None, :, None]
    scores = jnp.einsum("hqd,kd->hqk", queries, keys, preferred_element_type=F32)
    row_top = jnp.max(jnp.where(allowed, scores, NEGATIVE_FILL), axis=-1, keepdims=True)
    row_top = jnp.where(live, row_top, 0.0)
    weights_exp = jnp.where(allowed, jnp.exp(scores - row_top), 0.0)
    row_total = jnp.where(live, jnp.sum(weights_exp, axis=-1, keepdims=True), 1.0)
    prob = weights_exp / row_total
    prob_low = prob.astype(BF)
    attended = jnp.einsum("hqk,kd->qhd", prob_low, values, preferred_element_type=F32)
    attended = attended.reshape(160, 1280).astype(BF)

    branch = dot(attended, w_out, 1, 1)
    hidden_mine = x_mine + branch[:80] + shift(branch[80:], T, 1)

    inverse_two = inverse_root(hidden_mine)
    normed_two_mine = (hidden_mine * inverse_two * gain_two).astype(BF)
    normed_two = jnp.concatenate(gather_rows(after(normed_two_mine, grad_group)))
    hidden, grad_gate, grad_up = feed_forward(normed_two, grad_group, w_mlp)
    normed_two_low = core_sum(*row_products((grad_gate, grad_up), w_mlp, 0, 1024))
    got = own_and_received(normed_two_low, Y, 0)

    mlp_rows = row_products((hidden,), w_mlp, 2, 1024, normed_two_low)
    mlp_part = mlp_grads(
        normed_two, grad_group, grad_gate, grad_up, hidden, *got, *mlp_rows
    )
    mlp_sum = lax.psum_scatter(mlp_part, CONTEXT, scatter_dimension=0, tiled=True)
    grad_normed_two = sum(block.astype(F32) for block in got)

    grad_h_mine = grad_mine.astype(F32) + norm_back(
        grad_normed_two, hidden_mine, inverse_two, gain_two
    )
    branch_mine = grad_h_mine.astype(BF)
    branch_low = jnp.concatenate([branch_mine, shift(branch_mine, T, 1)])
    grad_attended = dot(branch_low, w_out, 1, 0).astype(BF).reshape(160, 5, head_dim)

    grad_prob = jnp.einsum("qhd,kd->hqk", grad_attended, values, preferred_element_type=F32)
    spread = jnp.sum(prob * grad_prob, axis=-1, keepdims=True)
    grad_scores = (prob * (grad_prob - spread)).astype(BF)
    grad_keys = jnp.einsum("hqk,hqd->kd", grad_scores, queries, preferred_element_type=F32)
    grad_values = jnp.einsum("hqk,qhd->kd", prob_low, grad_attended, preferred_element_type=F32)
    keep = jnp.where(t == 0, grad_keys, grad_values)
    give = jnp.where(t == 0, grad_values, grad_keys).astype(BF)
    grad_queries = jnp.einsum("hqk,kd->hqd", grad_scores, keys, preferred_element_type=F32)
    query_blocks = unturn(grad_queries, cosine, sine, query_scale)
    kv_part = (keep + shift(give, T, 1).astype(F32)).astype(BF).reshape(16, 160, 256)
    kv_part = after(kv_part, query_blocks)
    kv_home = exchange(kv_part, CONTEXT)
    branch_own = place(ring_blocks(after(branch_mine, kv_part), Y), Y).reshape(320, 2560)
    branch_other = shift(branch_own, T, 1)
    grad_query_group = columns_out(query_blocks)
    attended_group = columns_out(quarters(attended))
    kv_home = after(kv_home, branch_own, attended_group)
    grad_kv_group = columns_out(unturn_kv(kv_home, cosine, sine))
    grad_qkv = jnp.concatenate([grad_query_group, grad_kv_group], axis=1)
    normed_low = core_sum(*row_products((grad_qkv,), w_qkv, 0, 384))
    part_home = exchange(outer(normed, grad_qkv, branch_own, branch_other, attended_group), CONTEXT)
    (grad_normed,) = sums((own_and_received(normed_low, Y, 0),), (F32,))
    (mlp_mine,) = sums((own_and_received(after(core_sum(*mlp_rows), normed_low), Y, 0),), (F32,))
    inverse_one = inverse_root(x_mine)
    tokens_mine = from_piece_order(
        grad_h_mine + norm_back(grad_normed, x_mine, inverse_one, gain_one)
    )
    block_mine = from_piece_order(jnp.where(live_mine, hidden_mine + mlp_mine, 0.0))
    mlp_home = to_owners(mlp_sum)
    home = to_owners(pieces_sum(part_home))
    query_grad, kv_half, output_grad, gate_grad, up_grad, down_grad, gain_part, block_out, tokens_grad = owners(
        home,
        mlp_home,
        w_query,
        keyval_half,
        w_gate,
        w_up,
        (block_mine, shift(block_mine, T, 1)),
        (tokens_mine, shift(tokens_mine, T, 1)),
    )

    mine = jnp.concatenate([kv_half, gain_part], axis=1)
    other = shift(mine, T, 1)
    kv_other = other[:, :256]
    keyval_grad = jnp.where(
        t == 0,
        jnp.concatenate([kv_half, kv_other], axis=1),
        jnp.concatenate([kv_other, kv_half], axis=1),
    )
    attn_gain_grad = (mine[:, 256] + other[:, 256]) / attn_gain.astype(F32)
    mlp_gain_grad = (mine[:, 384] + other[:, 384]) / mlp_gain.astype(F32)

    return (
        block_out[None],
        tokens_grad[None],
        attn_gain_grad,
        query_grad,
        keyval_grad,
        output_grad,
        mlp_gain_grad,
        gate_grad,
        up_grad,
        down_grad,
    )


def solution(mesh):
    torus = Mesh(
        mesh.devices.reshape(mesh.shape["shard"], 4, 4, mesh.shape["tensor"]),
        ("shard", "context_0", "context_1", "tensor"),
    )
    in_specs = (
        P("shard", CONTEXT, None),
        P("shard"),
        P(SHARD_CONTEXT),
        P(SHARD_CONTEXT, "tensor"),
        P(SHARD_CONTEXT, None),
        P(SHARD_CONTEXT, "tensor"),
        P(SHARD_CONTEXT),
        P(SHARD_CONTEXT, "tensor"),
        P(SHARD_CONTEXT, "tensor"),
        P(SHARD_CONTEXT, "tensor"),
        P("shard", CONTEXT, None),
    )
    out_specs = (
        P("shard", CONTEXT, None),
        P("shard", CONTEXT, None),
        P(SHARD_CONTEXT),
        P(SHARD_CONTEXT, "tensor"),
        P(SHARD_CONTEXT, None),
        P(SHARD_CONTEXT, "tensor"),
        P(SHARD_CONTEXT),
        P(SHARD_CONTEXT, "tensor"),
        P(SHARD_CONTEXT, "tensor"),
        P(SHARD_CONTEXT, "tensor"),
    )
    return jax.shard_map(
        shards, mesh=torus, in_specs=in_specs, out_specs=out_specs, check_vma=False
    )
```

```python
import functools

import jax
import jax.numpy as jnp
from jax import lax
from jax.experimental import pallas as pl
from jax.experimental.pallas import tpu as pltpu
from jax.sharding import Mesh
from jax.sharding import PartitionSpec as P

WINDOW = 2048
SHARD_CONTEXT = ("shard", "context_0", "context_1")
CONTEXT = ("context_0", "context_1")
PIECES = ("context_0", "context_1", "shard")
Y, X, Z, T = "shard", "context_0", "context_1", "tensor"
VMEM = pltpu.CompilerParams(vmem_limit_bytes=48 * 2**20)
ANYWHERE = pl.BlockSpec(memory_space=pl.ANY)
FREE = pl.CostEstimate(flops=0, bytes_accessed=0, transcendentals=0)

EPSILON = 1e-06
NEGATIVE_FILL = -1e30
BF = jnp.bfloat16
F32 = jnp.float32


def shift(x, axis, by):
    n = lax.axis_size(axis)
    return lax.ppermute(x, axis, [(i, (i + by) % n) for i in range(n)])


def exchange(blocks, axis):
    return lax.all_to_all(blocks, axis, 0, 0, tiled=True)


def nothing(*refs):
    pass


def after(x, *others):
    return pl.pallas_call(
        nothing,
        out_shape=jax.ShapeDtypeStruct(x.shape, x.dtype),
        in_specs=[ANYWHERE] * (1 + len(others)),
        out_specs=ANYWHERE,
        input_output_aliases={0: 0},
        compiler_params=VMEM,
        cost_estimate=FREE,
    )(x, *others)


def small_trip(x, *others):
    corner = x.reshape(-1, x.shape[-1])[:8, :128]
    return shift(after(corner, *others) if others else corner, T, 1)


def ring_blocks(x, axis):
    return [x, shift(x, axis, -1), shift(x, axis, 2), shift(x, axis, 1)]


def place_kernel(axis, sign, *refs):
    blocks, out = refs[:4], refs[-1]
    me = lax.axis_index(axis)
    for r, block in enumerate(blocks):
        out[lax.rem(me + (sign * r) % 4, 4)] = block[...]


def place(blocks, axis, *first, sign=1):
    whole = pl.BlockSpec(memory_space=pltpu.VMEM)
    return pl.pallas_call(
        functools.partial(place_kernel, axis, sign),
        out_shape=jax.ShapeDtypeStruct((4, *blocks[0].shape), blocks[0].dtype),
        in_specs=[whole] * 4 + [ANYWHERE] * len(first),
        out_specs=whole,
        compiler_params=VMEM,
        cost_estimate=FREE,
    )(*blocks, *first)


def gather_rows(mine, *first):
    own = place(ring_blocks(mine, Y), Y, *first).reshape(320, -1)
    return own, shift(own, T, 1)


def rows_kernel(count, *refs):
    lefts, rights, (far_ref, near_ref) = refs[:count], refs[count : 2 * count], refs[-2:]
    total = dot(lefts[0][...], rights[0][...], 1, 1)
    for left, right in zip(lefts[1:], rights[1:]):
        total = total + dot(left[...], right[...], 1, 1)
    near_ref[...] = total[:320].astype(BF)
    far_ref[...] = total[320:].astype(BF)


def row_products(lefts, weight, at, width, *first):
    rows, count, n = 512, len(lefts), weight.shape[0]
    half = jax.ShapeDtypeStruct((320, n), BF)
    return pl.pallas_call(
        functools.partial(rows_kernel, count),
        grid=(n // rows,),
        out_shape=(half, half),
        in_specs=[pl.BlockSpec((640, width), lambda i: (0, 0))] * count
        + [pl.BlockSpec((rows, width), lambda i, j=j: (i, at + j)) for j in range(count)]
        + [ANYWHERE] * len(first),
        out_specs=(pl.BlockSpec((320, rows), lambda i: (0, i)),) * 2,
        compiler_params=VMEM,
        cost_estimate=FREE,
    )(*lefts, *[weight] * count, *first)


def core_sum(far, near):
    return (near.astype(F32) + shift(far, T, 1).astype(F32)).astype(BF).reshape(4, 80, -1)


def own_and_received(parts, axis, dim):
    me = lax.axis_index(axis)
    own, *rest = [
        lax.dynamic_index_in_dim(parts, (me + r) % 4, dim, keepdims=False) for r in range(4)
    ]
    return [own] + [shift(rest[r - 1], axis, r) for r in (1, 3, 2)]


def sums_kernel(kinds, *refs):
    for i, out in enumerate(refs[4 * len(kinds) :]):
        total = refs[4 * i][...].astype(F32)
        for ref in refs[4 * i + 1 : 4 * i + 4]:
            total = total + ref[...].astype(F32)
        out[...] = total.astype(kinds[i])


def sums(groups, kinds):
    return pl.pallas_call(
        functools.partial(sums_kernel, kinds),
        out_shape=tuple(jax.ShapeDtypeStruct(g[0].shape, k) for g, k in zip(groups, kinds)),
        compiler_params=VMEM,
        cost_estimate=FREE,
    )(*[block for group in groups for block in group])


def outer_kernel(x_ref, g_ref, out_ref):
    out_ref[...] = dot(x_ref[...], g_ref[...], 0, 0).astype(BF).reshape(4, 160, g_ref.shape[1])


def outer(x, g):
    cols = g.shape[1]
    return pl.pallas_call(
        outer_kernel,
        grid=(4,),
        out_shape=jax.ShapeDtypeStruct((16, 160, cols), BF),
        in_specs=[
            pl.BlockSpec((640, 640), lambda i: (0, i)),
            pl.BlockSpec((640, cols), lambda i: (0, 0)),
        ],
        out_specs=pl.BlockSpec((4, 160, cols), lambda i: (i, 0, 0)),
        compiler_params=VMEM,
        cost_estimate=FREE,
    )(x, g)


def outer_output_kernel(own_ref, other_ref, ob_ref, out_ref):
    cols = ob_ref.shape[2]
    part = dot(own_ref[...], ob_ref[:, :80].reshape(320, cols), 0, 0)
    part = part + dot(other_ref[...], ob_ref[:, 80:].reshape(320, cols), 0, 0)
    out_ref[...] = part.reshape(16, 40, cols).astype(BF)


def outer_output(own, other, ob):
    cols = 640
    half = pl.BlockSpec((320, 640), lambda i: (0, 0))
    return pl.pallas_call(
        outer_output_kernel,
        grid=(2,),
        out_shape=jax.ShapeDtypeStruct((16, 40, 1280), BF),
        in_specs=[half, half, pl.BlockSpec((4, 160, cols), lambda i: (0, 0, i))],
        out_specs=pl.BlockSpec((16, 40, cols), lambda i: (0, 0, i)),
        compiler_params=VMEM,
        cost_estimate=FREE,
    )(own, other, ob)


def to_owners(sums):
    me = lax.axis_index(Y)
    rows = sums.reshape(4, -1, sums.shape[-1])
    got = []
    for r in range(4):
        block = lax.dynamic_index_in_dim(rows, (me + r) % 4, 0, keepdims=False)
        got.append(shift(block, Y, r) if r else block)
    return got


def by_half(blocks):
    cols = blocks.shape[2]
    return blocks.reshape(4, 2, 80, cols).swapaxes(0, 1).reshape(640, cols)


def columns_out(blocks):
    me = lax.axis_index(Y)
    got = []
    for r in range(4):
        block = lax.dynamic_index_in_dim(blocks, (me + r) % 4, 0, keepdims=False)
        got.append(shift(block, Y, r) if r else block)
    return by_half(place(got, Y, sign=-1))


def quarters(x):
    rows = x.shape[0]
    return x.reshape(rows, 4, -1).swapaxes(0, 1)


def pack_attention_kernel(q_ref, kv_ref, gains_ref, attn_ref):
    attn_ref[...] = jnp.zeros_like(attn_ref)
    for j in range(4):
        attn_ref[j, :40, :320] = q_ref[:, 320 * j : 320 * j + 320]
        attn_ref[j, :40, 320:] = kv_ref[:, 64 * j : 64 * j + 64]
        attn_ref[j, 40:48, :128] = gains_ref[...]


def pack_attention(w_query, keyval_half, gains):
    return pl.pallas_call(
        pack_attention_kernel,
        out_shape=jax.ShapeDtypeStruct((4, 48, 384), BF),
        compiler_params=VMEM,
        cost_estimate=FREE,
    )(w_query, keyval_half, gains)


def pack_mlp_kernel(gate_ref, up_ref, down_ref, mlp_ref):
    mlp_ref[...] = jnp.zeros_like(mlp_ref)
    for j in range(4):
        mlp_ref[j, :, :960] = gate_ref[:, 960 * j : 960 * j + 960]
        mlp_ref[j, :, 1024:1984] = up_ref[:, 960 * j : 960 * j + 960]
        mlp_ref[j, :, 2048:3008] = down_ref[:, 960 * j : 960 * j + 960]


def pack_mlp(w_gate, w_up, w_down):
    return pl.pallas_call(
        pack_mlp_kernel,
        out_shape=jax.ShapeDtypeStruct((4, 40, 3072), BF),
        compiler_params=VMEM,
        cost_estimate=FREE,
    )(w_gate, w_up, w_down)


def down_grad_kernel(y_ref, hidden_ref, *rest):
    rest[-1][...] = dot(y_ref[...], hidden_ref[...], 0, 0).astype(BF)


def down_grads(grads, hidden, *first):
    rows = 512
    return pl.pallas_call(
        down_grad_kernel,
        grid=(2560 // rows,),
        out_shape=jax.ShapeDtypeStruct((2560, 3072), BF),
        in_specs=[
            pl.BlockSpec((640, rows), lambda i: (0, i)),
            pl.BlockSpec((640, 1024), lambda i: (0, 0)),
        ]
        + [ANYWHERE] * len(first),
        out_specs=pl.BlockSpec((rows, 1024), lambda i: (i, 2)),
        compiler_params=VMEM,
        cost_estimate=FREE,
    )(grads, hidden, *first)


def gate_up_grad_kernel(x_ref, gate_ref, up_ref, *rest):
    out_ref = rest[-1]
    out_ref[:, :1024] = dot(x_ref[...], gate_ref[...], 0, 0).astype(BF)
    out_ref[:, 1024:] = dot(x_ref[...], up_ref[...], 0, 0).astype(BF)


def gate_up_grads(normed, gate, up, held, *first):
    rows = 512
    whole = pl.BlockSpec((640, 1024), lambda i: (0, 0))
    return pl.pallas_call(
        gate_up_grad_kernel,
        grid=(2560 // rows,),
        out_shape=jax.ShapeDtypeStruct((2560, 3072), BF),
        in_specs=[pl.BlockSpec((640, rows), lambda i: (0, i)), whole, whole]
        + [ANYWHERE] * (1 + len(first)),
        out_specs=pl.BlockSpec((rows, 2048), lambda i: (i, 0)),
        input_output_aliases={3: 0},
        compiler_params=VMEM,
        cost_estimate=FREE,
    )(normed, gate, up, held, *first)


def feed_forward_kernel(x_ref, y_ref, gate_ref, up_ref, down_ref, *rest):
    hidden_out, gate_out, up_out = rest[-3:]
    gate = dot(x_ref[...], gate_ref[...], 1, 0)
    up = dot(x_ref[...], up_ref[...], 1, 0)
    grad = dot(y_ref[...], down_ref[...], 1, 0)
    scale = 0.7978845608028654
    square = gate * gate
    bent = jnp.tanh(scale * gate * (1.0 + 0.044715 * square))
    share = 0.5 * (1.0 + bent)
    slope = share + 0.5 * gate * (1.0 - bent * bent) * scale * (1.0 + 0.134145 * square)
    active = gate * share
    hidden_out[...] = (active * up).astype(BF)
    gate_out[...] = (grad * up * slope).astype(BF)
    up_out[...] = (grad * active).astype(BF)


def feed_forward(x, y, w_mlp, *first):
    cols = 256
    steps = 1024 // cols
    part = jax.ShapeDtypeStruct((640, 1024), BF)
    whole = pl.BlockSpec((640, 2560), lambda j: (0, 0))
    out = pl.BlockSpec((640, cols), lambda j: (0, j))
    return pl.pallas_call(
        feed_forward_kernel,
        grid=(steps,),
        out_shape=(part, part, part),
        in_specs=[whole, whole]
        + [pl.BlockSpec((2560, cols), lambda j, k=k: (0, k * steps + j)) for k in range(3)]
        + [ANYWHERE] * len(first),
        out_specs=(out, out, out),
        compiler_params=VMEM,
        cost_estimate=FREE,
    )(x, y, w_mlp, w_mlp, w_mlp, *first)


def to_piece_order(x):
    rows = x.shape[0]
    return x.reshape(rows, 4, 16, 40).swapaxes(1, 2).reshape(rows, 2560)


def inverse_root(values):
    return lax.rsqrt(jnp.mean(values * values, axis=-1, keepdims=True) + EPSILON)


def norm_back(grad, values, inverse, gain):
    scaled = gain * grad
    return inverse * scaled - values * inverse**3 * jnp.mean(
        scaled * values, axis=-1, keepdims=True
    )


def angles(position, head_dim):
    quarter = head_dim // 4
    frequency = 10000.0 ** (-jnp.arange(quarter, dtype=F32) / quarter)
    phase_angle = position[:, None].astype(F32) * frequency[None, :]
    return (jnp.cos(phase_angle), jnp.sin(phase_angle))


def dot(a, b, da, db):
    return lax.dot_general(a, b, (((da,), (db,)), ((), ())), preferred_element_type=F32)


def feature_quarters_kernel(x_ref, out_ref):
    for j in range(4):
        for p in range(16):
            at = 40 * (4 * p + j)
            out_ref[j, :, 40 * p : 40 * p + 40] = x_ref[:, at : at + 40].astype(BF)


def feature_quarters(x):
    return pl.pallas_call(
        feature_quarters_kernel,
        out_shape=jax.ShapeDtypeStruct((4, 80, 640), BF),
        compiler_params=VMEM,
        cost_estimate=FREE,
    )(x)


def project_kernel(own_ref, other_ref, gain_ref, weight_ref, *rest):
    normed_ref, out_ref = rest[-2:]

    def rows(block):
        x = block[0].astype(F32)
        normed = (x * inverse_root(x) * gain_ref[...]).astype(BF)
        normed_ref[...] = normed
        out_ref[0] = dot(normed, weight_ref[...], 1, 0).astype(BF)

    i = pl.program_id(0)

    @pl.when(i < 4)
    def _():
        rows(own_ref)

    @pl.when(i >= 4)
    def _():
        rows(other_ref)


def project(own, other, gain, weight, *first):
    return pl.pallas_call(
        project_kernel,
        grid=(8,),
        out_shape=(
            jax.ShapeDtypeStruct((640, 2560), BF),
            jax.ShapeDtypeStruct((4, 160, 384), BF),
        ),
        in_specs=[
            pl.BlockSpec((1, 80, 2560), lambda i: (jnp.minimum(i, 3), 0, 0)),
            pl.BlockSpec((1, 80, 2560), lambda i: (jnp.maximum(i, 4) - 4, 0, 0)),
            pl.BlockSpec((1, 2560), lambda i: (0, 0)),
            pl.BlockSpec((2560, 384), lambda i: (0, 0)),
        ]
        + [ANYWHERE] * len(first),
        out_specs=(
            pl.BlockSpec((80, 2560), lambda i: (i, 0)),
            pl.BlockSpec((1, 80, 384), lambda i: (i % 4, i // 4, 0)),
        ),
        compiler_params=VMEM,
        cost_estimate=FREE,
    )(own, other, gain, weight, *first)


def owners_kernel(*refs):
    home, mlp = refs[:4], refs[4:8]
    output_home, query_ref, keyval_ref, gate_ref, up_ref, block_mine, block_other, rows_mine, rows_other = refs[8:17]
    query_out, keyval_out, output_out, gate_out, up_out, down_out, gain_out, block_out, rows_out = refs[17:26]
    held, held_mlp = refs[26:]
    me = lax.axis_index(Y)
    for r in range(4):
        held[lax.rem(me + 4 - r, 4)] = home[r][...]
        held_mlp[lax.rem(me + 4 - r, 4)] = mlp[r][...]
    for j in range(4):
        columns = slice(960 * j, 960 * j + 960)
        gate_out[:, columns] = held_mlp[j, :, :960].astype(F32)
        up_out[:, columns] = held_mlp[j, :, 1024:1984].astype(F32)
        down_out[:, columns] = held_mlp[j, :, 2048:3008].astype(F32)
        total = held[j].astype(F32)
        query_out[:, 320 * j : 320 * j + 320] = total[:, :320]
        keyval_out[:, 64 * j : 64 * j + 64] = total[:, 320:384]
    total = output_home[0].astype(F32)
    for p in range(1, 16):
        total = total + output_home[p].astype(F32)
    output_out[...] = total

    def products(weight, grad):
        return jnp.sum(weight[...].astype(F32) * grad[...], axis=1, keepdims=True)

    one = products(query_ref, query_out) + products(keyval_ref, keyval_out)
    two = products(gate_ref, gate_out) + products(up_ref, up_out)
    gain_out[:, :128] = jnp.broadcast_to(one, (40, 128))
    gain_out[:, 128:] = jnp.broadcast_to(two, (40, 128))
    at = 80 * lax.axis_index(T)
    for mine, other, out in ((block_mine, block_other, block_out), (rows_mine, rows_other, rows_out)):
        out[pl.ds(pl.multiple_of(at, 16), 80), :] = mine[...]
        out[pl.ds(pl.multiple_of(80 - at, 16), 80), :] = other[...]


def owners(home, mlp, output_home, w_query, keyval_half, w_gate, w_up, block, rows):
    wide, narrow = (jax.ShapeDtypeStruct((40, n), F32) for n in (3840, 1280))
    small = jax.ShapeDtypeStruct((40, 256), F32)
    tokens = jax.ShapeDtypeStruct((160, 2560), BF)
    return pl.pallas_call(
        owners_kernel,
        out_shape=(narrow, small, narrow, wide, wide, wide, small, tokens, tokens),
        scratch_shapes=[pltpu.VMEM((4, 40, 384), BF), pltpu.VMEM((4, 40, 3072), BF)],
        compiler_params=VMEM,
        cost_estimate=FREE,
    )(*home, *mlp, output_home, w_query, keyval_half, w_gate, w_up, *block, *rows)


def turned(values, cosine, sine):
    one, two = values[:, :64], values[:, 64:128]
    return jnp.concatenate(
        [one * cosine - two * sine, two * cosine + one * sine, values[:, 128:]], axis=1
    )


def prepare_kernel(scale, home_ref, cosine_ref, sine_ref, query_ref, kv_ref, wide):
    cosine, sine = cosine_ref[...], sine_ref[...]
    for j in range(4):
        wide[:, 320 * j : 320 * j + 320] = home_ref[j, :, :320].astype(F32)
    for h in range(5):
        head = turned(wide[:, 256 * h : 256 * h + 256], cosine, sine)
        query_ref[h] = (head * scale).astype(BF)
    for j in range(4):
        wide[:, 64 * j : 64 * j + 64] = home_ref[j, :, 320:].astype(F32)
    first = lax.axis_index(T) == 0
    kv = wide[:, :256]
    kv = jnp.where(first, turned(kv, cosine, sine), kv).astype(BF)
    at = 80 * lax.axis_index(T)
    kv_ref[pl.ds(pl.multiple_of(at, 16), 80), :] = kv[:80]
    kv_ref[pl.ds(pl.multiple_of(80 - at, 16), 80), :] = kv[80:]


def prepare(home, cosine, sine, scale):
    return pl.pallas_call(
        functools.partial(prepare_kernel, scale),
        out_shape=(
            jax.ShapeDtypeStruct((5, 160, 256), BF),
            jax.ShapeDtypeStruct((160, 256), BF),
        ),
        scratch_shapes=[pltpu.VMEM((160, 1280), F32)],
        compiler_params=VMEM,
        cost_estimate=FREE,
    )(home, cosine, sine)


def unturn_kernel(scale, grad_ref, cosine_ref, sine_ref, out_ref, wide):
    cosine, sine = cosine_ref[...], -sine_ref[...]
    for h in range(5):
        wide[:, 256 * h : 256 * h + 256] = turned(grad_ref[h] * scale, cosine, sine)
    for j in range(4):
        out_ref[j] = wide[:, 320 * j : 320 * j + 320].astype(BF)


def unturn(grad, cosine, sine, scale):
    return pl.pallas_call(
        functools.partial(unturn_kernel, scale),
        out_shape=jax.ShapeDtypeStruct((4, 160, 320), BF),
        scratch_shapes=[pltpu.VMEM((160, 1280), F32)],
        compiler_params=VMEM,
        cost_estimate=FREE,
    )(grad, cosine, sine)


def unturn_kv_kernel(home_ref, cosine_ref, sine_ref, out_ref, held):
    total = home_ref[0].astype(F32)
    for p in range(1, 16):
        total = total + home_ref[p].astype(F32)
    held[...] = total
    at = 80 * lax.axis_index(T)
    total = jnp.concatenate(
        [held[pl.ds(pl.multiple_of(at, 16), 80), :], held[pl.ds(pl.multiple_of(80 - at, 16), 80), :]]
    )
    back = turned(total, cosine_ref[...], -sine_ref[...])
    total = jnp.where(lax.axis_index(T) == 0, back, total).astype(BF)
    for j in range(4):
        out_ref[j] = total[:, 64 * j : 64 * j + 64]


def unturn_kv(home, cosine, sine):
    return pl.pallas_call(
        unturn_kv_kernel,
        out_shape=jax.ShapeDtypeStruct((4, 160, 64), BF),
        scratch_shapes=[pltpu.VMEM((160, 256), F32)],
        compiler_params=VMEM,
        cost_estimate=FREE,
    )(home, cosine, sine)


def pieces_kernel(home_ref, out_ref):
    total = home_ref[0].astype(F32)
    for p in range(1, 16):
        total = total + home_ref[p].astype(F32)
    out_ref[...] = total.astype(BF)


def pieces_sum(home):
    cols = home.shape[2]
    return pl.pallas_call(
        pieces_kernel,
        grid=(2,),
        in_specs=[pl.BlockSpec((16, 80, cols), lambda i: (0, i, 0))],
        out_specs=pl.BlockSpec((80, cols), lambda i: (i, 0)),
        out_shape=jax.ShapeDtypeStruct((160, cols), BF),
        compiler_params=VMEM,
        cost_estimate=FREE,
    )(home)


def token_order_kernel(x_ref, out_ref):
    for j in range(4):
        for p in range(16):
            to, at = 40 * (16 * j + p), 40 * (4 * p + j)
            out_ref[:, to : to + 40] = x_ref[:, at : at + 40].astype(BF)


def from_piece_order(x):
    return pl.pallas_call(
        token_order_kernel, out_shape=jax.ShapeDtypeStruct(x.shape, BF), compiler_params=VMEM, cost_estimate=FREE
    )(x)


def shards(
    tokens,
    lengths,
    attn_gain,
    w_query,
    w_keyval,
    w_output,
    mlp_gain,
    w_gate,
    w_up,
    w_down,
    cotangent,
):
    t = lax.axis_index(T)
    me = lax.axis_index(Y)
    piece = lax.axis_index(CONTEXT)
    head_dim = 256
    query_scale = head_dim ** (-0.5)
    seq_count = 2560
    padding = seq_count - lengths[0]
    row_start = piece * 160
    turned_index = row_start + (jnp.arange(160, dtype=jnp.int32) + t * 80) % 160
    live_turned = turned_index >= padding
    live_mine = live_turned[:80, None]

    x_low = to_piece_order(lax.dynamic_slice_in_dim(tokens[0], t * 80, 80, 0))
    cot_mine = to_piece_order(lax.dynamic_slice_in_dim(cotangent[0], t * 80, 80, 0))
    grad_mine = jnp.where(live_mine, cot_mine, jnp.zeros_like(cot_mine))
    x_mine = x_low.astype(F32)
    x_blocks = ring_blocks(x_low, Y)
    out_rows = place(ring_blocks(w_output, Y), Y).reshape(160, 1280)
    w_out = lax.all_gather(out_rows, CONTEXT, axis=0, tiled=True)

    keyval_half = lax.dynamic_slice_in_dim(w_keyval, t * 256, 256, 1)
    gains = jnp.concatenate([attn_gain, mlp_gain])[None, :]
    gains = jnp.pad(gains, ((0, 7), (0, 48)))
    attn_blocks = pack_attention(w_query, keyval_half, gains)
    attn_rows = place(to_owners(attn_blocks), Y, sign=-1)
    attn_copies = jnp.broadcast_to(attn_rows[None], (16, 4, 48, 384))
    attn_all = exchange(attn_copies, CONTEXT).reshape(64, 48, 384)
    w_qkv = attn_all[:, :40].reshape(2560, 384)
    gain_one = attn_all[:, 40, :40].reshape(1, 2560).astype(F32)
    gain_two = attn_all[:, 40, 40:80].reshape(1, 2560).astype(F32)
    x_own = place(x_blocks, Y, attn_all)
    x_other = shift(x_own, T, 1)
    mlp_blocks = pack_mlp(w_gate, w_up, w_down)
    mlp_got = to_owners(mlp_blocks)
    mlp_block = place(mlp_got, Y, x_own, sign=-1).reshape(160, 3072)
    w_mlp = lax.all_gather(mlp_block, CONTEXT, axis=0, tiled=True)

    normed, projected = project(x_own, x_other, gain_one, w_qkv)
    home = exchange(projected, Y)
    cosine, sine = angles(turned_index - padding, head_dim)
    queries, kv_own = prepare(home, cosine, sine, query_scale)
    kv_mine = exchange(jnp.broadcast_to(kv_own[None], (16, 160, 256)), CONTEXT).reshape(2560, 256)
    grad_own = place(ring_blocks(after(grad_mine, kv_own), Y), Y).reshape(320, 2560)
    grad_group = jnp.concatenate([grad_own, shift(grad_own, T, 1)])
    kv_mine = after(kv_mine, grad_own)
    kv_other = shift(kv_mine, T, 1)
    keys = jnp.where(t == 0, kv_mine, kv_other)
    values = jnp.where(t == 0, kv_other, kv_mine)

    key_index = jnp.arange(seq_count, dtype=jnp.int32)
    offset = turned_index[:, None] - key_index[None, :]
    allowed = ((offset >= 0) & (offset < WINDOW) & (key_index >= padding)[None, :])[None]
    live = live_turned[None, :, None]
    scores = jnp.einsum("hqd,kd->hqk", queries, keys, preferred_element_type=F32)
    row_top = jnp.max(jnp.where(allowed, scores, NEGATIVE_FILL), axis=-1, keepdims=True)
    row_top = jnp.where(live, row_top, 0.0)
    weights_exp = jnp.where(allowed, jnp.exp(scores - row_top), 0.0)
    row_total = jnp.where(live, jnp.sum(weights_exp, axis=-1, keepdims=True), 1.0)
    prob = weights_exp / row_total
    prob_low = prob.astype(BF)
    attended = jnp.einsum("hqk,kd->qhd", prob_low, values, preferred_element_type=F32)
    attended = attended.reshape(160, 1280).astype(BF)

    branch = dot(attended, w_out, 1, 1)
    hidden_mine = x_mine + branch[:80] + shift(branch[80:], T, 1)

    inverse_two = inverse_root(hidden_mine)
    normed_two_mine = (hidden_mine * inverse_two * gain_two).astype(BF)
    normed_two = jnp.concatenate(gather_rows(after(normed_two_mine, grad_group)))
    hidden, grad_gate, grad_up = feed_forward(normed_two, grad_group, w_mlp)
    attended_group = place(ring_blocks(attended, Y), Y)
    normed_two_low = core_sum(*row_products((grad_gate, grad_up), w_mlp, 0, 1024, attended_group))
    got = own_and_received(normed_two_low, Y, 0)

    mlp_rows = row_products((hidden,), w_mlp, 2, 1024, normed_two_low)
    down_part = down_grads(grad_group, hidden, *mlp_rows)
    mlp_part = gate_up_grads(normed_two, grad_gate, grad_up, down_part, *got)
    mlp_sum = lax.psum_scatter(mlp_part, CONTEXT, scatter_dimension=0, tiled=True)
    grad_normed_two = sum(block.astype(F32) for block in got)

    grad_h_mine = grad_mine.astype(F32) + norm_back(
        grad_normed_two, hidden_mine, inverse_two, gain_two
    )
    branch_mine = grad_h_mine.astype(BF)
    branch_own = place(to_owners(feature_quarters(grad_h_mine)), Y, sign=-1).reshape(320, 640)
    branch_other = shift(branch_own, T, 1)
    branch_low = jnp.concatenate([branch_mine, shift(branch_mine, T, 1)])
    grad_attended = dot(branch_low, w_out, 1, 0).astype(BF).reshape(160, 5, head_dim)

    grad_prob = jnp.einsum("qhd,kd->hqk", grad_attended, values, preferred_element_type=F32)
    spread = jnp.sum(prob * grad_prob, axis=-1, keepdims=True)
    grad_scores = (prob * (grad_prob - spread)).astype(BF)
    grad_keys = jnp.einsum("hqk,hqd->kd", grad_scores, queries, preferred_element_type=F32)
    grad_values = jnp.einsum("hqk,qhd->kd", prob_low, grad_attended, preferred_element_type=F32)
    keep = jnp.where(t == 0, grad_keys, grad_values)
    give = jnp.where(t == 0, grad_values, grad_keys).astype(BF)
    grad_queries = jnp.einsum("hqk,kd->hqd", grad_scores, keys, preferred_element_type=F32)
    query_blocks = unturn(grad_queries, cosine, sine, query_scale)
    kv_part = (keep + shift(give, T, 1).astype(F32)).astype(BF).reshape(16, 160, 256)
    kv_part = after(kv_part, query_blocks)
    kv_home = exchange(kv_part, CONTEXT)
    grad_query_group = columns_out(query_blocks)
    output_part = outer_output(branch_own, branch_other, attended_group)
    output_home = exchange(after(output_part, kv_home), CONTEXT)
    kv_home = after(kv_home, output_part)
    grad_kv_group = columns_out(unturn_kv(kv_home, cosine, sine))
    grad_qkv = jnp.concatenate([grad_query_group, grad_kv_group], axis=1)
    normed_low = core_sum(*row_products((grad_qkv,), w_qkv, 0, 384))
    part_home = exchange(after(outer(normed, grad_qkv), output_home), CONTEXT)
    (grad_normed,) = sums((own_and_received(normed_low, Y, 0),), (F32,))
    (mlp_mine,) = sums((own_and_received(after(core_sum(*mlp_rows), normed_low), Y, 0),), (F32,))
    inverse_one = inverse_root(x_mine)
    tokens_mine = from_piece_order(
        grad_h_mine + norm_back(grad_normed, x_mine, inverse_one, gain_one)
    )
    block_mine = from_piece_order(jnp.where(live_mine, hidden_mine + mlp_mine, 0.0))
    mlp_home = to_owners(mlp_sum)
    home = to_owners(pieces_sum(part_home))
    query_grad, kv_half, output_grad, gate_grad, up_grad, down_grad, gain_part, block_out, tokens_grad = owners(
        home,
        mlp_home,
        output_home,
        w_query,
        keyval_half,
        w_gate,
        w_up,
        (block_mine, shift(block_mine, T, 1)),
        (tokens_mine, shift(tokens_mine, T, 1)),
    )

    mine = jnp.concatenate([kv_half, gain_part], axis=1)
    other = shift(mine, T, 1)
    kv_other = other[:, :256]
    keyval_grad = jnp.where(
        t == 0,
        jnp.concatenate([kv_half, kv_other], axis=1),
        jnp.concatenate([kv_other, kv_half], axis=1),
    )
    attn_gain_grad = (mine[:, 256] + other[:, 256]) / attn_gain.astype(F32)
    mlp_gain_grad = (mine[:, 384] + other[:, 384]) / mlp_gain.astype(F32)

    return (
        block_out[None],
        tokens_grad[None],
        attn_gain_grad,
        query_grad,
        keyval_grad,
        output_grad,
        mlp_gain_grad,
        gate_grad,
        up_grad,
        down_grad,
    )


def solution(mesh):
    torus = Mesh(
        mesh.devices.reshape(mesh.shape["shard"], 4, 4, mesh.shape["tensor"]),
        ("shard", "context_0", "context_1", "tensor"),
    )
    in_specs = (
        P("shard", CONTEXT, None),
        P("shard"),
        P(SHARD_CONTEXT),
        P(SHARD_CONTEXT, "tensor"),
        P(SHARD_CONTEXT, None),
        P(SHARD_CONTEXT, "tensor"),
        P(SHARD_CONTEXT),
        P(SHARD_CONTEXT, "tensor"),
        P(SHARD_CONTEXT, "tensor"),
        P(SHARD_CONTEXT, "tensor"),
        P("shard", CONTEXT, None),
    )
    out_specs = (
        P("shard", CONTEXT, None),
        P("shard", CONTEXT, None),
        P(SHARD_CONTEXT),
        P(SHARD_CONTEXT, "tensor"),
        P(SHARD_CONTEXT, None),
        P(SHARD_CONTEXT, "tensor"),
        P(SHARD_CONTEXT),
        P(SHARD_CONTEXT, "tensor"),
        P(SHARD_CONTEXT, "tensor"),
        P(SHARD_CONTEXT, "tensor"),
    )
    return jax.shard_map(
        shards, mesh=torus, in_specs=in_specs, out_specs=out_specs, check_vma=False
    )
```

```python
import functools

import jax
import jax.numpy as jnp
from jax import lax
from jax.experimental import pallas as pl
from jax.experimental.pallas import tpu as pltpu
from jax.sharding import Mesh
from jax.sharding import PartitionSpec as P

WINDOW = 2048
SHARD_CONTEXT = ("shard", "context_0", "context_1")
CONTEXT = ("context_0", "context_1")
PIECES = ("context_0", "context_1", "shard")
Y, X, Z, T = "shard", "context_0", "context_1", "tensor"
VMEM = pltpu.CompilerParams(vmem_limit_bytes=48 * 2**20)
ANYWHERE = pl.BlockSpec(memory_space=pl.ANY)
FREE = pl.CostEstimate(flops=0, bytes_accessed=0, transcendentals=0)

EPSILON = 1e-06
NEGATIVE_FILL = -1e30
BF = jnp.bfloat16
F32 = jnp.float32


def shift(x, axis, by):
    n = lax.axis_size(axis)
    return lax.ppermute(x, axis, [(i, (i + by) % n) for i in range(n)])


def exchange(blocks, axis):
    return lax.all_to_all(blocks, axis, 0, 0, tiled=True)


def nothing(*refs):
    pass


def after(x, *others):
    return pl.pallas_call(
        nothing,
        out_shape=jax.ShapeDtypeStruct(x.shape, x.dtype),
        in_specs=[ANYWHERE] * (1 + len(others)),
        out_specs=ANYWHERE,
        input_output_aliases={0: 0},
        compiler_params=VMEM,
        cost_estimate=FREE,
    )(x, *others)


def small_trip(x, *others):
    corner = x.reshape(-1, x.shape[-1])[:8, :128]
    return shift(after(corner, *others) if others else corner, T, 1)


def ring_blocks(x, axis):
    return [x, shift(x, axis, -1), shift(x, axis, 2), shift(x, axis, 1)]


def place_kernel(axis, sign, *refs):
    blocks, out = refs[:4], refs[-1]
    me = lax.axis_index(axis)
    for r, block in enumerate(blocks):
        out[lax.rem(me + (sign * r) % 4, 4)] = block[...]


def place(blocks, axis, *first, sign=1):
    whole = pl.BlockSpec(memory_space=pltpu.VMEM)
    return pl.pallas_call(
        functools.partial(place_kernel, axis, sign),
        out_shape=jax.ShapeDtypeStruct((4, *blocks[0].shape), blocks[0].dtype),
        in_specs=[whole] * 4 + [ANYWHERE] * len(first),
        out_specs=whole,
        compiler_params=VMEM,
        cost_estimate=FREE,
    )(*blocks, *first)


def gather_rows(mine, *first):
    own = place(ring_blocks(mine, Y), Y, *first).reshape(320, -1)
    return own, shift(own, T, 1)


def rows_kernel(count, *refs):
    lefts, rights, (far_ref, near_ref) = refs[:count], refs[count : 2 * count], refs[-2:]
    total = dot(lefts[0][...], rights[0][...], 1, 1)
    for left, right in zip(lefts[1:], rights[1:]):
        total = total + dot(left[...], right[...], 1, 1)
    near_ref[...] = total[:320].astype(BF)
    far_ref[...] = total[320:].astype(BF)


def row_products(lefts, weight, at, width, *first):
    rows, count, n = 512, len(lefts), weight.shape[0]
    half = jax.ShapeDtypeStruct((320, n), BF)
    return pl.pallas_call(
        functools.partial(rows_kernel, count),
        grid=(n // rows,),
        out_shape=(half, half),
        in_specs=[pl.BlockSpec((640, width), lambda i: (0, 0))] * count
        + [pl.BlockSpec((rows, width), lambda i, j=j: (i, at + j)) for j in range(count)]
        + [ANYWHERE] * len(first),
        out_specs=(pl.BlockSpec((320, rows), lambda i: (0, i)),) * 2,
        compiler_params=VMEM,
        cost_estimate=FREE,
    )(*lefts, *[weight] * count, *first)


def core_sum(far, near):
    return (near.astype(F32) + shift(far, T, 1).astype(F32)).astype(BF).reshape(4, 80, -1)


def own_and_received(parts, axis, dim):
    me = lax.axis_index(axis)
    own, *rest = [
        lax.dynamic_index_in_dim(parts, (me + r) % 4, dim, keepdims=False) for r in range(4)
    ]
    return [own] + [shift(rest[r - 1], axis, r) for r in (1, 3, 2)]


def sums_kernel(kinds, *refs):
    for i, out in enumerate(refs[4 * len(kinds) :]):
        total = refs[4 * i][...].astype(F32)
        for ref in refs[4 * i + 1 : 4 * i + 4]:
            total = total + ref[...].astype(F32)
        out[...] = total.astype(kinds[i])


def sums(groups, kinds):
    return pl.pallas_call(
        functools.partial(sums_kernel, kinds),
        out_shape=tuple(jax.ShapeDtypeStruct(g[0].shape, k) for g, k in zip(groups, kinds)),
        compiler_params=VMEM,
        cost_estimate=FREE,
    )(*[block for group in groups for block in group])


def outer_kernel(x_ref, g_ref, out_ref):
    out_ref[...] = dot(x_ref[...], g_ref[...], 0, 0).astype(BF).reshape(4, 160, g_ref.shape[1])


def outer(x, g):
    cols = g.shape[1]
    return pl.pallas_call(
        outer_kernel,
        grid=(4,),
        out_shape=jax.ShapeDtypeStruct((16, 160, cols), BF),
        in_specs=[
            pl.BlockSpec((640, 640), lambda i: (0, i)),
            pl.BlockSpec((640, cols), lambda i: (0, 0)),
        ],
        out_specs=pl.BlockSpec((4, 160, cols), lambda i: (i, 0, 0)),
        compiler_params=VMEM,
        cost_estimate=FREE,
    )(x, g)


def outer_output_kernel(own_ref, other_ref, ob_ref, out_ref):
    cols = ob_ref.shape[2]
    part = dot(own_ref[...], ob_ref[:, :80].reshape(320, cols), 0, 0)
    part = part + dot(other_ref[...], ob_ref[:, 80:].reshape(320, cols), 0, 0)
    out_ref[...] = part.reshape(16, 40, cols).astype(BF)


def outer_output(own, other, ob):
    cols = 640
    half = pl.BlockSpec((320, 640), lambda i: (0, 0))
    return pl.pallas_call(
        outer_output_kernel,
        grid=(2,),
        out_shape=jax.ShapeDtypeStruct((16, 40, 1280), BF),
        in_specs=[half, half, pl.BlockSpec((4, 160, cols), lambda i: (0, 0, i))],
        out_specs=pl.BlockSpec((16, 40, cols), lambda i: (0, 0, i)),
        compiler_params=VMEM,
        cost_estimate=FREE,
    )(own, other, ob)


def to_owners(sums):
    me = lax.axis_index(Y)
    rows = sums.reshape(4, -1, sums.shape[-1])
    got = []
    for r in range(4):
        block = lax.dynamic_index_in_dim(rows, (me + r) % 4, 0, keepdims=False)
        got.append(shift(block, Y, r) if r else block)
    return got


def by_half(blocks):
    cols = blocks.shape[2]
    return blocks.reshape(4, 2, 80, cols).swapaxes(0, 1).reshape(640, cols)


def columns_out(blocks):
    me = lax.axis_index(Y)
    got = []
    for r in range(4):
        block = lax.dynamic_index_in_dim(blocks, (me + r) % 4, 0, keepdims=False)
        got.append(shift(block, Y, r) if r else block)
    return by_half(place(got, Y, sign=-1))


def quarters(x):
    rows = x.shape[0]
    return x.reshape(rows, 4, -1).swapaxes(0, 1)


def pack_attention_kernel(q_ref, kv_ref, gains_ref, attn_ref):
    attn_ref[...] = jnp.zeros_like(attn_ref)
    for j in range(4):
        attn_ref[j, :40, :320] = q_ref[:, 320 * j : 320 * j + 320]
        attn_ref[j, :40, 320:] = kv_ref[:, 64 * j : 64 * j + 64]
        attn_ref[j, 40:48, :128] = gains_ref[...]


def pack_attention(w_query, keyval_half, gains):
    return pl.pallas_call(
        pack_attention_kernel,
        out_shape=jax.ShapeDtypeStruct((4, 48, 384), BF),
        compiler_params=VMEM,
        cost_estimate=FREE,
    )(w_query, keyval_half, gains)


def pack_mlp_kernel(gate_ref, up_ref, down_ref, mlp_ref):
    mlp_ref[...] = jnp.zeros_like(mlp_ref)
    for j in range(4):
        mlp_ref[j, :, :960] = gate_ref[:, 960 * j : 960 * j + 960]
        mlp_ref[j, :, 1024:1984] = up_ref[:, 960 * j : 960 * j + 960]
        mlp_ref[j, :, 2048:3008] = down_ref[:, 960 * j : 960 * j + 960]


def pack_mlp(w_gate, w_up, w_down):
    return pl.pallas_call(
        pack_mlp_kernel,
        out_shape=jax.ShapeDtypeStruct((4, 40, 3072), BF),
        compiler_params=VMEM,
        cost_estimate=FREE,
    )(w_gate, w_up, w_down)


def down_grad_kernel(y_ref, hidden_ref, *rest):
    rest[-1][...] = dot(y_ref[...], hidden_ref[...], 0, 0).astype(BF)


def down_grads(grads, hidden, *first):
    rows = 512
    return pl.pallas_call(
        down_grad_kernel,
        grid=(2560 // rows,),
        out_shape=jax.ShapeDtypeStruct((2560, 3072), BF),
        in_specs=[
            pl.BlockSpec((640, rows), lambda i: (0, i)),
            pl.BlockSpec((640, 1024), lambda i: (0, 0)),
        ]
        + [ANYWHERE] * len(first),
        out_specs=pl.BlockSpec((rows, 1024), lambda i: (i, 2)),
        compiler_params=VMEM,
        cost_estimate=FREE,
    )(grads, hidden, *first)


def gate_up_grad_kernel(x_ref, gate_ref, up_ref, *rest):
    out_ref = rest[-1]
    out_ref[:, :1024] = dot(x_ref[...], gate_ref[...], 0, 0).astype(BF)
    out_ref[:, 1024:] = dot(x_ref[...], up_ref[...], 0, 0).astype(BF)


def gate_up_grads(normed, gate, up, held, *first):
    rows = 512
    whole = pl.BlockSpec((640, 1024), lambda i: (0, 0))
    return pl.pallas_call(
        gate_up_grad_kernel,
        grid=(2560 // rows,),
        out_shape=jax.ShapeDtypeStruct((2560, 3072), BF),
        in_specs=[pl.BlockSpec((640, rows), lambda i: (0, i)), whole, whole]
        + [ANYWHERE] * (1 + len(first)),
        out_specs=pl.BlockSpec((rows, 2048), lambda i: (i, 0)),
        input_output_aliases={3: 0},
        compiler_params=VMEM,
        cost_estimate=FREE,
    )(normed, gate, up, held, *first)


def feed_forward_kernel(x_ref, y_ref, gate_ref, up_ref, down_ref, *rest):
    hidden_out, gate_out, up_out = rest[-3:]
    gate = dot(x_ref[...], gate_ref[...], 1, 0)
    up = dot(x_ref[...], up_ref[...], 1, 0)
    grad = dot(y_ref[...], down_ref[...], 1, 0)
    scale = 0.7978845608028654
    square = gate * gate
    bent = jnp.tanh(scale * gate * (1.0 + 0.044715 * square))
    share = 0.5 * (1.0 + bent)
    slope = share + 0.5 * gate * (1.0 - bent * bent) * scale * (1.0 + 0.134145 * square)
    active = gate * share
    hidden_out[...] = (active * up).astype(BF)
    gate_out[...] = (grad * up * slope).astype(BF)
    up_out[...] = (grad * active).astype(BF)


def feed_forward(x, y, w_mlp, *first):
    cols = 256
    steps = 1024 // cols
    part = jax.ShapeDtypeStruct((640, 1024), BF)
    whole = pl.BlockSpec((640, 2560), lambda j: (0, 0))
    out = pl.BlockSpec((640, cols), lambda j: (0, j))
    return pl.pallas_call(
        feed_forward_kernel,
        grid=(steps,),
        out_shape=(part, part, part),
        in_specs=[whole, whole]
        + [pl.BlockSpec((2560, cols), lambda j, k=k: (0, k * steps + j)) for k in range(3)]
        + [ANYWHERE] * len(first),
        out_specs=(out, out, out),
        compiler_params=VMEM,
        cost_estimate=FREE,
    )(x, y, w_mlp, w_mlp, w_mlp, *first)


def to_piece_order(x):
    rows = x.shape[0]
    return x.reshape(rows, 4, 16, 40).swapaxes(1, 2).reshape(rows, 2560)


def inverse_root(values):
    return lax.rsqrt(jnp.mean(values * values, axis=-1, keepdims=True) + EPSILON)


def norm_back(grad, values, inverse, gain):
    scaled = gain * grad
    return inverse * scaled - values * inverse**3 * jnp.mean(
        scaled * values, axis=-1, keepdims=True
    )


def angles(position, head_dim):
    quarter = head_dim // 4
    frequency = 10000.0 ** (-jnp.arange(quarter, dtype=F32) / quarter)
    phase_angle = position[:, None].astype(F32) * frequency[None, :]
    return (jnp.cos(phase_angle), jnp.sin(phase_angle))


def dot(a, b, da, db):
    return lax.dot_general(a, b, (((da,), (db,)), ((), ())), preferred_element_type=F32)


def feature_quarters_kernel(x_ref, out_ref):
    for j in range(4):
        for p in range(16):
            at = 40 * (4 * p + j)
            out_ref[j, :, 40 * p : 40 * p + 40] = x_ref[:, at : at + 40].astype(BF)


def feature_quarters(x):
    return pl.pallas_call(
        feature_quarters_kernel,
        out_shape=jax.ShapeDtypeStruct((4, 80, 640), BF),
        compiler_params=VMEM,
        cost_estimate=FREE,
    )(x)


def project_kernel(own_ref, other_ref, gain_ref, weight_ref, *rest):
    normed_ref, out_ref = rest[-2:]

    def rows(block):
        x = block[0].astype(F32)
        normed = (x * inverse_root(x) * gain_ref[...]).astype(BF)
        normed_ref[...] = normed
        out_ref[0] = dot(normed, weight_ref[...], 1, 0).astype(BF)

    i = pl.program_id(0)

    @pl.when(i < 4)
    def _():
        rows(own_ref)

    @pl.when(i >= 4)
    def _():
        rows(other_ref)


def project(own, other, gain, weight, *first):
    return pl.pallas_call(
        project_kernel,
        grid=(8,),
        out_shape=(
            jax.ShapeDtypeStruct((640, 2560), BF),
            jax.ShapeDtypeStruct((4, 160, 384), BF),
        ),
        in_specs=[
            pl.BlockSpec((1, 80, 2560), lambda i: (jnp.minimum(i, 3), 0, 0)),
            pl.BlockSpec((1, 80, 2560), lambda i: (jnp.maximum(i, 4) - 4, 0, 0)),
            pl.BlockSpec((1, 2560), lambda i: (0, 0)),
            pl.BlockSpec((2560, 384), lambda i: (0, 0)),
        ]
        + [ANYWHERE] * len(first),
        out_specs=(
            pl.BlockSpec((80, 2560), lambda i: (i, 0)),
            pl.BlockSpec((1, 80, 384), lambda i: (i % 4, i // 4, 0)),
        ),
        compiler_params=VMEM,
        cost_estimate=FREE,
    )(own, other, gain, weight, *first)


def owners_kernel(*refs):
    home, mlp = refs[:4], refs[4:8]
    output_home, query_ref, keyval_ref, gate_ref, up_ref, block_mine, block_other, rows_mine, rows_other = refs[8:17]
    query_out, keyval_out, output_out, gate_out, up_out, down_out, gain_out, block_out, rows_out = refs[17:26]
    held, held_mlp = refs[26:]
    me = lax.axis_index(Y)
    for r in range(4):
        held[lax.rem(me + 4 - r, 4)] = home[r][...]
        held_mlp[lax.rem(me + 4 - r, 4)] = mlp[r][...]
    for j in range(4):
        columns = slice(960 * j, 960 * j + 960)
        gate_out[:, columns] = held_mlp[j, :, :960].astype(F32)
        up_out[:, columns] = held_mlp[j, :, 1024:1984].astype(F32)
        down_out[:, columns] = held_mlp[j, :, 2048:3008].astype(F32)
        total = held[j].astype(F32)
        query_out[:, 320 * j : 320 * j + 320] = total[:, :320]
        keyval_out[:, 64 * j : 64 * j + 64] = total[:, 320:384]
    total = output_home[0].astype(F32)
    for p in range(1, 16):
        total = total + output_home[p].astype(F32)
    output_out[...] = total

    def products(weight, grad):
        return jnp.sum(weight[...].astype(F32) * grad[...], axis=1, keepdims=True)

    one = products(query_ref, query_out) + products(keyval_ref, keyval_out)
    two = products(gate_ref, gate_out) + products(up_ref, up_out)
    gain_out[:, :128] = jnp.broadcast_to(one, (40, 128))
    gain_out[:, 128:] = jnp.broadcast_to(two, (40, 128))
    at = 80 * lax.axis_index(T)
    for mine, other, out in ((block_mine, block_other, block_out), (rows_mine, rows_other, rows_out)):
        out[pl.ds(pl.multiple_of(at, 16), 80), :] = mine[...]
        out[pl.ds(pl.multiple_of(80 - at, 16), 80), :] = other[...]


def owners(home, mlp, output_home, w_query, keyval_half, w_gate, w_up, block, rows):
    wide, narrow = (jax.ShapeDtypeStruct((40, n), F32) for n in (3840, 1280))
    small = jax.ShapeDtypeStruct((40, 256), F32)
    tokens = jax.ShapeDtypeStruct((160, 2560), BF)
    return pl.pallas_call(
        owners_kernel,
        out_shape=(narrow, small, narrow, wide, wide, wide, small, tokens, tokens),
        scratch_shapes=[pltpu.VMEM((4, 40, 384), BF), pltpu.VMEM((4, 40, 3072), BF)],
        compiler_params=VMEM,
        cost_estimate=FREE,
    )(*home, *mlp, output_home, w_query, keyval_half, w_gate, w_up, *block, *rows)


def turned(values, cosine, sine):
    one, two = values[:, :64], values[:, 64:128]
    return jnp.concatenate(
        [one * cosine - two * sine, two * cosine + one * sine, values[:, 128:]], axis=1
    )


def prepare_kernel(scale, home_ref, cosine_ref, sine_ref, query_ref, kv_ref, wide):
    cosine, sine = cosine_ref[...], sine_ref[...]
    for j in range(4):
        wide[:, 320 * j : 320 * j + 320] = home_ref[j, :, :320].astype(F32)
    for h in range(5):
        head = turned(wide[:, 256 * h : 256 * h + 256], cosine, sine)
        query_ref[h] = (head * scale).astype(BF)
    for j in range(4):
        wide[:, 64 * j : 64 * j + 64] = home_ref[j, :, 320:].astype(F32)
    first = lax.axis_index(T) == 0
    kv = wide[:, :256]
    kv = jnp.where(first, turned(kv, cosine, sine), kv).astype(BF)
    at = 80 * lax.axis_index(T)
    kv_ref[pl.ds(pl.multiple_of(at, 16), 80), :] = kv[:80]
    kv_ref[pl.ds(pl.multiple_of(80 - at, 16), 80), :] = kv[80:]


def prepare(home, cosine, sine, scale):
    return pl.pallas_call(
        functools.partial(prepare_kernel, scale),
        out_shape=(
            jax.ShapeDtypeStruct((5, 160, 256), BF),
            jax.ShapeDtypeStruct((160, 256), BF),
        ),
        scratch_shapes=[pltpu.VMEM((160, 1280), F32)],
        compiler_params=VMEM,
        cost_estimate=FREE,
    )(home, cosine, sine)


def unturn_kernel(scale, grad_ref, cosine_ref, sine_ref, out_ref, wide):
    cosine, sine = cosine_ref[...], -sine_ref[...]
    for h in range(5):
        wide[:, 256 * h : 256 * h + 256] = turned(grad_ref[h] * scale, cosine, sine)
    for j in range(4):
        out_ref[j] = wide[:, 320 * j : 320 * j + 320].astype(BF)


def unturn(grad, cosine, sine, scale):
    return pl.pallas_call(
        functools.partial(unturn_kernel, scale),
        out_shape=jax.ShapeDtypeStruct((4, 160, 320), BF),
        scratch_shapes=[pltpu.VMEM((160, 1280), F32)],
        compiler_params=VMEM,
        cost_estimate=FREE,
    )(grad, cosine, sine)


def unturn_kv_kernel(home_ref, cosine_ref, sine_ref, out_ref, held):
    total = home_ref[0].astype(F32)
    for p in range(1, 16):
        total = total + home_ref[p].astype(F32)
    held[...] = total
    at = 80 * lax.axis_index(T)
    total = jnp.concatenate(
        [held[pl.ds(pl.multiple_of(at, 16), 80), :], held[pl.ds(pl.multiple_of(80 - at, 16), 80), :]]
    )
    back = turned(total, cosine_ref[...], -sine_ref[...])
    total = jnp.where(lax.axis_index(T) == 0, back, total).astype(BF)
    for j in range(4):
        out_ref[j] = total[:, 64 * j : 64 * j + 64]


def unturn_kv(home, cosine, sine):
    return pl.pallas_call(
        unturn_kv_kernel,
        out_shape=jax.ShapeDtypeStruct((4, 160, 64), BF),
        scratch_shapes=[pltpu.VMEM((160, 256), F32)],
        compiler_params=VMEM,
        cost_estimate=FREE,
    )(home, cosine, sine)


def pieces_kernel(home_ref, out_ref):
    total = home_ref[0].astype(F32)
    for p in range(1, 16):
        total = total + home_ref[p].astype(F32)
    out_ref[...] = total.astype(BF)


def pieces_sum(home):
    cols = home.shape[2]
    return pl.pallas_call(
        pieces_kernel,
        grid=(2,),
        in_specs=[pl.BlockSpec((16, 80, cols), lambda i: (0, i, 0))],
        out_specs=pl.BlockSpec((80, cols), lambda i: (i, 0)),
        out_shape=jax.ShapeDtypeStruct((160, cols), BF),
        compiler_params=VMEM,
        cost_estimate=FREE,
    )(home)


def token_order_kernel(x_ref, out_ref):
    for j in range(4):
        for p in range(16):
            to, at = 40 * (16 * j + p), 40 * (4 * p + j)
            out_ref[:, to : to + 40] = x_ref[:, at : at + 40].astype(BF)


def from_piece_order(x):
    return pl.pallas_call(
        token_order_kernel, out_shape=jax.ShapeDtypeStruct(x.shape, BF), compiler_params=VMEM, cost_estimate=FREE
    )(x)


def shards(
    tokens,
    lengths,
    attn_gain,
    w_query,
    w_keyval,
    w_output,
    mlp_gain,
    w_gate,
    w_up,
    w_down,
    cotangent,
):
    t = lax.axis_index(T)
    me = lax.axis_index(Y)
    piece = lax.axis_index(CONTEXT)
    head_dim = 256
    query_scale = head_dim ** (-0.5)
    seq_count = 2560
    padding = seq_count - lengths[0]
    row_start = piece * 160
    turned_index = row_start + (jnp.arange(160, dtype=jnp.int32) + t * 80) % 160
    live_turned = turned_index >= padding
    live_mine = live_turned[:80, None]

    x_low = to_piece_order(lax.dynamic_slice_in_dim(tokens[0], t * 80, 80, 0))
    cot_mine = to_piece_order(lax.dynamic_slice_in_dim(cotangent[0], t * 80, 80, 0))
    grad_mine = jnp.where(live_mine, cot_mine, jnp.zeros_like(cot_mine))
    x_mine = x_low.astype(F32)
    x_blocks = ring_blocks(x_low, Y)
    out_rows = place(ring_blocks(w_output, Y), Y).reshape(160, 1280)
    w_out = lax.all_gather(out_rows, CONTEXT, axis=0, tiled=True)

    keyval_half = lax.dynamic_slice_in_dim(w_keyval, t * 256, 256, 1)
    gains = jnp.concatenate([attn_gain, mlp_gain])[None, :]
    gains = jnp.pad(gains, ((0, 7), (0, 48)))
    attn_blocks = pack_attention(w_query, keyval_half, gains)
    attn_rows = place(to_owners(attn_blocks), Y, sign=-1)
    attn_copies = jnp.broadcast_to(attn_rows[None], (16, 4, 48, 384))
    attn_all = exchange(attn_copies, CONTEXT).reshape(64, 48, 384)
    w_qkv = attn_all[:, :40].reshape(2560, 384)
    gain_one = attn_all[:, 40, :40].reshape(1, 2560).astype(F32)
    gain_two = attn_all[:, 40, 40:80].reshape(1, 2560).astype(F32)
    x_own = place(x_blocks, Y, attn_all)
    x_other = shift(x_own, T, 1)
    mlp_blocks = pack_mlp(w_gate, w_up, w_down)
    mlp_got = to_owners(mlp_blocks)
    mlp_block = place(mlp_got, Y, x_own, sign=-1).reshape(160, 3072)
    w_mlp = lax.all_gather(mlp_block, CONTEXT, axis=0, tiled=True)

    normed, projected = project(x_own, x_other, gain_one, w_qkv)
    home = exchange(projected, Y)
    cosine, sine = angles(turned_index - padding, head_dim)
    queries, kv_own = prepare(home, cosine, sine, query_scale)
    kv_mine = exchange(jnp.broadcast_to(kv_own[None], (16, 160, 256)), CONTEXT).reshape(2560, 256)
    grad_own = place(ring_blocks(after(grad_mine, kv_own), Y), Y).reshape(320, 2560)
    grad_group = jnp.concatenate([grad_own, shift(grad_own, T, 1)])
    kv_mine = after(kv_mine, grad_own)
    kv_other = shift(kv_mine, T, 1)
    keys = jnp.where(t == 0, kv_mine, kv_other)
    values = jnp.where(t == 0, kv_other, kv_mine)

    key_index = jnp.arange(seq_count, dtype=jnp.int32)
    offset = turned_index[:, None] - key_index[None, :]
    allowed = ((offset >= 0) & (offset < WINDOW) & (key_index >= padding)[None, :])[None]
    live = live_turned[None, :, None]
    scores = jnp.einsum("hqd,kd->hqk", queries, keys, preferred_element_type=F32)
    row_top = jnp.max(jnp.where(allowed, scores, NEGATIVE_FILL), axis=-1, keepdims=True)
    row_top = jnp.where(live, row_top, 0.0)
    weights_exp = jnp.where(allowed, jnp.exp(scores - row_top), 0.0)
    row_total = jnp.where(live, jnp.sum(weights_exp, axis=-1, keepdims=True), 1.0)
    prob = weights_exp / row_total
    prob_low = prob.astype(BF)
    attended = jnp.einsum("hqk,kd->qhd", prob_low, values, preferred_element_type=F32)
    attended = attended.reshape(160, 1280).astype(BF)

    branch = dot(attended, w_out, 1, 1)
    hidden_mine = x_mine + branch[:80] + shift(branch[80:], T, 1)

    inverse_two = inverse_root(hidden_mine)
    normed_two_mine = (hidden_mine * inverse_two * gain_two).astype(BF)
    normed_two = jnp.concatenate(gather_rows(after(normed_two_mine, grad_group)))
    hidden, grad_gate, grad_up = feed_forward(normed_two, grad_group, w_mlp)
    attended_group = place(ring_blocks(attended, Y), Y)
    normed_two_low = core_sum(*row_products((grad_gate, grad_up), w_mlp, 0, 1024, attended_group))
    got = own_and_received(normed_two_low, Y, 0)

    mlp_rows = row_products((hidden,), w_mlp, 2, 1024, normed_two_low)
    down_part = down_grads(grad_group, hidden, *mlp_rows)
    mlp_part = gate_up_grads(normed_two, grad_gate, grad_up, down_part, *got)
    mlp_sum = lax.psum_scatter(mlp_part, CONTEXT, scatter_dimension=0, tiled=True)
    grad_normed_two = sum(block.astype(F32) for block in got)

    grad_h_mine = grad_mine.astype(F32) + norm_back(
        grad_normed_two, hidden_mine, inverse_two, gain_two
    )
    branch_mine = grad_h_mine.astype(BF)
    branch_own = place(to_owners(feature_quarters(grad_h_mine)), Y, sign=-1).reshape(320, 640)
    branch_other = shift(branch_own, T, 1)
    branch_low = jnp.concatenate([branch_mine, shift(branch_mine, T, 1)])
    grad_attended = dot(branch_low, w_out, 1, 0).astype(BF).reshape(160, 5, head_dim)

    grad_prob = jnp.einsum("qhd,kd->hqk", grad_attended, values, preferred_element_type=F32)
    spread = jnp.sum(prob * grad_prob, axis=-1, keepdims=True)
    grad_scores = (prob * (grad_prob - spread)).astype(BF)
    grad_keys = jnp.einsum("hqk,hqd->kd", grad_scores, queries, preferred_element_type=F32)
    grad_values = jnp.einsum("hqk,qhd->kd", prob_low, grad_attended, preferred_element_type=F32)
    keep = jnp.where(t == 0, grad_keys, grad_values)
    give = jnp.where(t == 0, grad_values, grad_keys).astype(BF)
    grad_queries = jnp.einsum("hqk,kd->hqd", grad_scores, keys, preferred_element_type=F32)
    query_blocks = unturn(grad_queries, cosine, sine, query_scale)
    kv_part = (keep + shift(give, T, 1).astype(F32)).astype(BF).reshape(16, 160, 256)
    output_part = outer_output(branch_own, branch_other, attended_group)
    output_home = exchange(output_part, CONTEXT)
    kv_part = after(kv_part, query_blocks, output_home)
    kv_home = exchange(kv_part, CONTEXT)
    grad_query_group = columns_out(query_blocks)
    grad_kv_group = columns_out(unturn_kv(kv_home, cosine, sine))
    grad_qkv = jnp.concatenate([grad_query_group, grad_kv_group], axis=1)
    normed_low = core_sum(*row_products((grad_qkv,), w_qkv, 0, 384))
    part_home = exchange(outer(normed, grad_qkv), CONTEXT)
    (grad_normed,) = sums((own_and_received(normed_low, Y, 0),), (F32,))
    (mlp_mine,) = sums((own_and_received(after(core_sum(*mlp_rows), normed_low), Y, 0),), (F32,))
    inverse_one = inverse_root(x_mine)
    tokens_mine = from_piece_order(
        grad_h_mine + norm_back(grad_normed, x_mine, inverse_one, gain_one)
    )
    block_mine = from_piece_order(jnp.where(live_mine, hidden_mine + mlp_mine, 0.0))
    mlp_home = to_owners(mlp_sum)
    home = to_owners(pieces_sum(part_home))
    query_grad, kv_half, output_grad, gate_grad, up_grad, down_grad, gain_part, block_out, tokens_grad = owners(
        home,
        mlp_home,
        output_home,
        w_query,
        keyval_half,
        w_gate,
        w_up,
        (block_mine, shift(block_mine, T, 1)),
        (tokens_mine, shift(tokens_mine, T, 1)),
    )

    mine = jnp.concatenate([kv_half, gain_part], axis=1)
    other = shift(mine, T, 1)
    kv_other = other[:, :256]
    keyval_grad = jnp.where(
        t == 0,
        jnp.concatenate([kv_half, kv_other], axis=1),
        jnp.concatenate([kv_other, kv_half], axis=1),
    )
    attn_gain_grad = (mine[:, 256] + other[:, 256]) / attn_gain.astype(F32)
    mlp_gain_grad = (mine[:, 384] + other[:, 384]) / mlp_gain.astype(F32)

    return (
        block_out[None],
        tokens_grad[None],
        attn_gain_grad,
        query_grad,
        keyval_grad,
        output_grad,
        mlp_gain_grad,
        gate_grad,
        up_grad,
        down_grad,
    )


def solution(mesh):
    torus = Mesh(
        mesh.devices.reshape(mesh.shape["shard"], 4, 4, mesh.shape["tensor"]),
        ("shard", "context_0", "context_1", "tensor"),
    )
    in_specs = (
        P("shard", CONTEXT, None),
        P("shard"),
        P(SHARD_CONTEXT),
        P(SHARD_CONTEXT, "tensor"),
        P(SHARD_CONTEXT, None),
        P(SHARD_CONTEXT, "tensor"),
        P(SHARD_CONTEXT),
        P(SHARD_CONTEXT, "tensor"),
        P(SHARD_CONTEXT, "tensor"),
        P(SHARD_CONTEXT, "tensor"),
        P("shard", CONTEXT, None),
    )
    out_specs = (
        P("shard", CONTEXT, None),
        P("shard", CONTEXT, None),
        P(SHARD_CONTEXT),
        P(SHARD_CONTEXT, "tensor"),
        P(SHARD_CONTEXT, None),
        P(SHARD_CONTEXT, "tensor"),
        P(SHARD_CONTEXT),
        P(SHARD_CONTEXT, "tensor"),
        P(SHARD_CONTEXT, "tensor"),
        P(SHARD_CONTEXT, "tensor"),
    )
    return jax.shard_map(
        shards, mesh=torus, in_specs=in_specs, out_specs=out_specs, check_vma=False
    )
```

```python
import functools

import jax
import jax.numpy as jnp
from jax import lax
from jax.experimental import pallas as pl
from jax.experimental.pallas import tpu as pltpu
from jax.sharding import Mesh
from jax.sharding import PartitionSpec as P

WINDOW = 2048
SHARD_CONTEXT = ("shard", "context_0", "context_1")
CONTEXT = ("context_0", "context_1")
PIECES = ("context_0", "context_1", "shard")
Y, X, Z, T = "shard", "context_0", "context_1", "tensor"


def room(mebibytes):
    return pltpu.CompilerParams(vmem_limit_bytes=mebibytes * 2**20)


ANYWHERE = pl.BlockSpec(memory_space=pl.ANY)
FREE = pl.CostEstimate(flops=0, bytes_accessed=0, transcendentals=0)

EPSILON = 1e-06
NEGATIVE_FILL = -1e30
BF = jnp.bfloat16
F32 = jnp.float32


def shift(x, axis, by):
    n = lax.axis_size(axis)
    return lax.ppermute(x, axis, [(i, (i + by) % n) for i in range(n)])


def exchange(blocks, axis):
    return lax.all_to_all(blocks, axis, 0, 0, tiled=True)


def nothing(*refs):
    pass


def after(x, *others):
    return pl.pallas_call(
        nothing,
        out_shape=jax.ShapeDtypeStruct(x.shape, x.dtype),
        in_specs=[ANYWHERE] * (1 + len(others)),
        out_specs=ANYWHERE,
        input_output_aliases={0: 0},
        compiler_params=room(1),
        cost_estimate=FREE,
    )(x, *others)


def small_trip(x, *others):
    corner = x.reshape(-1, x.shape[-1])[:8, :128]
    return shift(after(corner, *others) if others else corner, T, 1)


def ring_blocks(x, axis):
    return [x, shift(x, axis, -1), shift(x, axis, 2), shift(x, axis, 1)]


def place_kernel(axis, sign, *refs):
    blocks, out = refs[:4], refs[-1]
    me = lax.axis_index(axis)
    for r, block in enumerate(blocks):
        out[lax.rem(me + (sign * r) % 4, 4)] = block[...]


def place(blocks, axis, *first, sign=1):
    whole = pl.BlockSpec(memory_space=pltpu.VMEM)
    return pl.pallas_call(
        functools.partial(place_kernel, axis, sign),
        out_shape=jax.ShapeDtypeStruct((4, *blocks[0].shape), blocks[0].dtype),
        in_specs=[whole] * 4 + [ANYWHERE] * len(first),
        out_specs=whole,
        compiler_params=room(10),
        cost_estimate=FREE,
    )(*blocks, *first)


def gather_rows(mine, *first):
    own = place(ring_blocks(mine, Y), Y, *first).reshape(320, -1)
    return own, shift(own, T, 1)


def rows_kernel(count, *refs):
    lefts, rights, (far_ref, near_ref) = refs[:count], refs[count : 2 * count], refs[-2:]
    total = dot(lefts[0][...], rights[0][...], 1, 1)
    for left, right in zip(lefts[1:], rights[1:]):
        total = total + dot(left[...], right[...], 1, 1)
    near_ref[...] = total[:320].astype(BF)
    far_ref[...] = total[320:].astype(BF)


def row_products(lefts, weight, at, width, *first):
    rows, count, n = 512, len(lefts), weight.shape[0]
    half = jax.ShapeDtypeStruct((320, n), BF)
    return pl.pallas_call(
        functools.partial(rows_kernel, count),
        grid=(n // rows,),
        out_shape=(half, half),
        in_specs=[pl.BlockSpec((640, width), lambda i: (0, 0))] * count
        + [pl.BlockSpec((rows, width), lambda i, j=j: (i, at + j)) for j in range(count)]
        + [ANYWHERE] * len(first),
        out_specs=(pl.BlockSpec((320, rows), lambda i: (0, i)),) * 2,
        compiler_params=room(22),
        cost_estimate=FREE,
    )(*lefts, *[weight] * count, *first)


def core_sum(far, near):
    return (near.astype(F32) + shift(far, T, 1).astype(F32)).astype(BF).reshape(4, 80, -1)


def own_and_received(parts, axis, dim):
    me = lax.axis_index(axis)
    own, *rest = [
        lax.dynamic_index_in_dim(parts, (me + r) % 4, dim, keepdims=False) for r in range(4)
    ]
    return [own] + [shift(rest[r - 1], axis, r) for r in (1, 3, 2)]


def sums_kernel(kinds, *refs):
    for i, out in enumerate(refs[4 * len(kinds) :]):
        total = refs[4 * i][...].astype(F32)
        for ref in refs[4 * i + 1 : 4 * i + 4]:
            total = total + ref[...].astype(F32)
        out[...] = total.astype(kinds[i])


def sums(groups, kinds):
    return pl.pallas_call(
        functools.partial(sums_kernel, kinds),
        out_shape=tuple(jax.ShapeDtypeStruct(g[0].shape, k) for g, k in zip(groups, kinds)),
        compiler_params=room(10),
        cost_estimate=FREE,
    )(*[block for group in groups for block in group])


def outer_kernel(x_ref, g_ref, out_ref):
    out_ref[...] = dot(x_ref[...], g_ref[...], 0, 0).astype(BF).reshape(4, 160, g_ref.shape[1])


def outer(x, g):
    cols = g.shape[1]
    return pl.pallas_call(
        outer_kernel,
        grid=(4,),
        out_shape=jax.ShapeDtypeStruct((16, 160, cols), BF),
        in_specs=[
            pl.BlockSpec((640, 640), lambda i: (0, i)),
            pl.BlockSpec((640, cols), lambda i: (0, 0)),
        ],
        out_specs=pl.BlockSpec((4, 160, cols), lambda i: (i, 0, 0)),
        compiler_params=room(12),
        cost_estimate=FREE,
    )(x, g)


def outer_output_kernel(own_ref, other_ref, ob_ref, out_ref):
    cols = ob_ref.shape[2]
    part = dot(own_ref[...], ob_ref[:, :80].reshape(320, cols), 0, 0)
    part = part + dot(other_ref[...], ob_ref[:, 80:].reshape(320, cols), 0, 0)
    out_ref[...] = part.reshape(16, 40, cols).astype(BF)


def outer_output(own, other, ob):
    cols = 640
    half = pl.BlockSpec((320, 640), lambda i: (0, 0))
    return pl.pallas_call(
        outer_output_kernel,
        grid=(2,),
        out_shape=jax.ShapeDtypeStruct((16, 40, 1280), BF),
        in_specs=[half, half, pl.BlockSpec((4, 160, cols), lambda i: (0, 0, i))],
        out_specs=pl.BlockSpec((16, 40, cols), lambda i: (0, 0, i)),
        compiler_params=room(16),
        cost_estimate=FREE,
    )(own, other, ob)


def to_owners(sums):
    me = lax.axis_index(Y)
    rows = sums.reshape(4, -1, sums.shape[-1])
    got = []
    for r in range(4):
        block = lax.dynamic_index_in_dim(rows, (me + r) % 4, 0, keepdims=False)
        got.append(shift(block, Y, r) if r else block)
    return got


def by_half(blocks):
    cols = blocks.shape[2]
    return blocks.reshape(4, 2, 80, cols).swapaxes(0, 1).reshape(640, cols)


def columns_out(blocks):
    me = lax.axis_index(Y)
    got = []
    for r in range(4):
        block = lax.dynamic_index_in_dim(blocks, (me + r) % 4, 0, keepdims=False)
        got.append(shift(block, Y, r) if r else block)
    return by_half(place(got, Y, sign=-1))


def quarters(x):
    rows = x.shape[0]
    return x.reshape(rows, 4, -1).swapaxes(0, 1)


def pack_attention_kernel(q_ref, kv_ref, gains_ref, attn_ref):
    attn_ref[...] = jnp.zeros_like(attn_ref)
    for j in range(4):
        attn_ref[j, :40, :320] = q_ref[:, 320 * j : 320 * j + 320]
        attn_ref[j, :40, 320:] = kv_ref[:, 64 * j : 64 * j + 64]
        attn_ref[j, 40:48, :128] = gains_ref[...]


def pack_attention(w_query, keyval_half, gains):
    return pl.pallas_call(
        pack_attention_kernel,
        out_shape=jax.ShapeDtypeStruct((4, 48, 384), BF),
        compiler_params=room(8),
        cost_estimate=FREE,
    )(w_query, keyval_half, gains)


def pack_mlp_kernel(gate_ref, up_ref, down_ref, mlp_ref):
    mlp_ref[...] = jnp.zeros_like(mlp_ref)
    for j in range(4):
        mlp_ref[j, :, :960] = gate_ref[:, 960 * j : 960 * j + 960]
        mlp_ref[j, :, 1024:1984] = up_ref[:, 960 * j : 960 * j + 960]
        mlp_ref[j, :, 2048:3008] = down_ref[:, 960 * j : 960 * j + 960]


def pack_mlp(w_gate, w_up, w_down):
    return pl.pallas_call(
        pack_mlp_kernel,
        out_shape=jax.ShapeDtypeStruct((4, 40, 3072), BF),
        compiler_params=room(8),
        cost_estimate=FREE,
    )(w_gate, w_up, w_down)


def down_grad_kernel(y_ref, hidden_ref, *rest):
    rest[-1][...] = dot(y_ref[...], hidden_ref[...], 0, 0).astype(BF)


def down_grads(grads, hidden, *first):
    rows = 512
    return pl.pallas_call(
        down_grad_kernel,
        grid=(2560 // rows,),
        out_shape=jax.ShapeDtypeStruct((2560, 3072), BF),
        in_specs=[
            pl.BlockSpec((640, rows), lambda i: (0, i)),
            pl.BlockSpec((640, 1024), lambda i: (0, 0)),
        ]
        + [ANYWHERE] * len(first),
        out_specs=pl.BlockSpec((rows, 1024), lambda i: (i, 2)),
        compiler_params=room(48),
        cost_estimate=FREE,
    )(grads, hidden, *first)


def gate_up_grad_kernel(x_ref, gate_ref, up_ref, *rest):
    out_ref = rest[-1]
    out_ref[:, :1024] = dot(x_ref[...], gate_ref[...], 0, 0).astype(BF)
    out_ref[:, 1024:] = dot(x_ref[...], up_ref[...], 0, 0).astype(BF)


def gate_up_grads(normed, gate, up, held, *first):
    rows = 512
    whole = pl.BlockSpec((640, 1024), lambda i: (0, 0))
    return pl.pallas_call(
        gate_up_grad_kernel,
        grid=(2560 // rows,),
        out_shape=jax.ShapeDtypeStruct((2560, 3072), BF),
        in_specs=[pl.BlockSpec((640, rows), lambda i: (0, i)), whole, whole]
        + [ANYWHERE] * (1 + len(first)),
        out_specs=pl.BlockSpec((rows, 2048), lambda i: (i, 0)),
        input_output_aliases={3: 0},
        compiler_params=room(48),
        cost_estimate=FREE,
    )(normed, gate, up, held, *first)


def feed_forward_kernel(x_ref, y_ref, gate_ref, up_ref, down_ref, *rest):
    hidden_out, gate_out, up_out = rest[-3:]
    gate = dot(x_ref[...], gate_ref[...], 1, 0)
    up = dot(x_ref[...], up_ref[...], 1, 0)
    grad = dot(y_ref[...], down_ref[...], 1, 0)
    scale = 0.7978845608028654
    square = gate * gate
    bent = jnp.tanh(scale * gate * (1.0 + 0.044715 * square))
    share = 0.5 * (1.0 + bent)
    slope = share + 0.5 * gate * (1.0 - bent * bent) * scale * (1.0 + 0.134145 * square)
    active = gate * share
    hidden_out[...] = (active * up).astype(BF)
    gate_out[...] = (grad * up * slope).astype(BF)
    up_out[...] = (grad * active).astype(BF)


def feed_forward(x, y, w_mlp, *first):
    cols = 256
    steps = 1024 // cols
    part = jax.ShapeDtypeStruct((640, 1024), BF)
    whole = pl.BlockSpec((640, 2560), lambda j: (0, 0))
    out = pl.BlockSpec((640, cols), lambda j: (0, j))
    return pl.pallas_call(
        feed_forward_kernel,
        grid=(steps,),
        out_shape=(part, part, part),
        in_specs=[whole, whole]
        + [pl.BlockSpec((2560, cols), lambda j, k=k: (0, k * steps + j)) for k in range(3)]
        + [ANYWHERE] * len(first),
        out_specs=(out, out, out),
        compiler_params=room(34),
        cost_estimate=FREE,
    )(x, y, w_mlp, w_mlp, w_mlp, *first)


def to_piece_order(x):
    rows = x.shape[0]
    return x.reshape(rows, 4, 16, 40).swapaxes(1, 2).reshape(rows, 2560)


def inverse_root(values):
    return lax.rsqrt(jnp.mean(values * values, axis=-1, keepdims=True) + EPSILON)


def norm_back(grad, values, inverse, gain):
    scaled = gain * grad
    return inverse * scaled - values * inverse**3 * jnp.mean(
        scaled * values, axis=-1, keepdims=True
    )


def angles(position, head_dim):
    quarter = head_dim // 4
    frequency = 10000.0 ** (-jnp.arange(quarter, dtype=F32) / quarter)
    phase_angle = position[:, None].astype(F32) * frequency[None, :]
    return (jnp.cos(phase_angle), jnp.sin(phase_angle))


def dot(a, b, da, db):
    return lax.dot_general(a, b, (((da,), (db,)), ((), ())), preferred_element_type=F32)


def feature_quarters_kernel(x_ref, out_ref):
    for j in range(4):
        for p in range(16):
            at = 40 * (4 * p + j)
            out_ref[j, :, 40 * p : 40 * p + 40] = x_ref[:, at : at + 40].astype(BF)


def feature_quarters(x):
    return pl.pallas_call(
        feature_quarters_kernel,
        out_shape=jax.ShapeDtypeStruct((4, 80, 640), BF),
        compiler_params=room(8),
        cost_estimate=FREE,
    )(x)


def project_kernel(own_ref, other_ref, gain_ref, weight_ref, *rest):
    normed_ref, out_ref = rest[-2:]

    def rows(block):
        x = block[0].astype(F32)
        normed = (x * inverse_root(x) * gain_ref[...]).astype(BF)
        normed_ref[...] = normed
        out_ref[0] = dot(normed, weight_ref[...], 1, 0).astype(BF)

    i = pl.program_id(0)

    @pl.when(i < 4)
    def _():
        rows(own_ref)

    @pl.when(i >= 4)
    def _():
        rows(other_ref)


def project(own, other, gain, weight, *first):
    return pl.pallas_call(
        project_kernel,
        grid=(8,),
        out_shape=(
            jax.ShapeDtypeStruct((640, 2560), BF),
            jax.ShapeDtypeStruct((4, 160, 384), BF),
        ),
        in_specs=[
            pl.BlockSpec((1, 80, 2560), lambda i: (jnp.minimum(i, 3), 0, 0)),
            pl.BlockSpec((1, 80, 2560), lambda i: (jnp.maximum(i, 4) - 4, 0, 0)),
            pl.BlockSpec((1, 2560), lambda i: (0, 0)),
            pl.BlockSpec((2560, 384), lambda i: (0, 0)),
        ]
        + [ANYWHERE] * len(first),
        out_specs=(
            pl.BlockSpec((80, 2560), lambda i: (i, 0)),
            pl.BlockSpec((1, 80, 384), lambda i: (i % 4, i // 4, 0)),
        ),
        compiler_params=room(18),
        cost_estimate=FREE,
    )(own, other, gain, weight, *first)


def owners_kernel(*refs):
    home, output_home, query_ref, keyval_ref, block_mine, block_other, rows_mine, rows_other = refs[:4], *refs[4:11]
    query_out, keyval_out, output_out, block_out, rows_out, held = refs[11:]
    me = lax.axis_index(Y)
    for r in range(4):
        held[lax.rem(me + 4 - r, 4)] = home[r][...]
    for j in range(4):
        total = held[j].astype(F32)
        query_out[:, 320 * j : 320 * j + 320] = total[:, :320]
        keyval_out[:, 64 * j : 64 * j + 64] = total[:, 320:384]
    total = output_home[0].astype(F32)
    for p in range(1, 16):
        total = total + output_home[p].astype(F32)
    output_out[...] = total
    one = products(query_ref, query_out) + products(keyval_ref, keyval_out)
    keyval_out[:, 256:] = jnp.broadcast_to(one, (40, 128))
    at = 80 * lax.axis_index(T)
    for mine, other, out in ((block_mine, block_other, block_out), (rows_mine, rows_other, rows_out)):
        out[pl.ds(pl.multiple_of(at, 16), 80), :] = mine[...]
        out[pl.ds(pl.multiple_of(80 - at, 16), 80), :] = other[...]


def products(weight, grad):
    cols = weight.shape[1]
    return jnp.sum(weight[...].astype(F32) * grad[:, :cols], axis=1, keepdims=True)


def owners(home, output_home, w_query, keyval_half, block, rows):
    narrow = jax.ShapeDtypeStruct((40, 1280), F32)
    tokens = jax.ShapeDtypeStruct((160, 2560), BF)
    return pl.pallas_call(
        owners_kernel,
        out_shape=(narrow, jax.ShapeDtypeStruct((40, 384), F32), narrow, tokens, tokens),
        scratch_shapes=[pltpu.VMEM((4, 40, 384), BF)],
        compiler_params=room(14),
        cost_estimate=FREE,
    )(*home, output_home, w_query, keyval_half, *block, *rows)


def mlp_owners_kernel(*refs):
    blocks, gate_ref, up_ref = refs[:4], *refs[4:6]
    gate_out, up_out, down_out, gain_out, held = refs[-5:]
    me = lax.axis_index(Y)
    for r in range(4):
        held[lax.rem(me + 4 - r, 4)] = blocks[r][...]
    for j in range(4):
        columns = slice(960 * j, 960 * j + 960)
        gate_out[:, columns] = held[j, :, :960].astype(F32)
        up_out[:, columns] = held[j, :, 1024:1984].astype(F32)
        down_out[:, columns] = held[j, :, 2048:3008].astype(F32)
    two = products(gate_ref, gate_out) + products(up_ref, up_out)
    gain_out[...] = jnp.broadcast_to(two, (40, 128))


def mlp_owners(blocks, w_gate, w_up, *first):
    wide = jax.ShapeDtypeStruct((40, 3840), F32)
    whole = pl.BlockSpec(memory_space=pltpu.VMEM)
    return pl.pallas_call(
        mlp_owners_kernel,
        out_shape=(wide, wide, wide, jax.ShapeDtypeStruct((40, 128), F32)),
        in_specs=[whole] * 6 + [ANYWHERE] * len(first),
        scratch_shapes=[pltpu.VMEM((4, 40, 3072), BF)],
        compiler_params=room(14),
        cost_estimate=FREE,
    )(*blocks, w_gate, w_up, *first)


def turned(values, cosine, sine):
    one, two = values[:, :64], values[:, 64:128]
    return jnp.concatenate(
        [one * cosine - two * sine, two * cosine + one * sine, values[:, 128:]], axis=1
    )


def prepare_kernel(scale, home_ref, cosine_ref, sine_ref, query_ref, kv_ref, wide):
    cosine, sine = cosine_ref[...], sine_ref[...]
    for j in range(4):
        wide[:, 320 * j : 320 * j + 320] = home_ref[j, :, :320].astype(F32)
    for h in range(5):
        head = turned(wide[:, 256 * h : 256 * h + 256], cosine, sine)
        query_ref[h] = (head * scale).astype(BF)
    for j in range(4):
        wide[:, 64 * j : 64 * j + 64] = home_ref[j, :, 320:].astype(F32)
    first = lax.axis_index(T) == 0
    kv = wide[:, :256]
    kv = jnp.where(first, turned(kv, cosine, sine), kv).astype(BF)
    at = 80 * lax.axis_index(T)
    kv_ref[pl.ds(pl.multiple_of(at, 16), 80), :] = kv[:80]
    kv_ref[pl.ds(pl.multiple_of(80 - at, 16), 80), :] = kv[80:]


def prepare(home, cosine, sine, scale):
    return pl.pallas_call(
        functools.partial(prepare_kernel, scale),
        out_shape=(
            jax.ShapeDtypeStruct((5, 160, 256), BF),
            jax.ShapeDtypeStruct((160, 256), BF),
        ),
        scratch_shapes=[pltpu.VMEM((160, 1280), F32)],
        compiler_params=room(10),
        cost_estimate=FREE,
    )(home, cosine, sine)


def unturn_kernel(scale, grad_ref, cosine_ref, sine_ref, out_ref, wide):
    cosine, sine = cosine_ref[...], -sine_ref[...]
    for h in range(5):
        wide[:, 256 * h : 256 * h + 256] = turned(grad_ref[h] * scale, cosine, sine)
    for j in range(4):
        out_ref[j] = wide[:, 320 * j : 320 * j + 320].astype(BF)


def unturn(grad, cosine, sine, scale):
    return pl.pallas_call(
        functools.partial(unturn_kernel, scale),
        out_shape=jax.ShapeDtypeStruct((4, 160, 320), BF),
        scratch_shapes=[pltpu.VMEM((160, 1280), F32)],
        compiler_params=room(10),
        cost_estimate=FREE,
    )(grad, cosine, sine)


def unturn_kv_kernel(home_ref, cosine_ref, sine_ref, out_ref, held):
    total = home_ref[0].astype(F32)
    for p in range(1, 16):
        total = total + home_ref[p].astype(F32)
    held[...] = total
    at = 80 * lax.axis_index(T)
    total = jnp.concatenate(
        [held[pl.ds(pl.multiple_of(at, 16), 80), :], held[pl.ds(pl.multiple_of(80 - at, 16), 80), :]]
    )
    back = turned(total, cosine_ref[...], -sine_ref[...])
    total = jnp.where(lax.axis_index(T) == 0, back, total).astype(BF)
    for j in range(4):
        out_ref[j] = total[:, 64 * j : 64 * j + 64]


def unturn_kv(home, cosine, sine):
    return pl.pallas_call(
        unturn_kv_kernel,
        out_shape=jax.ShapeDtypeStruct((4, 160, 64), BF),
        scratch_shapes=[pltpu.VMEM((160, 256), F32)],
        compiler_params=room(12),
        cost_estimate=FREE,
    )(home, cosine, sine)


def pieces_kernel(home_ref, out_ref):
    total = home_ref[0].astype(F32)
    for p in range(1, 16):
        total = total + home_ref[p].astype(F32)
    out_ref[...] = total.astype(BF)


def pieces_sum(home):
    cols = home.shape[2]
    return pl.pallas_call(
        pieces_kernel,
        grid=(2,),
        in_specs=[pl.BlockSpec((16, 80, cols), lambda i: (0, i, 0))],
        out_specs=pl.BlockSpec((80, cols), lambda i: (i, 0)),
        out_shape=jax.ShapeDtypeStruct((160, cols), BF),
        compiler_params=room(12),
        cost_estimate=FREE,
    )(home)


def token_order_kernel(x_ref, out_ref):
    for j in range(4):
        for p in range(16):
            to, at = 40 * (16 * j + p), 40 * (4 * p + j)
            out_ref[:, to : to + 40] = x_ref[:, at : at + 40].astype(BF)


def from_piece_order(x):
    return pl.pallas_call(
        token_order_kernel, out_shape=jax.ShapeDtypeStruct(x.shape, BF), compiler_params=room(8), cost_estimate=FREE
    )(x)


def shards(
    tokens,
    lengths,
    attn_gain,
    w_query,
    w_keyval,
    w_output,
    mlp_gain,
    w_gate,
    w_up,
    w_down,
    cotangent,
):
    t = lax.axis_index(T)
    me = lax.axis_index(Y)
    piece = lax.axis_index(CONTEXT)
    head_dim = 256
    query_scale = head_dim ** (-0.5)
    seq_count = 2560
    padding = seq_count - lengths[0]
    row_start = piece * 160
    turned_index = row_start + (jnp.arange(160, dtype=jnp.int32) + t * 80) % 160
    live_turned = turned_index >= padding
    live_mine = live_turned[:80, None]

    x_low = to_piece_order(lax.dynamic_slice_in_dim(tokens[0], t * 80, 80, 0))
    cot_mine = to_piece_order(lax.dynamic_slice_in_dim(cotangent[0], t * 80, 80, 0))
    grad_mine = jnp.where(live_mine, cot_mine, jnp.zeros_like(cot_mine))
    x_mine = x_low.astype(F32)
    x_blocks = ring_blocks(x_low, Y)
    out_rows = place(ring_blocks(w_output, Y), Y).reshape(160, 1280)
    w_out = lax.all_gather(out_rows, CONTEXT, axis=0, tiled=True)

    keyval_half = lax.dynamic_slice_in_dim(w_keyval, t * 256, 256, 1)
    gains = jnp.concatenate([attn_gain, mlp_gain])[None, :]
    gains = jnp.pad(gains, ((0, 7), (0, 48)))
    attn_blocks = pack_attention(w_query, keyval_half, gains)
    attn_rows = place(to_owners(attn_blocks), Y, sign=-1)
    attn_copies = jnp.broadcast_to(attn_rows[None], (16, 4, 48, 384))
    attn_all = exchange(attn_copies, CONTEXT).reshape(64, 48, 384)
    w_qkv = attn_all[:, :40].reshape(2560, 384)
    gain_one = attn_all[:, 40, :40].reshape(1, 2560).astype(F32)
    gain_two = attn_all[:, 40, 40:80].reshape(1, 2560).astype(F32)
    x_own = place(x_blocks, Y, attn_all)
    x_other = shift(x_own, T, 1)
    mlp_blocks = pack_mlp(w_gate, w_up, w_down)
    mlp_got = to_owners(mlp_blocks)
    mlp_block = place(mlp_got, Y, x_own, sign=-1).reshape(160, 3072)
    w_mlp = lax.all_gather(mlp_block, CONTEXT, axis=0, tiled=True)

    normed, projected = project(x_own, x_other, gain_one, w_qkv)
    home = exchange(projected, Y)
    cosine, sine = angles(turned_index - padding, head_dim)
    queries, kv_own = prepare(home, cosine, sine, query_scale)
    kv_mine = exchange(jnp.broadcast_to(kv_own[None], (16, 160, 256)), CONTEXT).reshape(2560, 256)
    grad_own = place(ring_blocks(after(grad_mine, kv_own), Y), Y).reshape(320, 2560)
    grad_group = jnp.concatenate([grad_own, shift(grad_own, T, 1)])
    kv_mine = after(kv_mine, grad_own)
    kv_other = shift(kv_mine, T, 1)
    keys = jnp.where(t == 0, kv_mine, kv_other)
    values = jnp.where(t == 0, kv_other, kv_mine)

    key_index = jnp.arange(seq_count, dtype=jnp.int32)
    offset = turned_index[:, None] - key_index[None, :]
    allowed = ((offset >= 0) & (offset < WINDOW) & (key_index >= padding)[None, :])[None]
    live = live_turned[None, :, None]
    scores = jnp.einsum("hqd,kd->hqk", queries, keys, preferred_element_type=F32)
    row_top = jnp.max(jnp.where(allowed, scores, NEGATIVE_FILL), axis=-1, keepdims=True)
    row_top = jnp.where(live, row_top, 0.0)
    weights_exp = jnp.where(allowed, jnp.exp(scores - row_top), 0.0)
    row_total = jnp.where(live, jnp.sum(weights_exp, axis=-1, keepdims=True), 1.0)
    prob = weights_exp / row_total
    prob_low = prob.astype(BF)
    attended = jnp.einsum("hqk,kd->qhd", prob_low, values, preferred_element_type=F32)
    attended = attended.reshape(160, 1280).astype(BF)

    branch = dot(attended, w_out, 1, 1)
    hidden_mine = x_mine + branch[:80] + shift(branch[80:], T, 1)

    inverse_two = inverse_root(hidden_mine)
    normed_two_mine = (hidden_mine * inverse_two * gain_two).astype(BF)
    normed_two = jnp.concatenate(gather_rows(after(normed_two_mine, grad_group)))
    hidden, grad_gate, grad_up = feed_forward(normed_two, grad_group, w_mlp)
    attended_group = place(ring_blocks(attended, Y), Y)
    normed_two_low = core_sum(*row_products((grad_gate, grad_up), w_mlp, 0, 1024, attended_group))
    got = own_and_received(normed_two_low, Y, 0)

    mlp_rows = row_products((hidden,), w_mlp, 2, 1024, normed_two_low)
    down_part = down_grads(grad_group, hidden, *mlp_rows)
    mlp_part = gate_up_grads(normed_two, grad_gate, grad_up, down_part, *got)
    mlp_sum = lax.psum_scatter(mlp_part, CONTEXT, scatter_dimension=0, tiled=True)
    grad_normed_two = sum(block.astype(F32) for block in got)

    grad_h_mine = grad_mine.astype(F32) + norm_back(
        grad_normed_two, hidden_mine, inverse_two, gain_two
    )
    branch_mine = grad_h_mine.astype(BF)
    branch_own = place(to_owners(feature_quarters(grad_h_mine)), Y, sign=-1).reshape(320, 640)
    branch_other = shift(branch_own, T, 1)
    branch_low = jnp.concatenate([branch_mine, shift(branch_mine, T, 1)])
    grad_attended = dot(branch_low, w_out, 1, 0).astype(BF).reshape(160, 5, head_dim)

    grad_prob = jnp.einsum("qhd,kd->hqk", grad_attended, values, preferred_element_type=F32)
    spread = jnp.sum(prob * grad_prob, axis=-1, keepdims=True)
    grad_scores = (prob * (grad_prob - spread)).astype(BF)
    grad_keys = jnp.einsum("hqk,hqd->kd", grad_scores, queries, preferred_element_type=F32)
    grad_values = jnp.einsum("hqk,qhd->kd", prob_low, grad_attended, preferred_element_type=F32)
    keep = jnp.where(t == 0, grad_keys, grad_values)
    give = jnp.where(t == 0, grad_values, grad_keys).astype(BF)
    grad_queries = jnp.einsum("hqk,kd->hqd", grad_scores, keys, preferred_element_type=F32)
    query_blocks = unturn(grad_queries, cosine, sine, query_scale)
    kv_part = (keep + shift(give, T, 1).astype(F32)).astype(BF).reshape(16, 160, 256)
    kv_part = after(kv_part, query_blocks)
    kv_home = exchange(kv_part, CONTEXT)
    grad_query_group = columns_out(query_blocks)
    output_part = outer_output(branch_own, branch_other, attended_group)
    output_home = exchange(after(output_part, kv_home), CONTEXT)
    kv_home = after(kv_home, output_part)
    grad_kv_group = columns_out(unturn_kv(kv_home, cosine, sine))
    grad_qkv = jnp.concatenate([grad_query_group, grad_kv_group], axis=1)
    normed_low = core_sum(*row_products((grad_qkv,), w_qkv, 0, 384))
    part_home = exchange(after(outer(normed, grad_qkv), output_home), CONTEXT)
    (grad_normed,) = sums((own_and_received(normed_low, Y, 0),), (F32,))
    (mlp_mine,) = sums((own_and_received(after(core_sum(*mlp_rows), normed_low), Y, 0),), (F32,))
    inverse_one = inverse_root(x_mine)
    tokens_mine = from_piece_order(
        grad_h_mine + norm_back(grad_normed, x_mine, inverse_one, gain_one)
    )
    block_mine = from_piece_order(jnp.where(live_mine, hidden_mine + mlp_mine, 0.0))
    home = to_owners(pieces_sum(part_home))
    query_grad, kv_half, output_grad, block_out, tokens_grad = owners(
        home,
        output_home,
        w_query,
        keyval_half,
        (block_mine, shift(block_mine, T, 1)),
        (tokens_mine, shift(tokens_mine, T, 1)),
    )
    kv_other = shift(kv_half, T, 1)
    gate_grad, up_grad, down_grad, two_part = mlp_owners(
        to_owners(after(mlp_sum, *home[1:])), w_gate, w_up, kv_other
    )

    keyval_grad = jnp.where(
        t == 0,
        jnp.concatenate([kv_half[:, :256], kv_other[:, :256]], axis=1),
        jnp.concatenate([kv_other[:, :256], kv_half[:, :256]], axis=1),
    )
    attn_gain_grad = (kv_half[:, 256] + kv_other[:, 256]) / attn_gain.astype(F32)
    mlp_gain_grad = (two_part[:, 0] + shift(two_part, T, 1)[:, 0]) / mlp_gain.astype(F32)

    return (
        block_out[None],
        tokens_grad[None],
        attn_gain_grad,
        query_grad,
        keyval_grad,
        output_grad,
        mlp_gain_grad,
        gate_grad,
        up_grad,
        down_grad,
    )


def solution(mesh):
    torus = Mesh(
        mesh.devices.reshape(mesh.shape["shard"], 4, 4, mesh.shape["tensor"]),
        ("shard", "context_0", "context_1", "tensor"),
    )
    in_specs = (
        P("shard", CONTEXT, None),
        P("shard"),
        P(SHARD_CONTEXT),
        P(SHARD_CONTEXT, "tensor"),
        P(SHARD_CONTEXT, None),
        P(SHARD_CONTEXT, "tensor"),
        P(SHARD_CONTEXT),
        P(SHARD_CONTEXT, "tensor"),
        P(SHARD_CONTEXT, "tensor"),
        P(SHARD_CONTEXT, "tensor"),
        P("shard", CONTEXT, None),
    )
    out_specs = (
        P("shard", CONTEXT, None),
        P("shard", CONTEXT, None),
        P(SHARD_CONTEXT),
        P(SHARD_CONTEXT, "tensor"),
        P(SHARD_CONTEXT, None),
        P(SHARD_CONTEXT, "tensor"),
        P(SHARD_CONTEXT),
        P(SHARD_CONTEXT, "tensor"),
        P(SHARD_CONTEXT, "tensor"),
        P(SHARD_CONTEXT, "tensor"),
    )
    return jax.shard_map(
        shards, mesh=torus, in_specs=in_specs, out_specs=out_specs, check_vma=False
    )
```

```python
import functools

import jax
import jax.numpy as jnp
from jax import lax
from jax.experimental import pallas as pl
from jax.experimental.pallas import tpu as pltpu
from jax.sharding import Mesh
from jax.sharding import PartitionSpec as P

WINDOW = 2048
SHARD_CONTEXT = ("shard", "context_0", "context_1")
CONTEXT = ("context_0", "context_1")
PIECES = ("context_0", "context_1", "shard")
Y, X, Z, T = "shard", "context_0", "context_1", "tensor"
VMEM = pltpu.CompilerParams(vmem_limit_bytes=48 * 2**20)
ANYWHERE = pl.BlockSpec(memory_space=pl.ANY)
FREE = pl.CostEstimate(flops=0, bytes_accessed=0, transcendentals=0)

EPSILON = 1e-06
NEGATIVE_FILL = -1e30
BF = jnp.bfloat16
F32 = jnp.float32


def shift(x, axis, by):
    n = lax.axis_size(axis)
    return lax.ppermute(x, axis, [(i, (i + by) % n) for i in range(n)])


def exchange(blocks, axis):
    return lax.all_to_all(blocks, axis, 0, 0, tiled=True)


def nothing(*refs):
    pass


def after(x, *others):
    return pl.pallas_call(
        nothing,
        out_shape=jax.ShapeDtypeStruct(x.shape, x.dtype),
        in_specs=[ANYWHERE] * (1 + len(others)),
        out_specs=ANYWHERE,
        input_output_aliases={0: 0},
        compiler_params=VMEM,
        cost_estimate=FREE,
    )(x, *others)


def small_trip(x, *others):
    corner = x.reshape(-1, x.shape[-1])[:8, :128]
    return shift(after(corner, *others) if others else corner, T, 1)


def ring_blocks(x, axis):
    return [x, shift(x, axis, -1), shift(x, axis, 2), shift(x, axis, 1)]


def place_kernel(axis, sign, *refs):
    blocks, out = refs[:4], refs[-1]
    me = lax.axis_index(axis)
    for r, block in enumerate(blocks):
        out[lax.rem(me + (sign * r) % 4, 4)] = block[...]


def place(blocks, axis, *first, sign=1):
    whole = pl.BlockSpec(memory_space=pltpu.VMEM)
    return pl.pallas_call(
        functools.partial(place_kernel, axis, sign),
        out_shape=jax.ShapeDtypeStruct((4, *blocks[0].shape), blocks[0].dtype),
        in_specs=[whole] * 4 + [ANYWHERE] * len(first),
        out_specs=whole,
        compiler_params=VMEM,
        cost_estimate=FREE,
    )(*blocks, *first)


def gather_rows(mine, *first):
    own = place(ring_blocks(mine, Y), Y, *first).reshape(320, -1)
    return own, shift(own, T, 1)


def rows_kernel(count, *refs):
    lefts, rights, (far_ref, near_ref) = refs[:count], refs[count : 2 * count], refs[-2:]
    total = dot(lefts[0][...], rights[0][...], 1, 1)
    for left, right in zip(lefts[1:], rights[1:]):
        total = total + dot(left[...], right[...], 1, 1)
    near_ref[...] = total[:320].astype(BF)
    far_ref[...] = total[320:].astype(BF)


def row_products(lefts, weight, at, width, *first):
    rows, count, n = 512, len(lefts), weight.shape[0]
    half = jax.ShapeDtypeStruct((320, n), BF)
    return pl.pallas_call(
        functools.partial(rows_kernel, count),
        grid=(n // rows,),
        out_shape=(half, half),
        in_specs=[pl.BlockSpec((640, width), lambda i: (0, 0))] * count
        + [pl.BlockSpec((rows, width), lambda i, j=j: (i, at + j)) for j in range(count)]
        + [ANYWHERE] * len(first),
        out_specs=(pl.BlockSpec((320, rows), lambda i: (0, i)),) * 2,
        compiler_params=VMEM,
        cost_estimate=FREE,
    )(*lefts, *[weight] * count, *first)


def core_sum(far, near):
    return (near.astype(F32) + shift(far, T, 1).astype(F32)).astype(BF).reshape(4, 80, -1)


def own_and_received(parts, axis, dim):
    me = lax.axis_index(axis)
    own, *rest = [
        lax.dynamic_index_in_dim(parts, (me + r) % 4, dim, keepdims=False) for r in range(4)
    ]
    return [own] + [shift(rest[r - 1], axis, r) for r in (1, 3, 2)]


def sums_kernel(kinds, *refs):
    for i, out in enumerate(refs[4 * len(kinds) :]):
        total = refs[4 * i][...].astype(F32)
        for ref in refs[4 * i + 1 : 4 * i + 4]:
            total = total + ref[...].astype(F32)
        out[...] = total.astype(kinds[i])


def sums(groups, kinds):
    return pl.pallas_call(
        functools.partial(sums_kernel, kinds),
        out_shape=tuple(jax.ShapeDtypeStruct(g[0].shape, k) for g, k in zip(groups, kinds)),
        compiler_params=VMEM,
        cost_estimate=FREE,
    )(*[block for group in groups for block in group])


def outer_kernel(x_ref, g_ref, out_ref):
    out_ref[...] = dot(x_ref[...], g_ref[...], 0, 0).astype(BF).reshape(4, 160, g_ref.shape[1])


def outer(x, g):
    cols = g.shape[1]
    return pl.pallas_call(
        outer_kernel,
        grid=(4,),
        out_shape=jax.ShapeDtypeStruct((16, 160, cols), BF),
        in_specs=[
            pl.BlockSpec((640, 640), lambda i: (0, i)),
            pl.BlockSpec((640, cols), lambda i: (0, 0)),
        ],
        out_specs=pl.BlockSpec((4, 160, cols), lambda i: (i, 0, 0)),
        compiler_params=VMEM,
        cost_estimate=FREE,
    )(x, g)


def outer_output_kernel(own_ref, other_ref, ob_ref, out_ref):
    cols = ob_ref.shape[2]
    part = dot(own_ref[...], ob_ref[:, :80].reshape(320, cols), 0, 0)
    part = part + dot(other_ref[...], ob_ref[:, 80:].reshape(320, cols), 0, 0)
    out_ref[...] = part.reshape(16, 40, cols).astype(BF)


def outer_output(own, other, ob):
    cols = 640
    half = pl.BlockSpec((320, 640), lambda i: (0, 0))
    return pl.pallas_call(
        outer_output_kernel,
        grid=(2,),
        out_shape=jax.ShapeDtypeStruct((16, 40, 1280), BF),
        in_specs=[half, half, pl.BlockSpec((4, 160, cols), lambda i: (0, 0, i))],
        out_specs=pl.BlockSpec((16, 40, cols), lambda i: (0, 0, i)),
        compiler_params=VMEM,
        cost_estimate=FREE,
    )(own, other, ob)


def to_owners(sums):
    me = lax.axis_index(Y)
    rows = sums.reshape(4, -1, sums.shape[-1])
    got = []
    for r in range(4):
        block = lax.dynamic_index_in_dim(rows, (me + r) % 4, 0, keepdims=False)
        got.append(shift(block, Y, r) if r else block)
    return got


def by_half(blocks):
    cols = blocks.shape[2]
    return blocks.reshape(4, 2, 80, cols).swapaxes(0, 1).reshape(640, cols)


def columns_out(blocks):
    me = lax.axis_index(Y)
    got = []
    for r in range(4):
        block = lax.dynamic_index_in_dim(blocks, (me + r) % 4, 0, keepdims=False)
        got.append(shift(block, Y, r) if r else block)
    return by_half(place(got, Y, sign=-1))


def quarters(x):
    rows = x.shape[0]
    return x.reshape(rows, 4, -1).swapaxes(0, 1)


def pack_attention_kernel(q_ref, kv_ref, gains_ref, attn_ref):
    attn_ref[...] = jnp.zeros_like(attn_ref)
    for j in range(4):
        attn_ref[j, :40, :320] = q_ref[:, 320 * j : 320 * j + 320]
        attn_ref[j, :40, 320:] = kv_ref[:, 64 * j : 64 * j + 64]
        attn_ref[j, 40:48, :128] = gains_ref[...]


def pack_attention(w_query, keyval_half, gains):
    return pl.pallas_call(
        pack_attention_kernel,
        out_shape=jax.ShapeDtypeStruct((4, 48, 384), BF),
        compiler_params=VMEM,
        cost_estimate=FREE,
    )(w_query, keyval_half, gains)


def pack_mlp_kernel(gate_ref, up_ref, down_ref, mlp_ref):
    mlp_ref[...] = jnp.zeros_like(mlp_ref)
    for j in range(4):
        mlp_ref[j, :, :960] = gate_ref[:, 960 * j : 960 * j + 960]
        mlp_ref[j, :, 1024:1984] = up_ref[:, 960 * j : 960 * j + 960]
        mlp_ref[j, :, 2048:3008] = down_ref[:, 960 * j : 960 * j + 960]


def pack_mlp(w_gate, w_up, w_down):
    return pl.pallas_call(
        pack_mlp_kernel,
        out_shape=jax.ShapeDtypeStruct((4, 40, 3072), BF),
        compiler_params=VMEM,
        cost_estimate=FREE,
    )(w_gate, w_up, w_down)


def down_grad_kernel(y_ref, hidden_ref, *rest):
    rest[-1][...] = dot(y_ref[...], hidden_ref[...], 0, 0).astype(BF)


def down_grads(grads, hidden, *first):
    rows = 512
    return pl.pallas_call(
        down_grad_kernel,
        grid=(2560 // rows,),
        out_shape=jax.ShapeDtypeStruct((2560, 3072), BF),
        in_specs=[
            pl.BlockSpec((640, rows), lambda i: (0, i)),
            pl.BlockSpec((640, 1024), lambda i: (0, 0)),
        ]
        + [ANYWHERE] * len(first),
        out_specs=pl.BlockSpec((rows, 1024), lambda i: (i, 2)),
        compiler_params=VMEM,
        cost_estimate=FREE,
    )(grads, hidden, *first)


def gate_up_grad_kernel(x_ref, gate_ref, up_ref, *rest):
    out_ref = rest[-1]
    out_ref[:, :1024] = dot(x_ref[...], gate_ref[...], 0, 0).astype(BF)
    out_ref[:, 1024:] = dot(x_ref[...], up_ref[...], 0, 0).astype(BF)


def gate_up_grads(normed, gate, up, held, *first):
    rows = 512
    whole = pl.BlockSpec((640, 1024), lambda i: (0, 0))
    return pl.pallas_call(
        gate_up_grad_kernel,
        grid=(2560 // rows,),
        out_shape=jax.ShapeDtypeStruct((2560, 3072), BF),
        in_specs=[pl.BlockSpec((640, rows), lambda i: (0, i)), whole, whole]
        + [ANYWHERE] * (1 + len(first)),
        out_specs=pl.BlockSpec((rows, 2048), lambda i: (i, 0)),
        input_output_aliases={3: 0},
        compiler_params=VMEM,
        cost_estimate=FREE,
    )(normed, gate, up, held, *first)


def feed_forward_kernel(x_ref, y_ref, gate_ref, up_ref, down_ref, *rest):
    hidden_out, gate_out, up_out = rest[-3:]
    gate = dot(x_ref[...], gate_ref[...], 1, 0)
    up = dot(x_ref[...], up_ref[...], 1, 0)
    grad = dot(y_ref[...], down_ref[...], 1, 0)
    scale = 0.7978845608028654
    square = gate * gate
    bent = jnp.tanh(scale * gate * (1.0 + 0.044715 * square))
    share = 0.5 * (1.0 + bent)
    slope = share + 0.5 * gate * (1.0 - bent * bent) * scale * (1.0 + 0.134145 * square)
    active = gate * share
    hidden_out[...] = (active * up).astype(BF)
    gate_out[...] = (grad * up * slope).astype(BF)
    up_out[...] = (grad * active).astype(BF)


def feed_forward(x, y, w_mlp, *first):
    cols = 256
    steps = 1024 // cols
    part = jax.ShapeDtypeStruct((640, 1024), BF)
    whole = pl.BlockSpec((640, 2560), lambda j: (0, 0))
    out = pl.BlockSpec((640, cols), lambda j: (0, j))
    return pl.pallas_call(
        feed_forward_kernel,
        grid=(steps,),
        out_shape=(part, part, part),
        in_specs=[whole, whole]
        + [pl.BlockSpec((2560, cols), lambda j, k=k: (0, k * steps + j)) for k in range(3)]
        + [ANYWHERE] * len(first),
        out_specs=(out, out, out),
        compiler_params=VMEM,
        cost_estimate=FREE,
    )(x, y, w_mlp, w_mlp, w_mlp, *first)


def to_piece_order(x):
    rows = x.shape[0]
    return x.reshape(rows, 4, 16, 40).swapaxes(1, 2).reshape(rows, 2560)


def inverse_root(values):
    return lax.rsqrt(jnp.mean(values * values, axis=-1, keepdims=True) + EPSILON)


def norm_back(grad, values, inverse, gain):
    scaled = gain * grad
    return inverse * scaled - values * inverse**3 * jnp.mean(
        scaled * values, axis=-1, keepdims=True
    )


def angles(position, head_dim):
    quarter = head_dim // 4
    frequency = 10000.0 ** (-jnp.arange(quarter, dtype=F32) / quarter)
    phase_angle = position[:, None].astype(F32) * frequency[None, :]
    return (jnp.cos(phase_angle), jnp.sin(phase_angle))


def dot(a, b, da, db):
    return lax.dot_general(a, b, (((da,), (db,)), ((), ())), preferred_element_type=F32)


def feature_quarters_kernel(x_ref, out_ref):
    for j in range(4):
        for p in range(16):
            at = 40 * (4 * p + j)
            out_ref[j, :, 40 * p : 40 * p + 40] = x_ref[:, at : at + 40].astype(BF)


def feature_quarters(x):
    return pl.pallas_call(
        feature_quarters_kernel,
        out_shape=jax.ShapeDtypeStruct((4, 80, 640), BF),
        compiler_params=VMEM,
        cost_estimate=FREE,
    )(x)


def project_kernel(own_ref, other_ref, gain_ref, weight_ref, normed_ref, out_ref):
    x = jnp.concatenate([own_ref[0], other_ref[0]]).astype(F32)
    normed = (x * inverse_root(x) * gain_ref[...]).astype(BF)
    normed_ref[0] = normed[:80]
    normed_ref[1] = normed[80:]
    out_ref[0] = dot(normed, weight_ref[...], 1, 0).astype(BF)


def project(own, other, gain, weight):
    rows = pl.BlockSpec((1, 80, 2560), lambda i: (i, 0, 0))
    normed, out = pl.pallas_call(
        project_kernel,
        grid=(4,),
        out_shape=(
            jax.ShapeDtypeStruct((2, 320, 2560), BF),
            jax.ShapeDtypeStruct((4, 160, 384), BF),
        ),
        in_specs=[
            rows,
            rows,
            pl.BlockSpec((1, 2560), lambda i: (0, 0)),
            pl.BlockSpec((2560, 384), lambda i: (0, 0)),
        ],
        out_specs=(
            pl.BlockSpec((2, 80, 2560), lambda i: (0, i, 0)),
            pl.BlockSpec((1, 160, 384), lambda i: (i, 0, 0)),
        ),
        compiler_params=VMEM,
        cost_estimate=FREE,
    )(own, other, gain, weight)
    return normed.reshape(640, 2560), out


def owners_kernel(*refs):
    home, mlp = refs[:4], refs[4:8]
    output_home, query_ref, keyval_ref, gate_ref, up_ref, block_mine, block_other, rows_mine, rows_other = refs[8:17]
    query_out, keyval_out, output_out, gate_out, up_out, down_out, gain_out, block_out, rows_out = refs[17:26]
    held, held_mlp = refs[26:]
    me = lax.axis_index(Y)
    for r in range(4):
        held[lax.rem(me + 4 - r, 4)] = home[r][...]
        held_mlp[lax.rem(me + 4 - r, 4)] = mlp[r][...]
    for j in range(4):
        columns = slice(960 * j, 960 * j + 960)
        gate_out[:, columns] = held_mlp[j, :, :960].astype(F32)
        up_out[:, columns] = held_mlp[j, :, 1024:1984].astype(F32)
        down_out[:, columns] = held_mlp[j, :, 2048:3008].astype(F32)
        total = held[j].astype(F32)
        query_out[:, 320 * j : 320 * j + 320] = total[:, :320]
        keyval_out[:, 64 * j : 64 * j + 64] = total[:, 320:384]
    total = output_home[0].astype(F32)
    for p in range(1, 16):
        total = total + output_home[p].astype(F32)
    output_out[...] = total

    def products(weight, grad):
        return jnp.sum(weight[...].astype(F32) * grad[...], axis=1, keepdims=True)

    one = products(query_ref, query_out) + products(keyval_ref, keyval_out)
    two = products(gate_ref, gate_out) + products(up_ref, up_out)
    gain_out[:, :128] = jnp.broadcast_to(one, (40, 128))
    gain_out[:, 128:] = jnp.broadcast_to(two, (40, 128))
    at = 80 * lax.axis_index(T)
    for mine, other, out in ((block_mine, block_other, block_out), (rows_mine, rows_other, rows_out)):
        out[pl.ds(pl.multiple_of(at, 16), 80), :] = mine[...]
        out[pl.ds(pl.multiple_of(80 - at, 16), 80), :] = other[...]


def owners(home, mlp, output_home, w_query, keyval_half, w_gate, w_up, block, rows):
    wide, narrow = (jax.ShapeDtypeStruct((40, n), F32) for n in (3840, 1280))
    small = jax.ShapeDtypeStruct((40, 256), F32)
    tokens = jax.ShapeDtypeStruct((160, 2560), BF)
    return pl.pallas_call(
        owners_kernel,
        out_shape=(narrow, small, narrow, wide, wide, wide, small, tokens, tokens),
        scratch_shapes=[pltpu.VMEM((4, 40, 384), BF), pltpu.VMEM((4, 40, 3072), BF)],
        compiler_params=VMEM,
        cost_estimate=FREE,
    )(*home, *mlp, output_home, w_query, keyval_half, w_gate, w_up, *block, *rows)


def turned(values, cosine, sine):
    one, two = values[:, :64], values[:, 64:128]
    return jnp.concatenate(
        [one * cosine - two * sine, two * cosine + one * sine, values[:, 128:]], axis=1
    )


def prepare_kernel(scale, home_ref, cosine_ref, sine_ref, query_ref, kv_ref, wide):
    cosine, sine = cosine_ref[...], sine_ref[...]
    for j in range(4):
        wide[:, 320 * j : 320 * j + 320] = home_ref[j, :, :320].astype(F32)
    for h in range(5):
        head = turned(wide[:, 256 * h : 256 * h + 256], cosine, sine)
        query_ref[h] = (head * scale).astype(BF)
    for j in range(4):
        wide[:, 64 * j : 64 * j + 64] = home_ref[j, :, 320:].astype(F32)
    first = lax.axis_index(T) == 0
    kv = wide[:, :256]
    kv = jnp.where(first, turned(kv, cosine, sine), kv).astype(BF)
    at = 80 * lax.axis_index(T)
    kv_ref[pl.ds(pl.multiple_of(at, 16), 80), :] = kv[:80]
    kv_ref[pl.ds(pl.multiple_of(80 - at, 16), 80), :] = kv[80:]


def prepare(home, cosine, sine, scale):
    return pl.pallas_call(
        functools.partial(prepare_kernel, scale),
        out_shape=(
            jax.ShapeDtypeStruct((5, 160, 256), BF),
            jax.ShapeDtypeStruct((160, 256), BF),
        ),
        scratch_shapes=[pltpu.VMEM((160, 1280), F32)],
        compiler_params=VMEM,
        cost_estimate=FREE,
    )(home, cosine, sine)


def unturn_kernel(scale, grad_ref, cosine_ref, sine_ref, out_ref, wide):
    cosine, sine = cosine_ref[...], -sine_ref[...]
    for h in range(5):
        wide[:, 256 * h : 256 * h + 256] = turned(grad_ref[h] * scale, cosine, sine)
    for j in range(4):
        out_ref[j] = wide[:, 320 * j : 320 * j + 320].astype(BF)


def unturn(grad, cosine, sine, scale):
    return pl.pallas_call(
        functools.partial(unturn_kernel, scale),
        out_shape=jax.ShapeDtypeStruct((4, 160, 320), BF),
        scratch_shapes=[pltpu.VMEM((160, 1280), F32)],
        compiler_params=VMEM,
        cost_estimate=FREE,
    )(grad, cosine, sine)


def unturn_kv_kernel(home_ref, cosine_ref, sine_ref, out_ref, held):
    total = home_ref[0].astype(F32)
    for p in range(1, 16):
        total = total + home_ref[p].astype(F32)
    held[...] = total
    at = 80 * lax.axis_index(T)
    total = jnp.concatenate(
        [held[pl.ds(pl.multiple_of(at, 16), 80), :], held[pl.ds(pl.multiple_of(80 - at, 16), 80), :]]
    )
    back = turned(total, cosine_ref[...], -sine_ref[...])
    total = jnp.where(lax.axis_index(T) == 0, back, total).astype(BF)
    for j in range(4):
        out_ref[j] = total[:, 64 * j : 64 * j + 64]


def unturn_kv(home, cosine, sine):
    return pl.pallas_call(
        unturn_kv_kernel,
        out_shape=jax.ShapeDtypeStruct((4, 160, 64), BF),
        scratch_shapes=[pltpu.VMEM((160, 256), F32)],
        compiler_params=VMEM,
        cost_estimate=FREE,
    )(home, cosine, sine)


def pieces_kernel(home_ref, out_ref):
    total = home_ref[0].astype(F32)
    for p in range(1, 16):
        total = total + home_ref[p].astype(F32)
    out_ref[...] = total.astype(BF)


def pieces_sum(home):
    cols = home.shape[2]
    return pl.pallas_call(
        pieces_kernel,
        grid=(2,),
        in_specs=[pl.BlockSpec((16, 80, cols), lambda i: (0, i, 0))],
        out_specs=pl.BlockSpec((80, cols), lambda i: (i, 0)),
        out_shape=jax.ShapeDtypeStruct((160, cols), BF),
        compiler_params=VMEM,
        cost_estimate=FREE,
    )(home)


def token_order_kernel(x_ref, out_ref):
    for j in range(4):
        for p in range(16):
            to, at = 40 * (16 * j + p), 40 * (4 * p + j)
            out_ref[:, to : to + 40] = x_ref[:, at : at + 40].astype(BF)


def from_piece_order(x):
    return pl.pallas_call(
        token_order_kernel, out_shape=jax.ShapeDtypeStruct(x.shape, BF), compiler_params=VMEM, cost_estimate=FREE
    )(x)


def shards(
    tokens,
    lengths,
    attn_gain,
    w_query,
    w_keyval,
    w_output,
    mlp_gain,
    w_gate,
    w_up,
    w_down,
    cotangent,
):
    t = lax.axis_index(T)
    me = lax.axis_index(Y)
    piece = lax.axis_index(CONTEXT)
    head_dim = 256
    query_scale = head_dim ** (-0.5)
    seq_count = 2560
    padding = seq_count - lengths[0]
    row_start = piece * 160
    turned_index = row_start + (jnp.arange(160, dtype=jnp.int32) + t * 80) % 160
    live_turned = turned_index >= padding
    live_mine = live_turned[:80, None]

    x_low = to_piece_order(lax.dynamic_slice_in_dim(tokens[0], t * 80, 80, 0))
    cot_mine = to_piece_order(lax.dynamic_slice_in_dim(cotangent[0], t * 80, 80, 0))
    grad_mine = jnp.where(live_mine, cot_mine, jnp.zeros_like(cot_mine))
    x_mine = x_low.astype(F32)
    x_blocks = ring_blocks(x_low, Y)
    w_out = lax.all_gather(w_output, PIECES, axis=0, tiled=True)

    keyval_half = lax.dynamic_slice_in_dim(w_keyval, t * 256, 256, 1)
    gains = jnp.concatenate([attn_gain, mlp_gain])[None, :]
    gains = jnp.pad(gains, ((0, 7), (0, 48)))
    attn_blocks = pack_attention(w_query, keyval_half, gains)
    attn_rows = place(to_owners(attn_blocks), Y, sign=-1)
    attn_copies = jnp.broadcast_to(attn_rows[None], (16, 4, 48, 384))
    attn_all = exchange(attn_copies, CONTEXT).reshape(64, 48, 384)
    w_qkv = attn_all[:, :40].reshape(2560, 384)
    gain_one = attn_all[:, 40, :40].reshape(1, 2560).astype(F32)
    gain_two = attn_all[:, 40, 40:80].reshape(1, 2560).astype(F32)
    x_own = place(x_blocks, Y, attn_all)
    x_other = shift(x_own, T, 1)
    mlp_blocks = pack_mlp(w_gate, w_up, w_down)
    mlp_got = to_owners(mlp_blocks)
    mlp_block = place(mlp_got, Y, x_own, sign=-1).reshape(160, 3072)
    w_mlp = lax.all_gather(mlp_block, CONTEXT, axis=0, tiled=True)

    normed, projected = project(x_own, x_other, gain_one, w_qkv)
    home = exchange(projected, Y)
    cosine, sine = angles(turned_index - padding, head_dim)
    queries, kv_own = prepare(home, cosine, sine, query_scale)
    kv_mine = exchange(jnp.broadcast_to(kv_own[None], (16, 160, 256)), CONTEXT).reshape(2560, 256)
    grad_own = place(ring_blocks(after(grad_mine, kv_own), Y), Y).reshape(320, 2560)
    grad_group = jnp.concatenate([grad_own, shift(grad_own, T, 1)])
    kv_mine = after(kv_mine, grad_own)
    kv_other = shift(kv_mine, T, 1)
    keys = jnp.where(t == 0, kv_mine, kv_other)
    values = jnp.where(t == 0, kv_other, kv_mine)

    key_index = jnp.arange(seq_count, dtype=jnp.int32)
    offset = turned_index[:, None] - key_index[None, :]
    allowed = ((offset >= 0) & (offset < WINDOW) & (key_index >= padding)[None, :])[None]
    live = live_turned[None, :, None]
    scores = jnp.einsum("hqd,kd->hqk", queries, keys, preferred_element_type=F32)
    row_top = jnp.max(jnp.where(allowed, scores, NEGATIVE_FILL), axis=-1, keepdims=True)
    row_top = jnp.where(live, row_top, 0.0)
    weights_exp = jnp.where(allowed, jnp.exp(scores - row_top), 0.0)
    row_total = jnp.where(live, jnp.sum(weights_exp, axis=-1, keepdims=True), 1.0)
    prob = weights_exp / row_total
    prob_low = prob.astype(BF)
    attended = jnp.einsum("hqk,kd->qhd", prob_low, values, preferred_element_type=F32)
    attended = attended.reshape(160, 1280).astype(BF)

    branch = dot(attended, w_out, 1, 1)
    hidden_mine = x_mine + branch[:80] + shift(branch[80:], T, 1)

    inverse_two = inverse_root(hidden_mine)
    normed_two_mine = (hidden_mine * inverse_two * gain_two).astype(BF)
    normed_two = jnp.concatenate(gather_rows(after(normed_two_mine, grad_group)))
    hidden, grad_gate, grad_up = feed_forward(normed_two, grad_group, w_mlp)
    attended_group = place(ring_blocks(attended, Y), Y)
    normed_two_low = core_sum(*row_products((grad_gate, grad_up), w_mlp, 0, 1024, attended_group))
    got = own_and_received(normed_two_low, Y, 0)

    mlp_rows = row_products((hidden,), w_mlp, 2, 1024, normed_two_low)
    down_part = down_grads(grad_group, hidden, *mlp_rows)
    mlp_part = gate_up_grads(normed_two, grad_gate, grad_up, down_part, *got)
    mlp_sum = lax.psum_scatter(mlp_part, CONTEXT, scatter_dimension=0, tiled=True)
    grad_normed_two = sum(block.astype(F32) for block in got)

    grad_h_mine = grad_mine.astype(F32) + norm_back(
        grad_normed_two, hidden_mine, inverse_two, gain_two
    )
    branch_mine = grad_h_mine.astype(BF)
    branch_own = place(to_owners(feature_quarters(grad_h_mine)), Y, sign=-1).reshape(320, 640)
    branch_other = shift(branch_own, T, 1)
    branch_low = jnp.concatenate([branch_mine, shift(branch_mine, T, 1)])
    grad_attended = dot(branch_low, w_out, 1, 0).astype(BF).reshape(160, 5, head_dim)

    grad_prob = jnp.einsum("qhd,kd->hqk", grad_attended, values, preferred_element_type=F32)
    spread = jnp.sum(prob * grad_prob, axis=-1, keepdims=True)
    grad_scores = (prob * (grad_prob - spread)).astype(BF)
    grad_keys = jnp.einsum("hqk,hqd->kd", grad_scores, queries, preferred_element_type=F32)
    grad_values = jnp.einsum("hqk,qhd->kd", prob_low, grad_attended, preferred_element_type=F32)
    keep = jnp.where(t == 0, grad_keys, grad_values)
    give = jnp.where(t == 0, grad_values, grad_keys).astype(BF)
    grad_queries = jnp.einsum("hqk,kd->hqd", grad_scores, keys, preferred_element_type=F32)
    query_blocks = unturn(grad_queries, cosine, sine, query_scale)
    kv_part = (keep + shift(give, T, 1).astype(F32)).astype(BF).reshape(16, 160, 256)
    kv_part = after(kv_part, query_blocks)
    kv_home = exchange(kv_part, CONTEXT)
    grad_query_group = columns_out(query_blocks)
    output_part = outer_output(branch_own, branch_other, attended_group)
    output_home = exchange(after(output_part, kv_home), CONTEXT)
    kv_home = after(kv_home, output_part)
    grad_kv_group = columns_out(unturn_kv(kv_home, cosine, sine))
    grad_qkv = jnp.concatenate([grad_query_group, grad_kv_group], axis=1)
    normed_low = core_sum(*row_products((grad_qkv,), w_qkv, 0, 384))
    part_home = exchange(after(outer(normed, grad_qkv), output_home), CONTEXT)
    (grad_normed,) = sums((own_and_received(normed_low, Y, 0),), (F32,))
    (mlp_mine,) = sums((own_and_received(after(core_sum(*mlp_rows), normed_low), Y, 0),), (F32,))
    inverse_one = inverse_root(x_mine)
    tokens_mine = from_piece_order(
        grad_h_mine + norm_back(grad_normed, x_mine, inverse_one, gain_one)
    )
    block_mine = from_piece_order(jnp.where(live_mine, hidden_mine + mlp_mine, 0.0))
    mlp_home = to_owners(mlp_sum)
    home = to_owners(pieces_sum(part_home))
    query_grad, kv_half, output_grad, gate_grad, up_grad, down_grad, gain_part, block_out, tokens_grad = owners(
        home,
        mlp_home,
        output_home,
        w_query,
        keyval_half,
        w_gate,
        w_up,
        (block_mine, shift(block_mine, T, 1)),
        (tokens_mine, shift(tokens_mine, T, 1)),
    )

    mine = jnp.concatenate([kv_half, gain_part], axis=1)
    other = shift(mine, T, 1)
    kv_other = other[:, :256]
    keyval_grad = jnp.where(
        t == 0,
        jnp.concatenate([kv_half, kv_other], axis=1),
        jnp.concatenate([kv_other, kv_half], axis=1),
    )
    attn_gain_grad = (mine[:, 256] + other[:, 256]) / attn_gain.astype(F32)
    mlp_gain_grad = (mine[:, 384] + other[:, 384]) / mlp_gain.astype(F32)

    return (
        block_out[None],
        tokens_grad[None],
        attn_gain_grad,
        query_grad,
        keyval_grad,
        output_grad,
        mlp_gain_grad,
        gate_grad,
        up_grad,
        down_grad,
    )


def solution(mesh):
    torus = Mesh(
        mesh.devices.reshape(mesh.shape["shard"], 4, 4, mesh.shape["tensor"]),
        ("shard", "context_0", "context_1", "tensor"),
    )
    in_specs = (
        P("shard", CONTEXT, None),
        P("shard"),
        P(SHARD_CONTEXT),
        P(SHARD_CONTEXT, "tensor"),
        P(SHARD_CONTEXT, None),
        P(SHARD_CONTEXT, "tensor"),
        P(SHARD_CONTEXT),
        P(SHARD_CONTEXT, "tensor"),
        P(SHARD_CONTEXT, "tensor"),
        P(SHARD_CONTEXT, "tensor"),
        P("shard", CONTEXT, None),
    )
    out_specs = (
        P("shard", CONTEXT, None),
        P("shard", CONTEXT, None),
        P(SHARD_CONTEXT),
        P(SHARD_CONTEXT, "tensor"),
        P(SHARD_CONTEXT, None),
        P(SHARD_CONTEXT, "tensor"),
        P(SHARD_CONTEXT),
        P(SHARD_CONTEXT, "tensor"),
        P(SHARD_CONTEXT, "tensor"),
        P(SHARD_CONTEXT, "tensor"),
    )
    return jax.shard_map(
        shards, mesh=torus, in_specs=in_specs, out_specs=out_specs, check_vma=False
    )
```

```python
import functools

import jax
import jax.numpy as jnp
from jax import lax
from jax.experimental import pallas as pl
from jax.experimental.pallas import tpu as pltpu
from jax.sharding import Mesh
from jax.sharding import PartitionSpec as P

WINDOW = 2048
SHARD_CONTEXT = ("shard", "context_0", "context_1")
CONTEXT = ("context_0", "context_1")
PIECES = ("context_0", "context_1", "shard")
Y, X, Z, T = "shard", "context_0", "context_1", "tensor"
VMEM = pltpu.CompilerParams(vmem_limit_bytes=48 * 2**20)
ANYWHERE = pl.BlockSpec(memory_space=pl.ANY)
FREE = pl.CostEstimate(flops=0, bytes_accessed=0, transcendentals=0)

EPSILON = 1e-06
NEGATIVE_FILL = -1e30
BF = jnp.bfloat16
F32 = jnp.float32


def shift(x, axis, by):
    n = lax.axis_size(axis)
    return lax.ppermute(x, axis, [(i, (i + by) % n) for i in range(n)])


def exchange(blocks, axis):
    return lax.all_to_all(blocks, axis, 0, 0, tiled=True)


def nothing(*refs):
    pass


def after(x, *others):
    return pl.pallas_call(
        nothing,
        out_shape=jax.ShapeDtypeStruct(x.shape, x.dtype),
        in_specs=[ANYWHERE] * (1 + len(others)),
        out_specs=ANYWHERE,
        input_output_aliases={0: 0},
        compiler_params=VMEM,
        cost_estimate=FREE,
    )(x, *others)


def small_trip(x, *others):
    corner = x.reshape(-1, x.shape[-1])[:8, :128]
    return shift(after(corner, *others) if others else corner, T, 1)


def ring_blocks(x, axis):
    return [x, shift(x, axis, -1), shift(x, axis, 2), shift(x, axis, 1)]


def place_kernel(axis, sign, *refs):
    blocks, out = refs[:4], refs[-1]
    me = lax.axis_index(axis)
    for r, block in enumerate(blocks):
        out[lax.rem(me + (sign * r) % 4, 4)] = block[...]


def place(blocks, axis, *first, sign=1):
    whole = pl.BlockSpec(memory_space=pltpu.VMEM)
    return pl.pallas_call(
        functools.partial(place_kernel, axis, sign),
        out_shape=jax.ShapeDtypeStruct((4, *blocks[0].shape), blocks[0].dtype),
        in_specs=[whole] * 4 + [ANYWHERE] * len(first),
        out_specs=whole,
        compiler_params=VMEM,
        cost_estimate=FREE,
    )(*blocks, *first)


def gather_rows(mine, *first):
    own = place(ring_blocks(mine, Y), Y, *first).reshape(320, -1)
    return own, shift(own, T, 1)


def rows_kernel(count, *refs):
    lefts, rights, (far_ref, near_ref) = refs[:count], refs[count : 2 * count], refs[-2:]
    total = dot(lefts[0][...], rights[0][...], 1, 1)
    for left, right in zip(lefts[1:], rights[1:]):
        total = total + dot(left[...], right[...], 1, 1)
    near_ref[...] = total[:320].astype(BF)
    far_ref[...] = total[320:].astype(BF)


def row_products(lefts, weight, at, width, *first):
    rows, count, n = 512, len(lefts), weight.shape[0]
    half = jax.ShapeDtypeStruct((320, n), BF)
    return pl.pallas_call(
        functools.partial(rows_kernel, count),
        grid=(n // rows,),
        out_shape=(half, half),
        in_specs=[pl.BlockSpec((640, width), lambda i: (0, 0))] * count
        + [pl.BlockSpec((rows, width), lambda i, j=j: (i, at + j)) for j in range(count)]
        + [ANYWHERE] * len(first),
        out_specs=(pl.BlockSpec((320, rows), lambda i: (0, i)),) * 2,
        compiler_params=VMEM,
        cost_estimate=FREE,
    )(*lefts, *[weight] * count, *first)


def core_sum(far, near):
    return (near.astype(F32) + shift(far, T, 1).astype(F32)).astype(BF).reshape(4, 80, -1)


def own_and_received(parts, axis, dim):
    me = lax.axis_index(axis)
    own, *rest = [
        lax.dynamic_index_in_dim(parts, (me + r) % 4, dim, keepdims=False) for r in range(4)
    ]
    return [own] + [shift(rest[r - 1], axis, r) for r in (1, 3, 2)]


def sums_kernel(kinds, *refs):
    for i, out in enumerate(refs[4 * len(kinds) :]):
        total = refs[4 * i][...].astype(F32)
        for ref in refs[4 * i + 1 : 4 * i + 4]:
            total = total + ref[...].astype(F32)
        out[...] = total.astype(kinds[i])


def sums(groups, kinds):
    return pl.pallas_call(
        functools.partial(sums_kernel, kinds),
        out_shape=tuple(jax.ShapeDtypeStruct(g[0].shape, k) for g, k in zip(groups, kinds)),
        compiler_params=VMEM,
        cost_estimate=FREE,
    )(*[block for group in groups for block in group])


def outer_kernel(x_ref, g_ref, out_ref):
    out_ref[...] = dot(x_ref[...], g_ref[...], 0, 0).astype(BF).reshape(4, 160, g_ref.shape[1])


def outer(x, g):
    cols = g.shape[1]
    return pl.pallas_call(
        outer_kernel,
        grid=(4,),
        out_shape=jax.ShapeDtypeStruct((16, 160, cols), BF),
        in_specs=[
            pl.BlockSpec((640, 640), lambda i: (0, i)),
            pl.BlockSpec((640, cols), lambda i: (0, 0)),
        ],
        out_specs=pl.BlockSpec((4, 160, cols), lambda i: (i, 0, 0)),
        compiler_params=VMEM,
        cost_estimate=FREE,
    )(x, g)


def outer_output_kernel(own_ref, other_ref, ob_ref, out_ref):
    cols = ob_ref.shape[2]
    part = dot(own_ref[...], ob_ref[:, :80].reshape(320, cols), 0, 0)
    part = part + dot(other_ref[...], ob_ref[:, 80:].reshape(320, cols), 0, 0)
    out_ref[...] = part.reshape(16, 40, cols).astype(BF)


def outer_output(own, other, ob):
    cols = 640
    half = pl.BlockSpec((320, 640), lambda i: (0, 0))
    return pl.pallas_call(
        outer_output_kernel,
        grid=(2,),
        out_shape=jax.ShapeDtypeStruct((16, 40, 1280), BF),
        in_specs=[half, half, pl.BlockSpec((4, 160, cols), lambda i: (0, 0, i))],
        out_specs=pl.BlockSpec((16, 40, cols), lambda i: (0, 0, i)),
        compiler_params=VMEM,
        cost_estimate=FREE,
    )(own, other, ob)


def to_owners(sums):
    me = lax.axis_index(Y)
    rows = sums.reshape(4, -1, sums.shape[-1])
    got = []
    for r in range(4):
        block = lax.dynamic_index_in_dim(rows, (me + r) % 4, 0, keepdims=False)
        got.append(shift(block, Y, r) if r else block)
    return got


def by_half(blocks):
    cols = blocks.shape[2]
    return blocks.reshape(4, 2, 80, cols).swapaxes(0, 1).reshape(640, cols)


def columns_out(blocks):
    me = lax.axis_index(Y)
    got = []
    for r in range(4):
        block = lax.dynamic_index_in_dim(blocks, (me + r) % 4, 0, keepdims=False)
        got.append(shift(block, Y, r) if r else block)
    return by_half(place(got, Y, sign=-1))


def quarters(x):
    rows = x.shape[0]
    return x.reshape(rows, 4, -1).swapaxes(0, 1)


def pack_attention_kernel(q_ref, kv_ref, gains_ref, attn_ref):
    attn_ref[...] = jnp.zeros_like(attn_ref)
    for j in range(4):
        attn_ref[j, :40, :320] = q_ref[:, 320 * j : 320 * j + 320]
        attn_ref[j, :40, 320:] = kv_ref[:, 64 * j : 64 * j + 64]
        attn_ref[j, 40:48, :128] = gains_ref[...]


def pack_attention(w_query, keyval_half, gains):
    return pl.pallas_call(
        pack_attention_kernel,
        out_shape=jax.ShapeDtypeStruct((4, 48, 384), BF),
        compiler_params=VMEM,
        cost_estimate=FREE,
    )(w_query, keyval_half, gains)


def pack_mlp_kernel(gate_ref, up_ref, down_ref, mlp_ref):
    mlp_ref[...] = jnp.zeros_like(mlp_ref)
    for j in range(4):
        mlp_ref[j, :, :960] = gate_ref[:, 960 * j : 960 * j + 960]
        mlp_ref[j, :, 1024:1984] = up_ref[:, 960 * j : 960 * j + 960]
        mlp_ref[j, :, 2048:3008] = down_ref[:, 960 * j : 960 * j + 960]


def pack_mlp(w_gate, w_up, w_down):
    return pl.pallas_call(
        pack_mlp_kernel,
        out_shape=jax.ShapeDtypeStruct((4, 40, 3072), BF),
        compiler_params=VMEM,
        cost_estimate=FREE,
    )(w_gate, w_up, w_down)


def gate_up_grad_kernel(x_ref, gate_ref, up_ref, *rest):
    out_ref = rest[-1]
    out_ref[:, :1024] = dot(x_ref[...], gate_ref[...], 0, 0).astype(BF)
    out_ref[:, 1024:] = dot(x_ref[...], up_ref[...], 0, 0).astype(BF)


def gate_up_grads(normed, gate, up, *first):
    rows = 512
    whole = pl.BlockSpec((640, 1024), lambda i: (0, 0))
    return pl.pallas_call(
        gate_up_grad_kernel,
        grid=(2560 // rows,),
        out_shape=jax.ShapeDtypeStruct((2560, 3072), BF),
        in_specs=[pl.BlockSpec((640, rows), lambda i: (0, i)), whole, whole]
        + [ANYWHERE] * len(first),
        out_specs=pl.BlockSpec((rows, 2048), lambda i: (i, 0)),
        compiler_params=VMEM,
        cost_estimate=FREE,
    )(normed, gate, up, *first)


def down_grad_kernel(y_ref, hidden_ref, *rest):
    rest[-1][...] = dot(y_ref[...], hidden_ref[...], 0, 0).astype(BF)


def down_grads(grads, hidden, held, *first):
    rows = 512
    return pl.pallas_call(
        down_grad_kernel,
        grid=(2560 // rows,),
        out_shape=jax.ShapeDtypeStruct((2560, 3072), BF),
        in_specs=[
            pl.BlockSpec((640, rows), lambda i: (0, i)),
            pl.BlockSpec((640, 1024), lambda i: (0, 0)),
        ]
        + [ANYWHERE] * (1 + len(first)),
        out_specs=pl.BlockSpec((rows, 1024), lambda i: (i, 2)),
        input_output_aliases={2: 0},
        compiler_params=VMEM,
        cost_estimate=FREE,
    )(grads, hidden, held, *first)


def feed_forward_kernel(x_ref, y_ref, gate_ref, up_ref, down_ref, *rest):
    hidden_out, gate_out, up_out = rest[-3:]
    gate = dot(x_ref[...], gate_ref[...], 1, 0)
    up = dot(x_ref[...], up_ref[...], 1, 0)
    grad = dot(y_ref[...], down_ref[...], 1, 0)
    scale = 0.7978845608028654
    square = gate * gate
    bent = jnp.tanh(scale * gate * (1.0 + 0.044715 * square))
    share = 0.5 * (1.0 + bent)
    slope = share + 0.5 * gate * (1.0 - bent * bent) * scale * (1.0 + 0.134145 * square)
    active = gate * share
    hidden_out[...] = (active * up).astype(BF)
    gate_out[...] = (grad * up * slope).astype(BF)
    up_out[...] = (grad * active).astype(BF)


def feed_forward(x, y, w_mlp, *first):
    cols = 256
    steps = 1024 // cols
    part = jax.ShapeDtypeStruct((640, 1024), BF)
    whole = pl.BlockSpec((640, 2560), lambda j: (0, 0))
    out = pl.BlockSpec((640, cols), lambda j: (0, j))
    return pl.pallas_call(
        feed_forward_kernel,
        grid=(steps,),
        out_shape=(part, part, part),
        in_specs=[whole, whole]
        + [pl.BlockSpec((2560, cols), lambda j, k=k: (0, k * steps + j)) for k in range(3)]
        + [ANYWHERE] * len(first),
        out_specs=(out, out, out),
        compiler_params=VMEM,
        cost_estimate=FREE,
    )(x, y, w_mlp, w_mlp, w_mlp, *first)


def to_piece_order(x):
    rows = x.shape[0]
    return x.reshape(rows, 4, 16, 40).swapaxes(1, 2).reshape(rows, 2560)


def inverse_root(values):
    return lax.rsqrt(jnp.mean(values * values, axis=-1, keepdims=True) + EPSILON)


def norm_back(grad, values, inverse, gain):
    scaled = gain * grad
    return inverse * scaled - values * inverse**3 * jnp.mean(
        scaled * values, axis=-1, keepdims=True
    )


def angles(position, head_dim):
    quarter = head_dim // 4
    frequency = 10000.0 ** (-jnp.arange(quarter, dtype=F32) / quarter)
    phase_angle = position[:, None].astype(F32) * frequency[None, :]
    return (jnp.cos(phase_angle), jnp.sin(phase_angle))


def dot(a, b, da, db):
    return lax.dot_general(a, b, (((da,), (db,)), ((), ())), preferred_element_type=F32)


def feature_quarters_kernel(x_ref, out_ref):
    for j in range(4):
        for p in range(16):
            at = 40 * (4 * p + j)
            out_ref[j, :, 40 * p : 40 * p + 40] = x_ref[:, at : at + 40].astype(BF)


def feature_quarters(x):
    return pl.pallas_call(
        feature_quarters_kernel,
        out_shape=jax.ShapeDtypeStruct((4, 80, 640), BF),
        compiler_params=VMEM,
        cost_estimate=FREE,
    )(x)


def project_kernel(own_ref, other_ref, gain_ref, weight_ref, normed_ref, out_ref):
    x = jnp.concatenate([own_ref[0], other_ref[0]]).astype(F32)
    normed = (x * inverse_root(x) * gain_ref[...]).astype(BF)
    normed_ref[0] = normed[:80]
    normed_ref[1] = normed[80:]
    out_ref[0] = dot(normed, weight_ref[...], 1, 0).astype(BF)


def project(own, other, gain, weight):
    rows = pl.BlockSpec((1, 80, 2560), lambda i: (i, 0, 0))
    normed, out = pl.pallas_call(
        project_kernel,
        grid=(4,),
        out_shape=(
            jax.ShapeDtypeStruct((2, 320, 2560), BF),
            jax.ShapeDtypeStruct((4, 160, 384), BF),
        ),
        in_specs=[
            rows,
            rows,
            pl.BlockSpec((1, 2560), lambda i: (0, 0)),
            pl.BlockSpec((2560, 384), lambda i: (0, 0)),
        ],
        out_specs=(
            pl.BlockSpec((2, 80, 2560), lambda i: (0, i, 0)),
            pl.BlockSpec((1, 160, 384), lambda i: (i, 0, 0)),
        ),
        compiler_params=VMEM,
        cost_estimate=FREE,
    )(own, other, gain, weight)
    return normed.reshape(640, 2560), out


def owners_kernel(*refs):
    home, mlp = refs[:4], refs[4:8]
    output_home, query_ref, keyval_ref, gate_ref, up_ref, block_mine, block_other, rows_mine, rows_other = refs[8:17]
    query_out, keyval_out, output_out, gate_out, up_out, down_out, gain_out, block_out, rows_out = refs[17:26]
    held, held_mlp = refs[26:]
    me = lax.axis_index(Y)
    for r in range(4):
        held[lax.rem(me + 4 - r, 4)] = home[r][...]
        held_mlp[lax.rem(me + 4 - r, 4)] = mlp[r][...]
    for j in range(4):
        columns = slice(960 * j, 960 * j + 960)
        gate_out[:, columns] = held_mlp[j, :, :960].astype(F32)
        up_out[:, columns] = held_mlp[j, :, 1024:1984].astype(F32)
        down_out[:, columns] = held_mlp[j, :, 2048:3008].astype(F32)
        total = held[j].astype(F32)
        query_out[:, 320 * j : 320 * j + 320] = total[:, :320]
        keyval_out[:, 64 * j : 64 * j + 64] = total[:, 320:384]
    total = output_home[0].astype(F32)
    for p in range(1, 16):
        total = total + output_home[p].astype(F32)
    output_out[...] = total

    def products(weight, grad):
        return jnp.sum(weight[...].astype(F32) * grad[...], axis=1, keepdims=True)

    one = products(query_ref, query_out) + products(keyval_ref, keyval_out)
    two = products(gate_ref, gate_out) + products(up_ref, up_out)
    gain_out[:, :128] = jnp.broadcast_to(one, (40, 128))
    gain_out[:, 128:] = jnp.broadcast_to(two, (40, 128))
    at = 80 * lax.axis_index(T)
    for mine, other, out in ((block_mine, block_other, block_out), (rows_mine, rows_other, rows_out)):
        out[pl.ds(pl.multiple_of(at, 16), 80), :] = mine[...]
        out[pl.ds(pl.multiple_of(80 - at, 16), 80), :] = other[...]


def owners(home, mlp, output_home, w_query, keyval_half, w_gate, w_up, block, rows):
    wide, narrow = (jax.ShapeDtypeStruct((40, n), F32) for n in (3840, 1280))
    small = jax.ShapeDtypeStruct((40, 256), F32)
    tokens = jax.ShapeDtypeStruct((160, 2560), BF)
    return pl.pallas_call(
        owners_kernel,
        out_shape=(narrow, small, narrow, wide, wide, wide, small, tokens, tokens),
        scratch_shapes=[pltpu.VMEM((4, 40, 384), BF), pltpu.VMEM((4, 40, 3072), BF)],
        compiler_params=VMEM,
        cost_estimate=FREE,
    )(*home, *mlp, output_home, w_query, keyval_half, w_gate, w_up, *block, *rows)


def turned(values, cosine, sine):
    one, two = values[:, :64], values[:, 64:128]
    return jnp.concatenate(
        [one * cosine - two * sine, two * cosine + one * sine, values[:, 128:]], axis=1
    )


def prepare_kernel(scale, home_ref, cosine_ref, sine_ref, query_ref, kv_ref, wide):
    cosine, sine = cosine_ref[...], sine_ref[...]
    for j in range(4):
        wide[:, 320 * j : 320 * j + 320] = home_ref[j, :, :320].astype(F32)
    for h in range(5):
        head = turned(wide[:, 256 * h : 256 * h + 256], cosine, sine)
        query_ref[h] = (head * scale).astype(BF)
    for j in range(4):
        wide[:, 64 * j : 64 * j + 64] = home_ref[j, :, 320:].astype(F32)
    first = lax.axis_index(T) == 0
    kv = wide[:, :256]
    kv = jnp.where(first, turned(kv, cosine, sine), kv).astype(BF)
    at = 80 * lax.axis_index(T)
    kv_ref[pl.ds(pl.multiple_of(at, 16), 80), :] = kv[:80]
    kv_ref[pl.ds(pl.multiple_of(80 - at, 16), 80), :] = kv[80:]


def prepare(home, cosine, sine, scale):
    return pl.pallas_call(
        functools.partial(prepare_kernel, scale),
        out_shape=(
            jax.ShapeDtypeStruct((5, 160, 256), BF),
            jax.ShapeDtypeStruct((160, 256), BF),
        ),
        scratch_shapes=[pltpu.VMEM((160, 1280), F32)],
        compiler_params=VMEM,
        cost_estimate=FREE,
    )(home, cosine, sine)


def unturn_kernel(scale, grad_ref, cosine_ref, sine_ref, out_ref, wide):
    cosine, sine = cosine_ref[...], -sine_ref[...]
    for h in range(5):
        wide[:, 256 * h : 256 * h + 256] = turned(grad_ref[h] * scale, cosine, sine)
    for j in range(4):
        out_ref[j] = wide[:, 320 * j : 320 * j + 320].astype(BF)


def unturn(grad, cosine, sine, scale):
    return pl.pallas_call(
        functools.partial(unturn_kernel, scale),
        out_shape=jax.ShapeDtypeStruct((4, 160, 320), BF),
        scratch_shapes=[pltpu.VMEM((160, 1280), F32)],
        compiler_params=VMEM,
        cost_estimate=FREE,
    )(grad, cosine, sine)


def unturn_kv_kernel(home_ref, cosine_ref, sine_ref, out_ref, held):
    total = home_ref[0].astype(F32)
    for p in range(1, 16):
        total = total + home_ref[p].astype(F32)
    held[...] = total
    at = 80 * lax.axis_index(T)
    total = jnp.concatenate(
        [held[pl.ds(pl.multiple_of(at, 16), 80), :], held[pl.ds(pl.multiple_of(80 - at, 16), 80), :]]
    )
    back = turned(total, cosine_ref[...], -sine_ref[...])
    total = jnp.where(lax.axis_index(T) == 0, back, total).astype(BF)
    for j in range(4):
        out_ref[j] = total[:, 64 * j : 64 * j + 64]


def unturn_kv(home, cosine, sine):
    return pl.pallas_call(
        unturn_kv_kernel,
        out_shape=jax.ShapeDtypeStruct((4, 160, 64), BF),
        scratch_shapes=[pltpu.VMEM((160, 256), F32)],
        compiler_params=VMEM,
        cost_estimate=FREE,
    )(home, cosine, sine)


def pieces_kernel(home_ref, out_ref):
    total = home_ref[0].astype(F32)
    for p in range(1, 16):
        total = total + home_ref[p].astype(F32)
    out_ref[...] = total.astype(BF)


def pieces_sum(home):
    cols = home.shape[2]
    return pl.pallas_call(
        pieces_kernel,
        grid=(2,),
        in_specs=[pl.BlockSpec((16, 80, cols), lambda i: (0, i, 0))],
        out_specs=pl.BlockSpec((80, cols), lambda i: (i, 0)),
        out_shape=jax.ShapeDtypeStruct((160, cols), BF),
        compiler_params=VMEM,
        cost_estimate=FREE,
    )(home)


def token_order_kernel(x_ref, out_ref):
    for j in range(4):
        for p in range(16):
            to, at = 40 * (16 * j + p), 40 * (4 * p + j)
            out_ref[:, to : to + 40] = x_ref[:, at : at + 40].astype(BF)


def from_piece_order(x):
    return pl.pallas_call(
        token_order_kernel, out_shape=jax.ShapeDtypeStruct(x.shape, BF), compiler_params=VMEM, cost_estimate=FREE
    )(x)


def shards(
    tokens,
    lengths,
    attn_gain,
    w_query,
    w_keyval,
    w_output,
    mlp_gain,
    w_gate,
    w_up,
    w_down,
    cotangent,
):
    t = lax.axis_index(T)
    me = lax.axis_index(Y)
    piece = lax.axis_index(CONTEXT)
    head_dim = 256
    query_scale = head_dim ** (-0.5)
    seq_count = 2560
    padding = seq_count - lengths[0]
    row_start = piece * 160
    turned_index = row_start + (jnp.arange(160, dtype=jnp.int32) + t * 80) % 160
    live_turned = turned_index >= padding
    live_mine = live_turned[:80, None]

    x_low = to_piece_order(lax.dynamic_slice_in_dim(tokens[0], t * 80, 80, 0))
    cot_mine = to_piece_order(lax.dynamic_slice_in_dim(cotangent[0], t * 80, 80, 0))
    grad_mine = jnp.where(live_mine, cot_mine, jnp.zeros_like(cot_mine))
    x_mine = x_low.astype(F32)
    x_blocks = ring_blocks(x_low, Y)
    w_out = lax.all_gather(w_output, PIECES, axis=0, tiled=True)

    keyval_half = lax.dynamic_slice_in_dim(w_keyval, t * 256, 256, 1)
    gains = jnp.concatenate([attn_gain, mlp_gain])[None, :]
    gains = jnp.pad(gains, ((0, 7), (0, 48)))
    attn_blocks = pack_attention(w_query, keyval_half, gains)
    attn_rows = place(to_owners(attn_blocks), Y, sign=-1)
    attn_copies = jnp.broadcast_to(attn_rows[None], (16, 4, 48, 384))
    attn_all = exchange(attn_copies, CONTEXT).reshape(64, 48, 384)
    w_qkv = attn_all[:, :40].reshape(2560, 384)
    gain_one = attn_all[:, 40, :40].reshape(1, 2560).astype(F32)
    gain_two = attn_all[:, 40, 40:80].reshape(1, 2560).astype(F32)
    x_own = place(x_blocks, Y, attn_all)
    x_other = shift(x_own, T, 1)
    mlp_blocks = pack_mlp(w_gate, w_up, w_down)
    mlp_got = to_owners(mlp_blocks)
    mlp_block = place(mlp_got, Y, x_own, sign=-1).reshape(160, 3072)
    w_mlp = lax.all_gather(mlp_block, CONTEXT, axis=0, tiled=True)

    normed, projected = project(x_own, x_other, gain_one, w_qkv)
    home = exchange(projected, Y)
    cosine, sine = angles(turned_index - padding, head_dim)
    queries, kv_own = prepare(home, cosine, sine, query_scale)
    kv_mine = exchange(jnp.broadcast_to(kv_own[None], (16, 160, 256)), CONTEXT).reshape(2560, 256)
    grad_own = place(ring_blocks(after(grad_mine, kv_own), Y), Y).reshape(320, 2560)
    grad_group = jnp.concatenate([grad_own, shift(grad_own, T, 1)])
    kv_mine = after(kv_mine, grad_own)
    kv_other = shift(kv_mine, T, 1)
    keys = jnp.where(t == 0, kv_mine, kv_other)
    values = jnp.where(t == 0, kv_other, kv_mine)

    key_index = jnp.arange(seq_count, dtype=jnp.int32)
    offset = turned_index[:, None] - key_index[None, :]
    allowed = ((offset >= 0) & (offset < WINDOW) & (key_index >= padding)[None, :])[None]
    live = live_turned[None, :, None]
    scores = jnp.einsum("hqd,kd->hqk", queries, keys, preferred_element_type=F32)
    row_top = jnp.max(jnp.where(allowed, scores, NEGATIVE_FILL), axis=-1, keepdims=True)
    row_top = jnp.where(live, row_top, 0.0)
    weights_exp = jnp.where(allowed, jnp.exp(scores - row_top), 0.0)
    row_total = jnp.where(live, jnp.sum(weights_exp, axis=-1, keepdims=True), 1.0)
    prob = weights_exp / row_total
    prob_low = prob.astype(BF)
    attended = jnp.einsum("hqk,kd->qhd", prob_low, values, preferred_element_type=F32)
    attended = attended.reshape(160, 1280).astype(BF)

    branch = dot(attended, w_out, 1, 1)
    hidden_mine = x_mine + branch[:80] + shift(branch[80:], T, 1)

    inverse_two = inverse_root(hidden_mine)
    normed_two_mine = (hidden_mine * inverse_two * gain_two).astype(BF)
    normed_two = jnp.concatenate(gather_rows(after(normed_two_mine, grad_group)))
    hidden, grad_gate, grad_up = feed_forward(normed_two, grad_group, w_mlp)
    attended_group = place(ring_blocks(attended, Y), Y)
    normed_two_low = core_sum(*row_products((grad_gate, grad_up), w_mlp, 0, 1024, attended_group))
    got = own_and_received(normed_two_low, Y, 0)

    gate_up_part = gate_up_grads(normed_two, grad_gate, grad_up, normed_two_low)
    mlp_part = down_grads(grad_group, hidden, gate_up_part, *got)
    mlp_sum = lax.psum_scatter(mlp_part, CONTEXT, scatter_dimension=0, tiled=True)
    grad_normed_two = sum(block.astype(F32) for block in got)

    grad_h_mine = grad_mine.astype(F32) + norm_back(
        grad_normed_two, hidden_mine, inverse_two, gain_two
    )
    branch_mine = grad_h_mine.astype(BF)
    branch_own = place(to_owners(feature_quarters(grad_h_mine)), Y, sign=-1).reshape(320, 640)
    branch_other = shift(branch_own, T, 1)
    branch_low = jnp.concatenate([branch_mine, shift(branch_mine, T, 1)])
    grad_attended = dot(branch_low, w_out, 1, 0).astype(BF).reshape(160, 5, head_dim)

    grad_prob = jnp.einsum("qhd,kd->hqk", grad_attended, values, preferred_element_type=F32)
    spread = jnp.sum(prob * grad_prob, axis=-1, keepdims=True)
    grad_scores = (prob * (grad_prob - spread)).astype(BF)
    grad_keys = jnp.einsum("hqk,hqd->kd", grad_scores, queries, preferred_element_type=F32)
    grad_values = jnp.einsum("hqk,qhd->kd", prob_low, grad_attended, preferred_element_type=F32)
    keep = jnp.where(t == 0, grad_keys, grad_values)
    give = jnp.where(t == 0, grad_values, grad_keys).astype(BF)
    grad_queries = jnp.einsum("hqk,kd->hqd", grad_scores, keys, preferred_element_type=F32)
    query_blocks = unturn(grad_queries, cosine, sine, query_scale)
    kv_part = (keep + shift(give, T, 1).astype(F32)).astype(BF).reshape(16, 160, 256)
    kv_part = after(kv_part, query_blocks)
    kv_home = exchange(kv_part, CONTEXT)
    grad_query_group = columns_out(query_blocks)
    output_part = outer_output(branch_own, branch_other, attended_group)
    output_home = exchange(after(output_part, kv_home), CONTEXT)
    mlp_rows = row_products((hidden,), w_mlp, 2, 1024, output_part)
    kv_home = after(kv_home, output_part, *mlp_rows)
    grad_kv_group = columns_out(unturn_kv(kv_home, cosine, sine))
    grad_qkv = jnp.concatenate([grad_query_group, grad_kv_group], axis=1)
    normed_low = core_sum(*row_products((grad_qkv,), w_qkv, 0, 384))
    part_home = exchange(after(outer(normed, grad_qkv), output_home), CONTEXT)
    (grad_normed,) = sums((own_and_received(normed_low, Y, 0),), (F32,))
    (mlp_mine,) = sums((own_and_received(after(core_sum(*mlp_rows), normed_low), Y, 0),), (F32,))
    inverse_one = inverse_root(x_mine)
    tokens_mine = from_piece_order(
        grad_h_mine + norm_back(grad_normed, x_mine, inverse_one, gain_one)
    )
    block_mine = from_piece_order(jnp.where(live_mine, hidden_mine + mlp_mine, 0.0))
    mlp_home = to_owners(mlp_sum)
    home = to_owners(pieces_sum(part_home))
    query_grad, kv_half, output_grad, gate_grad, up_grad, down_grad, gain_part, block_out, tokens_grad = owners(
        home,
        mlp_home,
        output_home,
        w_query,
        keyval_half,
        w_gate,
        w_up,
        (block_mine, shift(block_mine, T, 1)),
        (tokens_mine, shift(tokens_mine, T, 1)),
    )

    mine = jnp.concatenate([kv_half, gain_part], axis=1)
    other = shift(mine, T, 1)
    kv_other = other[:, :256]
    keyval_grad = jnp.where(
        t == 0,
        jnp.concatenate([kv_half, kv_other], axis=1),
        jnp.concatenate([kv_other, kv_half], axis=1),
    )
    attn_gain_grad = (mine[:, 256] + other[:, 256]) / attn_gain.astype(F32)
    mlp_gain_grad = (mine[:, 384] + other[:, 384]) / mlp_gain.astype(F32)

    return (
        block_out[None],
        tokens_grad[None],
        attn_gain_grad,
        query_grad,
        keyval_grad,
        output_grad,
        mlp_gain_grad,
        gate_grad,
        up_grad,
        down_grad,
    )


def solution(mesh):
    torus = Mesh(
        mesh.devices.reshape(mesh.shape["shard"], 4, 4, mesh.shape["tensor"]),
        ("shard", "context_0", "context_1", "tensor"),
    )
    in_specs = (
        P("shard", CONTEXT, None),
        P("shard"),
        P(SHARD_CONTEXT),
        P(SHARD_CONTEXT, "tensor"),
        P(SHARD_CONTEXT, None),
        P(SHARD_CONTEXT, "tensor"),
        P(SHARD_CONTEXT),
        P(SHARD_CONTEXT, "tensor"),
        P(SHARD_CONTEXT, "tensor"),
        P(SHARD_CONTEXT, "tensor"),
        P("shard", CONTEXT, None),
    )
    out_specs = (
        P("shard", CONTEXT, None),
        P("shard", CONTEXT, None),
        P(SHARD_CONTEXT),
        P(SHARD_CONTEXT, "tensor"),
        P(SHARD_CONTEXT, None),
        P(SHARD_CONTEXT, "tensor"),
        P(SHARD_CONTEXT),
        P(SHARD_CONTEXT, "tensor"),
        P(SHARD_CONTEXT, "tensor"),
        P(SHARD_CONTEXT, "tensor"),
    )
    return jax.shard_map(
        shards, mesh=torus, in_specs=in_specs, out_specs=out_specs, check_vma=False
    )
```

```python
import functools

import jax
import jax.numpy as jnp
from jax import lax
from jax.experimental import pallas as pl
from jax.experimental.pallas import tpu as pltpu
from jax.sharding import Mesh
from jax.sharding import PartitionSpec as P

WINDOW = 2048
SHARD_CONTEXT = ("shard", "context_0", "context_1")
CONTEXT = ("context_0", "context_1")
PIECES = ("context_0", "context_1", "shard")
Y, X, Z, T = "shard", "context_0", "context_1", "tensor"
VMEM = pltpu.CompilerParams(vmem_limit_bytes=48 * 2**20)
ANYWHERE = pl.BlockSpec(memory_space=pl.ANY)
FREE = pl.CostEstimate(flops=0, bytes_accessed=0, transcendentals=0)

EPSILON = 1e-06
NEGATIVE_FILL = -1e30
BF = jnp.bfloat16
F32 = jnp.float32


def shift(x, axis, by):
    n = lax.axis_size(axis)
    return lax.ppermute(x, axis, [(i, (i + by) % n) for i in range(n)])


def exchange(blocks, axis):
    return lax.all_to_all(blocks, axis, 0, 0, tiled=True)


def nothing(*refs):
    pass


def after(x, *others):
    return pl.pallas_call(
        nothing,
        out_shape=jax.ShapeDtypeStruct(x.shape, x.dtype),
        in_specs=[ANYWHERE] * (1 + len(others)),
        out_specs=ANYWHERE,
        input_output_aliases={0: 0},
        compiler_params=VMEM,
        cost_estimate=FREE,
    )(x, *others)


def small_trip(x, *others):
    corner = x.reshape(-1, x.shape[-1])[:8, :128]
    return shift(after(corner, *others) if others else corner, T, 1)


def ring_blocks(x, axis):
    return [x, shift(x, axis, -1), shift(x, axis, 2), shift(x, axis, 1)]


def place_kernel(axis, sign, *refs):
    blocks, out = refs[:4], refs[-1]
    me = lax.axis_index(axis)
    for r, block in enumerate(blocks):
        out[lax.rem(me + (sign * r) % 4, 4)] = block[...]


def place(blocks, axis, *first, sign=1):
    whole = pl.BlockSpec(memory_space=pltpu.VMEM)
    return pl.pallas_call(
        functools.partial(place_kernel, axis, sign),
        out_shape=jax.ShapeDtypeStruct((4, *blocks[0].shape), blocks[0].dtype),
        in_specs=[whole] * 4 + [ANYWHERE] * len(first),
        out_specs=whole,
        compiler_params=VMEM,
        cost_estimate=FREE,
    )(*blocks, *first)


def gather_rows(mine, *first):
    own = place(ring_blocks(mine, Y), Y, *first).reshape(320, -1)
    return own, shift(own, T, 1)


def rows_kernel(count, *refs):
    lefts, rights, (far_ref, near_ref) = refs[:count], refs[count : 2 * count], refs[-2:]
    total = dot(lefts[0][...], rights[0][...], 1, 1)
    for left, right in zip(lefts[1:], rights[1:]):
        total = total + dot(left[...], right[...], 1, 1)
    near_ref[...] = total[:320].astype(BF)
    far_ref[...] = total[320:].astype(BF)


def row_products(lefts, weight, at, width, *first):
    rows, count, n = 512, len(lefts), weight.shape[0]
    half = jax.ShapeDtypeStruct((320, n), BF)
    return pl.pallas_call(
        functools.partial(rows_kernel, count),
        grid=(n // rows,),
        out_shape=(half, half),
        in_specs=[pl.BlockSpec((640, width), lambda i: (0, 0))] * count
        + [pl.BlockSpec((rows, width), lambda i, j=j: (i, at + j)) for j in range(count)]
        + [ANYWHERE] * len(first),
        out_specs=(pl.BlockSpec((320, rows), lambda i: (0, i)),) * 2,
        compiler_params=VMEM,
        cost_estimate=FREE,
    )(*lefts, *[weight] * count, *first)


def core_sum(far, near):
    return (near.astype(F32) + shift(far, T, 1).astype(F32)).astype(BF).reshape(4, 80, -1)


def own_and_received(parts, axis, dim):
    me = lax.axis_index(axis)
    own, *rest = [
        lax.dynamic_index_in_dim(parts, (me + r) % 4, dim, keepdims=False) for r in range(4)
    ]
    return [own] + [shift(rest[r - 1], axis, r) for r in (1, 3, 2)]


def sums_kernel(kinds, *refs):
    for i, out in enumerate(refs[4 * len(kinds) :]):
        total = refs[4 * i][...].astype(F32)
        for ref in refs[4 * i + 1 : 4 * i + 4]:
            total = total + ref[...].astype(F32)
        out[...] = total.astype(kinds[i])


def sums(groups, kinds):
    return pl.pallas_call(
        functools.partial(sums_kernel, kinds),
        out_shape=tuple(jax.ShapeDtypeStruct(g[0].shape, k) for g, k in zip(groups, kinds)),
        compiler_params=VMEM,
        cost_estimate=FREE,
    )(*[block for group in groups for block in group])


def outer_kernel(x_ref, g_ref, out_ref):
    out_ref[...] = dot(x_ref[...], g_ref[...], 0, 0).astype(BF).reshape(4, 160, g_ref.shape[1])


def outer(x, g):
    cols = g.shape[1]
    return pl.pallas_call(
        outer_kernel,
        grid=(4,),
        out_shape=jax.ShapeDtypeStruct((16, 160, cols), BF),
        in_specs=[
            pl.BlockSpec((640, 640), lambda i: (0, i)),
            pl.BlockSpec((640, cols), lambda i: (0, 0)),
        ],
        out_specs=pl.BlockSpec((4, 160, cols), lambda i: (i, 0, 0)),
        compiler_params=VMEM,
        cost_estimate=FREE,
    )(x, g)


def outer_output_kernel(own_ref, other_ref, ob_ref, out_ref):
    cols = ob_ref.shape[2]
    part = dot(own_ref[...], ob_ref[:, :80].reshape(320, cols), 0, 0)
    part = part + dot(other_ref[...], ob_ref[:, 80:].reshape(320, cols), 0, 0)
    out_ref[...] = part.reshape(16, 40, cols).astype(BF)


def outer_output(own, other, ob):
    cols = 640
    half = pl.BlockSpec((320, 640), lambda i: (0, 0))
    return pl.pallas_call(
        outer_output_kernel,
        grid=(2,),
        out_shape=jax.ShapeDtypeStruct((16, 40, 1280), BF),
        in_specs=[half, half, pl.BlockSpec((4, 160, cols), lambda i: (0, 0, i))],
        out_specs=pl.BlockSpec((16, 40, cols), lambda i: (0, 0, i)),
        compiler_params=VMEM,
        cost_estimate=FREE,
    )(own, other, ob)


def to_owners(sums):
    me = lax.axis_index(Y)
    rows = sums.reshape(4, -1, sums.shape[-1])
    got = []
    for r in range(4):
        block = lax.dynamic_index_in_dim(rows, (me + r) % 4, 0, keepdims=False)
        got.append(shift(block, Y, r) if r else block)
    return got


def by_half(blocks):
    cols = blocks.shape[2]
    return blocks.reshape(4, 2, 80, cols).swapaxes(0, 1).reshape(640, cols)


def columns_out(blocks):
    me = lax.axis_index(Y)
    got = []
    for r in range(4):
        block = lax.dynamic_index_in_dim(blocks, (me + r) % 4, 0, keepdims=False)
        got.append(shift(block, Y, r) if r else block)
    return by_half(place(got, Y, sign=-1))


def quarters(x):
    rows = x.shape[0]
    return x.reshape(rows, 4, -1).swapaxes(0, 1)


def pack_attention_kernel(q_ref, kv_ref, gains_ref, attn_ref):
    attn_ref[...] = jnp.zeros_like(attn_ref)
    for j in range(4):
        attn_ref[j, :40, :320] = q_ref[:, 320 * j : 320 * j + 320]
        attn_ref[j, :40, 320:] = kv_ref[:, 64 * j : 64 * j + 64]
        attn_ref[j, 40:48, :128] = gains_ref[...]


def pack_attention(w_query, keyval_half, gains):
    return pl.pallas_call(
        pack_attention_kernel,
        out_shape=jax.ShapeDtypeStruct((4, 48, 384), BF),
        compiler_params=VMEM,
        cost_estimate=FREE,
    )(w_query, keyval_half, gains)


def pack_mlp_kernel(gate_ref, up_ref, down_ref, mlp_ref):
    mlp_ref[...] = jnp.zeros_like(mlp_ref)
    for j in range(4):
        mlp_ref[j, :, :960] = gate_ref[:, 960 * j : 960 * j + 960]
        mlp_ref[j, :, 1024:1984] = up_ref[:, 960 * j : 960 * j + 960]
        mlp_ref[j, :, 2048:3008] = down_ref[:, 960 * j : 960 * j + 960]


def pack_mlp(w_gate, w_up, w_down):
    return pl.pallas_call(
        pack_mlp_kernel,
        out_shape=jax.ShapeDtypeStruct((4, 40, 3072), BF),
        compiler_params=VMEM,
        cost_estimate=FREE,
    )(w_gate, w_up, w_down)


def gate_up_grad_kernel(x_ref, gate_ref, up_ref, *rest):
    out_ref = rest[-1]
    out_ref[:, :1024] = dot(x_ref[...], gate_ref[...], 0, 0).astype(BF)
    out_ref[:, 1024:] = dot(x_ref[...], up_ref[...], 0, 0).astype(BF)


def gate_up_grads(normed, gate, up, *first):
    rows = 512
    whole = pl.BlockSpec((640, 1024), lambda i: (0, 0))
    return pl.pallas_call(
        gate_up_grad_kernel,
        grid=(2560 // rows,),
        out_shape=jax.ShapeDtypeStruct((2560, 3072), BF),
        in_specs=[pl.BlockSpec((640, rows), lambda i: (0, i)), whole, whole]
        + [ANYWHERE] * len(first),
        out_specs=pl.BlockSpec((rows, 2048), lambda i: (i, 0)),
        compiler_params=VMEM,
        cost_estimate=FREE,
    )(normed, gate, up, *first)


def down_grad_kernel(y_ref, hidden_ref, *rest):
    rest[-1][...] = dot(y_ref[...], hidden_ref[...], 0, 0).astype(BF)


def down_grads(grads, hidden, held, *first):
    rows = 512
    return pl.pallas_call(
        down_grad_kernel,
        grid=(2560 // rows,),
        out_shape=jax.ShapeDtypeStruct((2560, 3072), BF),
        in_specs=[
            pl.BlockSpec((640, rows), lambda i: (0, i)),
            pl.BlockSpec((640, 1024), lambda i: (0, 0)),
        ]
        + [ANYWHERE] * (1 + len(first)),
        out_specs=pl.BlockSpec((rows, 1024), lambda i: (i, 2)),
        input_output_aliases={2: 0},
        compiler_params=VMEM,
        cost_estimate=FREE,
    )(grads, hidden, held, *first)


def feed_forward_kernel(x_ref, y_ref, gate_ref, up_ref, down_ref, *rest):
    hidden_out, gate_out, up_out = rest[-3:]
    gate = dot(x_ref[...], gate_ref[...], 1, 0)
    up = dot(x_ref[...], up_ref[...], 1, 0)
    grad = dot(y_ref[...], down_ref[...], 1, 0)
    scale = 0.7978845608028654
    square = gate * gate
    bent = jnp.tanh(scale * gate * (1.0 + 0.044715 * square))
    share = 0.5 * (1.0 + bent)
    slope = share + 0.5 * gate * (1.0 - bent * bent) * scale * (1.0 + 0.134145 * square)
    active = gate * share
    hidden_out[...] = (active * up).astype(BF)
    gate_out[...] = (grad * up * slope).astype(BF)
    up_out[...] = (grad * active).astype(BF)


def feed_forward(x, y, w_mlp, *first):
    cols = 256
    steps = 1024 // cols
    part = jax.ShapeDtypeStruct((640, 1024), BF)
    whole = pl.BlockSpec((640, 2560), lambda j: (0, 0))
    out = pl.BlockSpec((640, cols), lambda j: (0, j))
    return pl.pallas_call(
        feed_forward_kernel,
        grid=(steps,),
        out_shape=(part, part, part),
        in_specs=[whole, whole]
        + [pl.BlockSpec((2560, cols), lambda j, k=k: (0, k * steps + j)) for k in range(3)]
        + [ANYWHERE] * len(first),
        out_specs=(out, out, out),
        compiler_params=VMEM,
        cost_estimate=FREE,
    )(x, y, w_mlp, w_mlp, w_mlp, *first)


def to_piece_order(x):
    rows = x.shape[0]
    return x.reshape(rows, 4, 16, 40).swapaxes(1, 2).reshape(rows, 2560)


def inverse_root(values):
    return lax.rsqrt(jnp.mean(values * values, axis=-1, keepdims=True) + EPSILON)


def norm_back(grad, values, inverse, gain):
    scaled = gain * grad
    return inverse * scaled - values * inverse**3 * jnp.mean(
        scaled * values, axis=-1, keepdims=True
    )


def angles(position, head_dim):
    quarter = head_dim // 4
    frequency = 10000.0 ** (-jnp.arange(quarter, dtype=F32) / quarter)
    phase_angle = position[:, None].astype(F32) * frequency[None, :]
    return (jnp.cos(phase_angle), jnp.sin(phase_angle))


def dot(a, b, da, db):
    return lax.dot_general(a, b, (((da,), (db,)), ((), ())), preferred_element_type=F32)


def feature_quarters_kernel(x_ref, out_ref):
    for j in range(4):
        for p in range(16):
            at = 40 * (4 * p + j)
            out_ref[j, :, 40 * p : 40 * p + 40] = x_ref[:, at : at + 40].astype(BF)


def feature_quarters(x):
    return pl.pallas_call(
        feature_quarters_kernel,
        out_shape=jax.ShapeDtypeStruct((4, 80, 640), BF),
        compiler_params=VMEM,
        cost_estimate=FREE,
    )(x)


def project_kernel(own_ref, other_ref, gain_ref, weight_ref, normed_ref, out_ref):
    x = jnp.concatenate([own_ref[0], other_ref[0]]).astype(F32)
    normed = (x * inverse_root(x) * gain_ref[...]).astype(BF)
    normed_ref[0] = normed[:80]
    normed_ref[1] = normed[80:]
    out_ref[0] = dot(normed, weight_ref[...], 1, 0).astype(BF)


def project(own, other, gain, weight):
    rows = pl.BlockSpec((1, 80, 2560), lambda i: (i, 0, 0))
    normed, out = pl.pallas_call(
        project_kernel,
        grid=(4,),
        out_shape=(
            jax.ShapeDtypeStruct((2, 320, 2560), BF),
            jax.ShapeDtypeStruct((4, 160, 384), BF),
        ),
        in_specs=[
            rows,
            rows,
            pl.BlockSpec((1, 2560), lambda i: (0, 0)),
            pl.BlockSpec((2560, 384), lambda i: (0, 0)),
        ],
        out_specs=(
            pl.BlockSpec((2, 80, 2560), lambda i: (0, i, 0)),
            pl.BlockSpec((1, 160, 384), lambda i: (i, 0, 0)),
        ),
        compiler_params=VMEM,
        cost_estimate=FREE,
    )(own, other, gain, weight)
    return normed.reshape(640, 2560), out


def owners_kernel(*refs):
    home, mlp = refs[:4], refs[4:8]
    output_home, query_ref, keyval_ref, gate_ref, up_ref, block_mine, block_other, rows_mine, rows_other = refs[8:17]
    query_out, keyval_out, output_out, gate_out, up_out, down_out, gain_out, block_out, rows_out = refs[17:26]
    held, held_mlp = refs[26:]
    me = lax.axis_index(Y)
    for r in range(4):
        held[lax.rem(me + 4 - r, 4)] = home[r][...]
        held_mlp[lax.rem(me + 4 - r, 4)] = mlp[r][...]
    for j in range(4):
        columns = slice(960 * j, 960 * j + 960)
        gate_out[:, columns] = held_mlp[j, :, :960].astype(F32)
        up_out[:, columns] = held_mlp[j, :, 1024:1984].astype(F32)
        down_out[:, columns] = held_mlp[j, :, 2048:3008].astype(F32)
        total = held[j].astype(F32)
        query_out[:, 320 * j : 320 * j + 320] = total[:, :320]
        keyval_out[:, 64 * j : 64 * j + 64] = total[:, 320:384]
    total = output_home[0].astype(F32)
    for p in range(1, 16):
        total = total + output_home[p].astype(F32)
    output_out[...] = total

    def products(weight, grad):
        return jnp.sum(weight[...].astype(F32) * grad[...], axis=1, keepdims=True)

    one = products(query_ref, query_out) + products(keyval_ref, keyval_out)
    two = products(gate_ref, gate_out) + products(up_ref, up_out)
    gain_out[:, :128] = jnp.broadcast_to(one, (40, 128))
    gain_out[:, 128:] = jnp.broadcast_to(two, (40, 128))
    at = 80 * lax.axis_index(T)
    for mine, other, out in ((block_mine, block_other, block_out), (rows_mine, rows_other, rows_out)):
        out[pl.ds(pl.multiple_of(at, 16), 80), :] = mine[...]
        out[pl.ds(pl.multiple_of(80 - at, 16), 80), :] = other[...]


def owners(home, mlp, output_home, w_query, keyval_half, w_gate, w_up, block, rows):
    wide, narrow = (jax.ShapeDtypeStruct((40, n), F32) for n in (3840, 1280))
    small = jax.ShapeDtypeStruct((40, 256), F32)
    tokens = jax.ShapeDtypeStruct((160, 2560), BF)
    return pl.pallas_call(
        owners_kernel,
        out_shape=(narrow, small, narrow, wide, wide, wide, small, tokens, tokens),
        scratch_shapes=[pltpu.VMEM((4, 40, 384), BF), pltpu.VMEM((4, 40, 3072), BF)],
        compiler_params=VMEM,
        cost_estimate=FREE,
    )(*home, *mlp, output_home, w_query, keyval_half, w_gate, w_up, *block, *rows)


def turned(values, cosine, sine):
    one, two = values[:, :64], values[:, 64:128]
    return jnp.concatenate(
        [one * cosine - two * sine, two * cosine + one * sine, values[:, 128:]], axis=1
    )


def prepare_kernel(scale, home_ref, cosine_ref, sine_ref, query_ref, kv_ref, wide):
    cosine, sine = cosine_ref[...], sine_ref[...]
    for j in range(4):
        wide[:, 320 * j : 320 * j + 320] = home_ref[j, :, :320].astype(F32)
    for h in range(5):
        head = turned(wide[:, 256 * h : 256 * h + 256], cosine, sine)
        query_ref[h] = (head * scale).astype(BF)
    for j in range(4):
        wide[:, 64 * j : 64 * j + 64] = home_ref[j, :, 320:].astype(F32)
    first = lax.axis_index(T) == 0
    kv = wide[:, :256]
    kv = jnp.where(first, turned(kv, cosine, sine), kv).astype(BF)
    at = 80 * lax.axis_index(T)
    kv_ref[pl.ds(pl.multiple_of(at, 16), 80), :] = kv[:80]
    kv_ref[pl.ds(pl.multiple_of(80 - at, 16), 80), :] = kv[80:]


def prepare(home, cosine, sine, scale):
    return pl.pallas_call(
        functools.partial(prepare_kernel, scale),
        out_shape=(
            jax.ShapeDtypeStruct((5, 160, 256), BF),
            jax.ShapeDtypeStruct((160, 256), BF),
        ),
        scratch_shapes=[pltpu.VMEM((160, 1280), F32)],
        compiler_params=VMEM,
        cost_estimate=FREE,
    )(home, cosine, sine)


def unturn_kernel(scale, grad_ref, cosine_ref, sine_ref, out_ref, wide):
    cosine, sine = cosine_ref[...], -sine_ref[...]
    for h in range(5):
        wide[:, 256 * h : 256 * h + 256] = turned(grad_ref[h] * scale, cosine, sine)
    for j in range(4):
        out_ref[j] = wide[:, 320 * j : 320 * j + 320].astype(BF)


def unturn(grad, cosine, sine, scale):
    return pl.pallas_call(
        functools.partial(unturn_kernel, scale),
        out_shape=jax.ShapeDtypeStruct((4, 160, 320), BF),
        scratch_shapes=[pltpu.VMEM((160, 1280), F32)],
        compiler_params=VMEM,
        cost_estimate=FREE,
    )(grad, cosine, sine)


def unturn_kv_kernel(home_ref, cosine_ref, sine_ref, out_ref, held):
    total = home_ref[0].astype(F32)
    for p in range(1, 16):
        total = total + home_ref[p].astype(F32)
    held[...] = total
    at = 80 * lax.axis_index(T)
    total = jnp.concatenate(
        [held[pl.ds(pl.multiple_of(at, 16), 80), :], held[pl.ds(pl.multiple_of(80 - at, 16), 80), :]]
    )
    back = turned(total, cosine_ref[...], -sine_ref[...])
    total = jnp.where(lax.axis_index(T) == 0, back, total).astype(BF)
    for j in range(4):
        out_ref[j] = total[:, 64 * j : 64 * j + 64]


def unturn_kv(home, cosine, sine):
    return pl.pallas_call(
        unturn_kv_kernel,
        out_shape=jax.ShapeDtypeStruct((4, 160, 64), BF),
        scratch_shapes=[pltpu.VMEM((160, 256), F32)],
        compiler_params=VMEM,
        cost_estimate=FREE,
    )(home, cosine, sine)


def pieces_kernel(home_ref, out_ref):
    total = home_ref[0].astype(F32)
    for p in range(1, 16):
        total = total + home_ref[p].astype(F32)
    out_ref[...] = total.astype(BF)


def pieces_sum(home):
    cols = home.shape[2]
    return pl.pallas_call(
        pieces_kernel,
        grid=(2,),
        in_specs=[pl.BlockSpec((16, 80, cols), lambda i: (0, i, 0))],
        out_specs=pl.BlockSpec((80, cols), lambda i: (i, 0)),
        out_shape=jax.ShapeDtypeStruct((160, cols), BF),
        compiler_params=VMEM,
        cost_estimate=FREE,
    )(home)


def token_order_kernel(x_ref, out_ref):
    for j in range(4):
        for p in range(16):
            to, at = 40 * (16 * j + p), 40 * (4 * p + j)
            out_ref[:, to : to + 40] = x_ref[:, at : at + 40].astype(BF)


def from_piece_order(x):
    return pl.pallas_call(
        token_order_kernel, out_shape=jax.ShapeDtypeStruct(x.shape, BF), compiler_params=VMEM, cost_estimate=FREE
    )(x)


def shards(
    tokens,
    lengths,
    attn_gain,
    w_query,
    w_keyval,
    w_output,
    mlp_gain,
    w_gate,
    w_up,
    w_down,
    cotangent,
):
    t = lax.axis_index(T)
    me = lax.axis_index(Y)
    piece = lax.axis_index(CONTEXT)
    head_dim = 256
    query_scale = head_dim ** (-0.5)
    seq_count = 2560
    padding = seq_count - lengths[0]
    row_start = piece * 160
    turned_index = row_start + (jnp.arange(160, dtype=jnp.int32) + t * 80) % 160
    live_turned = turned_index >= padding
    live_mine = live_turned[:80, None]

    x_low = to_piece_order(lax.dynamic_slice_in_dim(tokens[0], t * 80, 80, 0))
    cot_mine = to_piece_order(lax.dynamic_slice_in_dim(cotangent[0], t * 80, 80, 0))
    grad_mine = jnp.where(live_mine, cot_mine, jnp.zeros_like(cot_mine))
    x_mine = x_low.astype(F32)
    x_blocks = ring_blocks(x_low, Y)
    w_out = lax.all_gather(w_output, PIECES, axis=0, tiled=True)

    keyval_half = lax.dynamic_slice_in_dim(w_keyval, t * 256, 256, 1)
    gains = jnp.concatenate([attn_gain, mlp_gain])[None, :]
    gains = jnp.pad(gains, ((0, 7), (0, 48)))
    attn_blocks = pack_attention(w_query, keyval_half, gains)
    attn_rows = place(to_owners(attn_blocks), Y, sign=-1)
    attn_copies = jnp.broadcast_to(attn_rows[None], (16, 4, 48, 384))
    attn_all = exchange(attn_copies, CONTEXT).reshape(64, 48, 384)
    w_qkv = attn_all[:, :40].reshape(2560, 384)
    gain_one = attn_all[:, 40, :40].reshape(1, 2560).astype(F32)
    gain_two = attn_all[:, 40, 40:80].reshape(1, 2560).astype(F32)
    x_own = place(x_blocks, Y, attn_all)
    x_other = shift(x_own, T, 1)
    mlp_blocks = pack_mlp(w_gate, w_up, w_down)
    mlp_got = to_owners(mlp_blocks)

    normed, projected = project(x_own, x_other, gain_one, w_qkv)
    home = exchange(projected, Y)
    mlp_block = place(mlp_got, Y, home, sign=-1).reshape(160, 3072)
    w_mlp = lax.all_gather(mlp_block, CONTEXT, axis=0, tiled=True)
    cosine, sine = angles(turned_index - padding, head_dim)
    queries, kv_own = prepare(home, cosine, sine, query_scale)
    kv_mine = exchange(jnp.broadcast_to(kv_own[None], (16, 160, 256)), CONTEXT).reshape(2560, 256)
    grad_own = place(ring_blocks(after(grad_mine, kv_own), Y), Y).reshape(320, 2560)
    grad_group = jnp.concatenate([grad_own, shift(grad_own, T, 1)])
    kv_mine = after(kv_mine, grad_own)
    kv_other = shift(kv_mine, T, 1)
    keys = jnp.where(t == 0, kv_mine, kv_other)
    values = jnp.where(t == 0, kv_other, kv_mine)

    key_index = jnp.arange(seq_count, dtype=jnp.int32)
    offset = turned_index[:, None] - key_index[None, :]
    allowed = ((offset >= 0) & (offset < WINDOW) & (key_index >= padding)[None, :])[None]
    live = live_turned[None, :, None]
    scores = jnp.einsum("hqd,kd->hqk", queries, keys, preferred_element_type=F32)
    row_top = jnp.max(jnp.where(allowed, scores, NEGATIVE_FILL), axis=-1, keepdims=True)
    row_top = jnp.where(live, row_top, 0.0)
    weights_exp = jnp.where(allowed, jnp.exp(scores - row_top), 0.0)
    row_total = jnp.where(live, jnp.sum(weights_exp, axis=-1, keepdims=True), 1.0)
    prob = weights_exp / row_total
    prob_low = prob.astype(BF)
    attended = jnp.einsum("hqk,kd->qhd", prob_low, values, preferred_element_type=F32)
    attended = attended.reshape(160, 1280).astype(BF)

    branch = dot(attended, w_out, 1, 1)
    hidden_mine = x_mine + branch[:80] + shift(branch[80:], T, 1)

    inverse_two = inverse_root(hidden_mine)
    normed_two_mine = (hidden_mine * inverse_two * gain_two).astype(BF)
    normed_two = jnp.concatenate(gather_rows(after(normed_two_mine, grad_group)))
    hidden, grad_gate, grad_up = feed_forward(normed_two, grad_group, w_mlp)
    attended_group = place(ring_blocks(attended, Y), Y)
    normed_two_low = core_sum(*row_products((grad_gate, grad_up), w_mlp, 0, 1024, attended_group))
    got = own_and_received(normed_two_low, Y, 0)

    gate_up_part = gate_up_grads(normed_two, grad_gate, grad_up, normed_two_low)
    mlp_part = down_grads(grad_group, hidden, gate_up_part, *got)
    mlp_sum = lax.psum_scatter(mlp_part, CONTEXT, scatter_dimension=0, tiled=True)
    grad_normed_two = sum(block.astype(F32) for block in got)

    grad_h_mine = grad_mine.astype(F32) + norm_back(
        grad_normed_two, hidden_mine, inverse_two, gain_two
    )
    branch_mine = grad_h_mine.astype(BF)
    branch_own = place(to_owners(feature_quarters(grad_h_mine)), Y, sign=-1).reshape(320, 640)
    branch_other = shift(branch_own, T, 1)
    branch_low = jnp.concatenate([branch_mine, shift(branch_mine, T, 1)])
    grad_attended = dot(branch_low, w_out, 1, 0).astype(BF).reshape(160, 5, head_dim)

    grad_prob = jnp.einsum("qhd,kd->hqk", grad_attended, values, preferred_element_type=F32)
    spread = jnp.sum(prob * grad_prob, axis=-1, keepdims=True)
    grad_scores = (prob * (grad_prob - spread)).astype(BF)
    grad_keys = jnp.einsum("hqk,hqd->kd", grad_scores, queries, preferred_element_type=F32)
    grad_values = jnp.einsum("hqk,qhd->kd", prob_low, grad_attended, preferred_element_type=F32)
    keep = jnp.where(t == 0, grad_keys, grad_values)
    give = jnp.where(t == 0, grad_values, grad_keys).astype(BF)
    grad_queries = jnp.einsum("hqk,kd->hqd", grad_scores, keys, preferred_element_type=F32)
    query_blocks = unturn(grad_queries, cosine, sine, query_scale)
    kv_part = (keep + shift(give, T, 1).astype(F32)).astype(BF).reshape(16, 160, 256)
    kv_part = after(kv_part, query_blocks)
    kv_home = exchange(kv_part, CONTEXT)
    grad_query_group = columns_out(query_blocks)
    output_part = outer_output(branch_own, branch_other, attended_group)
    output_home = exchange(after(output_part, kv_home), CONTEXT)
    mlp_rows = row_products((hidden,), w_mlp, 2, 1024, output_part)
    kv_home = after(kv_home, output_part, *mlp_rows)
    grad_kv_group = columns_out(unturn_kv(kv_home, cosine, sine))
    grad_qkv = jnp.concatenate([grad_query_group, grad_kv_group], axis=1)
    normed_low = core_sum(*row_products((grad_qkv,), w_qkv, 0, 384))
    part_home = exchange(after(outer(normed, grad_qkv), output_home), CONTEXT)
    (grad_normed,) = sums((own_and_received(normed_low, Y, 0),), (F32,))
    (mlp_mine,) = sums((own_and_received(after(core_sum(*mlp_rows), normed_low), Y, 0),), (F32,))
    inverse_one = inverse_root(x_mine)
    tokens_mine = from_piece_order(
        grad_h_mine + norm_back(grad_normed, x_mine, inverse_one, gain_one)
    )
    block_mine = from_piece_order(jnp.where(live_mine, hidden_mine + mlp_mine, 0.0))
    mlp_home = to_owners(mlp_sum)
    home = to_owners(pieces_sum(part_home))
    query_grad, kv_half, output_grad, gate_grad, up_grad, down_grad, gain_part, block_out, tokens_grad = owners(
        home,
        mlp_home,
        output_home,
        w_query,
        keyval_half,
        w_gate,
        w_up,
        (block_mine, shift(block_mine, T, 1)),
        (tokens_mine, shift(tokens_mine, T, 1)),
    )

    mine = jnp.concatenate([kv_half, gain_part], axis=1)
    other = shift(mine, T, 1)
    kv_other = other[:, :256]
    keyval_grad = jnp.where(
        t == 0,
        jnp.concatenate([kv_half, kv_other], axis=1),
        jnp.concatenate([kv_other, kv_half], axis=1),
    )
    attn_gain_grad = (mine[:, 256] + other[:, 256]) / attn_gain.astype(F32)
    mlp_gain_grad = (mine[:, 384] + other[:, 384]) / mlp_gain.astype(F32)

    return (
        block_out[None],
        tokens_grad[None],
        attn_gain_grad,
        query_grad,
        keyval_grad,
        output_grad,
        mlp_gain_grad,
        gate_grad,
        up_grad,
        down_grad,
    )


def solution(mesh):
    torus = Mesh(
        mesh.devices.reshape(mesh.shape["shard"], 4, 4, mesh.shape["tensor"]),
        ("shard", "context_0", "context_1", "tensor"),
    )
    in_specs = (
        P("shard", CONTEXT, None),
        P("shard"),
        P(SHARD_CONTEXT),
        P(SHARD_CONTEXT, "tensor"),
        P(SHARD_CONTEXT, None),
        P(SHARD_CONTEXT, "tensor"),
        P(SHARD_CONTEXT),
        P(SHARD_CONTEXT, "tensor"),
        P(SHARD_CONTEXT, "tensor"),
        P(SHARD_CONTEXT, "tensor"),
        P("shard", CONTEXT, None),
    )
    out_specs = (
        P("shard", CONTEXT, None),
        P("shard", CONTEXT, None),
        P(SHARD_CONTEXT),
        P(SHARD_CONTEXT, "tensor"),
        P(SHARD_CONTEXT, None),
        P(SHARD_CONTEXT, "tensor"),
        P(SHARD_CONTEXT),
        P(SHARD_CONTEXT, "tensor"),
        P(SHARD_CONTEXT, "tensor"),
        P(SHARD_CONTEXT, "tensor"),
    )
    return jax.shard_map(
        shards, mesh=torus, in_specs=in_specs, out_specs=out_specs, check_vma=False
    )
```
